256 devices in a mesh: gx: 4 (over x), gyz: 32 (over z, y), band: 2 (over core).
Axes of the slice: x: 4, y: 4, z: 8, core: 2. Of those that a mesh axis runs over, the one named last changes fastest.
Arguments:
- block: float32 [16, 16, 256, 128], P('band', 'gx', 'gyz'), may hold values from -6 to 6
- potential: float32 [16, 256, 128], P('gx', 'gyz'), may hold values from -1 to 1
- proj_index: int32 [1024, 128], P(('gx', 'gyz')), may hold values from 0 to 4095
- proj_value: float32 [1024, 128], P(('gx', 'gyz')), may hold values from -0.5 to 0.5
- proj_strength: float32 [1024], P(('gx', 'gyz')), may hold values from 0.5 to 2
- stored: float32 [1024, 16, 256, 128], P('band', 'gx', 'gyz'), may hold values from -0.0078125 to 0.0078125
Outputs:
- projected: float32 [16, 16, 256, 128], P('band', 'gx', 'gyz')
- intersection: float32 [1024, 16], P('band')
The draws below stay inside these ranges and needn't reach their ends.
Inputs may be any that keep to these rules, and one draw needn't show every extreme that they name: `proj_index`: flat index of a cell within the grid block of 4 x 8 x 128 cells that holds the projector, z fastest; cells of one projector may repeat.
All inputs are finite; a program needn't handle non-finite values.
Results may differ from the reference program's by a relative error of at most 0.00008.
Values sent between devices are 32-bit elements; how exact they have to be, the bound alone decides.
A program may use at most 64 MiB of HBM per device.

```python
import math
from functools import partial
import jax
import jax.numpy as jnp
from jax import lax

NBLOCK = 16
NSTORED = 1024
DEGREE = 8
CX = 4
CY = 8
CZ = 128
PROJ_DEV = 8
PROJ_CELLS = 128
NX = 16
NY = 256
NZ = 128
NPROJ = 1024
N_GYZ = 32


def plant(drawn, key, low, high):
    dims = drawn.shape
    place = [jax.random.randint(jax.random.fold_in(key, axis), (), 0, dims[axis]) for axis in range(len(dims))]
    drawn = drawn.at[tuple(place)].set(low)
    longest = dims.index(max(dims))
    place[longest] = (place[longest] + 1) % dims[longest]
    return drawn.at[tuple(place)].set(high)


def block_scale(stream_key, extent, cuts, low, largest):
    factor_of = 1.0
    for position, blocks in cuts:
        steps = jax.random.uniform(jax.random.fold_in(jax.random.fold_in(stream_key, 6), position), (blocks,), jnp.float32, low / len(cuts), largest / len(cuts))
        factor_of = factor_of * jnp.repeat(jnp.exp(steps), extent[position] // blocks).reshape((-1,) + (1,) * (len(extent) - 1 - position))
    return factor_of


def scatter_about(key, shape, scale, reach, cuts=(), held_as=jnp.bfloat16):
    array = scale * jax.random.normal(key, shape, jnp.float32)
    if cuts:
        array = array * block_scale(key, shape, cuts, -0.22, 0.18)
    return jnp.clip(array, -reach, reach).astype(held_as)


def setup_inputs(seed: int = 0) -> dict:
    keys = jax.random.split(jax.random.key(seed), 7)
    return {
        "block": scatter_about(keys[0], (NBLOCK, NX, NY, NZ), 1.0, 6.0, ((0, 2), (1, 4), (2, 32)), jnp.float32),
        "potential": jnp.clip(jax.random.uniform(keys[1], (NX, NY, NZ), jnp.float32, -1.0, 1.0) * block_scale(keys[1], (NX, NY, NZ), ((0, 4), (1, 32)), -0.4, 0.0), -1.0, 1.0),
        "proj_index": plant(jax.random.randint(keys[2], (NPROJ, PROJ_CELLS), 0, CX * CY * CZ), jax.random.fold_in(keys[2], 1), 0, (CX * CY * CZ) - 1).astype(jnp.int32),
        "proj_value": scatter_about(keys[3], (NPROJ, PROJ_CELLS), PROJ_CELLS ** -0.5, 0.5, ((0, 128),), jnp.float32),
        "proj_strength": jnp.clip(jnp.exp(math.log(2.0) - 1.3862944 * jax.random.uniform(keys[4], (NPROJ,), jnp.float32) ** block_scale(keys[4], (NPROJ,), ((0, 128),), -0.2, 0.2)), 0.5, 2.0),
        "stored": scatter_about(keys[5], (NSTORED, NX, NY, NZ), (NX * NY * NZ) ** -0.5, 0.0078125, ((0, 2), (1, 4), (2, 32)), jnp.float32),
    }


LOW_EDGE = 0.0
CUT_EDGE = 1.0
TOP_EDGE = 10.0


def chebyshev(start_block, hamiltonian):
    half_width = (TOP_EDGE - CUT_EDGE) / 2.0
    center = (TOP_EDGE + CUT_EDGE) / 2.0
    sigma_first = half_width / (LOW_EDGE - center)
    previous = start_block
    current = (sigma_first / half_width) * (hamiltonian(start_block) - center * start_block)
    sigma_now = sigma_first
    for turn_index in range(DEGREE - 1):
        sigma_next = 1.0 / (2.0 / sigma_first - sigma_now)
        following = (2.0 * sigma_next / half_width) * (hamiltonian(current) - center * current) - (sigma_now * sigma_next) * previous
        previous, current, sigma_now = current, following, sigma_next
    return current


def nonlocal_term(flat_block, cell_index, proj_value, proj_strength):
    picked = flat_block[:, cell_index]
    weights = jnp.sum(picked * proj_value[None], axis=2) * proj_strength[None]
    spread = weights[:, :, None] * proj_value[None]
    return jnp.zeros_like(flat_block).at[:, cell_index].add(spread)


def hamiltonian_whole(field, potential, cell_index, proj_value, proj_strength):
    neighbours = jnp.roll(field, 1, 1) + jnp.roll(field, -1, 1) + jnp.roll(field, 1, 2) + jnp.roll(field, -1, 2)
    padded = jnp.pad(field, ((0, 0), (0, 0), (0, 0), (1, 1)))
    neighbours = neighbours + padded[..., 2:] + padded[..., :-2]
    local_part = -0.5 * (neighbours - 6.0 * field) + potential[None] * field
    count = field.shape[0]
    flat = field.reshape(count, -1)
    return local_part + nonlocal_term(flat, cell_index, proj_value, proj_strength).reshape(field.shape)


def reference(block, potential, proj_index, proj_value, proj_strength, stored):
    domain = jnp.arange(proj_index.shape[0], dtype=jnp.int32) // PROJ_DEV
    block_x = (domain // N_GYZ)[:, None]
    block_y = (domain % N_GYZ)[:, None]
    local_x = proj_index // (CY * CZ)
    local_y = (proj_index // CZ) % CY
    local_z = proj_index % CZ
    global_x = block_x * CX + local_x
    global_y = block_y * CY + local_y
    cell_index = ((global_x * NY + global_y) * NZ + local_z).astype(jnp.int32)
    hamiltonian = partial(hamiltonian_whole, potential=potential, cell_index=cell_index, proj_value=proj_value, proj_strength=proj_strength)
    filtered = chebyshev(block, hamiltonian)
    flat_filtered = filtered.reshape(NBLOCK, -1)
    flat_stored = stored.reshape(NSTORED, -1)
    intersection = jnp.dot(flat_stored, flat_filtered.T, precision=lax.Precision.HIGHEST)
    correction = jnp.dot(intersection.T, flat_stored, precision=lax.Precision.HIGHEST)
    projected = (flat_filtered - correction).reshape(block.shape)
    return projected, intersection
```

```python
import functools

import jax
import jax.numpy as jnp
from jax import lax
from jax.experimental import pallas as pl
from jax.experimental.pallas import tpu as pltpu
from jax.sharding import PartitionSpec as P

DEGREE = 8
LOW_EDGE = 0.0
CUT_EDGE = 1.0
TOP_EDGE = 10.0
HALF = (TOP_EDGE - CUT_EDGE) / 2.0
CENTER = (TOP_EDGE + CUT_EDGE) / 2.0

MESH = pl.DeviceIdType.MESH
F32 = jnp.float32
BF16 = jnp.bfloat16

CX, CY, CZ = 4, 8, 128
NXY = CX * CY
CELLS = NXY * CZ
ORB = 8
NPROJ = 8
NJ = 512
NG_X, NG_Y, NG_Z = 4, 4, 8
PLANE = NG_X * NG_Y


def recurrence():
    first = HALF / (LOW_EDGE - CENTER)
    scales, backs = [first / HALF], [0.0]
    now = first
    for _ in range(DEGREE - 1):
        after = 1.0 / (2.0 / first - now)
        scales.append(2.0 * after / HALF)
        backs.append(now * after)
        now = after
    return scales, backs


SCALES, BACKS = recurrence()


def pick(k, values):
    out = jnp.float32(values[-1])
    for i in range(len(values) - 2, -1, -1):
        out = jnp.where(k == i, jnp.float32(values[i]), out)
    return out


def kernel(
    block_ref, pot_ref, idx_ref, val_ref, str_ref, stored_ref,
    out_ref, int_ref,
    field, raw, halo_x, halo_y, beta, pot, sraw, s_hi, s_lo, other, wmat,
    pbuf, r1, g2, q3, csend, crecv,
    in_sem, st_sem, hs_sem, hr_sem, b_sem, p1s, p1r, p2s, p2r, p3s, p3r, cs_sem, cr_sem,
):
    gx = lax.axis_index("gx")
    gyz = lax.axis_index("gyz")
    band = lax.axis_index("band")
    mz = lax.div(gyz, NG_Y)
    my = lax.rem(gyz, NG_Y)
    plane = gx * NG_Y + my
    xl = (lax.rem(gx + NG_X - 1, NG_X), gyz, band)
    xr = (lax.rem(gx + 1, NG_X), gyz, band)
    yl = (gx, lax.rem(gyz + NG_Y * NG_Z - 1, NG_Y * NG_Z), band)
    yr = (gx, lax.rem(gyz + 1, NG_Y * NG_Z), band)
    twin = (gx, gyz, 1 - band)

    def plane_peer(i):
        at = lax.rem(plane + i, PLANE)
        return at, (lax.div(at, NG_Y), mz * NG_Y + lax.rem(at, NG_Y), band)

    def z_peer(i):
        at = lax.rem(mz + i, NG_Z)
        return at, (gx, at * NG_Y + my, band)

    barrier = pltpu.get_barrier_semaphore()

    def greet(device):
        pl.semaphore_signal(barrier, inc=1, device_id=device, device_id_type=MESH)

    for device in (yl, yr, twin):
        greet(device)
    for i in range(1, PLANE):
        greet(plane_peer(i)[1])
    for i in range(1, NG_Z):
        greet(z_peer(i)[1])

    load_block = pltpu.make_async_copy(block_ref, raw, in_sem)
    load_block.start()
    rows = NJ * NXY // DEGREE

    def load_stored(k):
        at = pl.ds(pl.multiple_of(k * rows, rows), rows)
        return pltpu.make_async_copy(stored_ref.at[at], sraw.at[at], st_sem.at[k])

    load_block.wait()
    for k in range(DEGREE):
        load_stored(k).start()

    for xy in range(NXY):
        field[0, xy // CY, xy % CY] = raw[pl.ds(xy, ORB, stride=NXY), :]
    field[1] = jnp.zeros((CX, CY, ORB, CZ), F32)

    pl.semaphore_wait(barrier, 3 + PLANE - 1 + NG_Z - 1)

    def halo_copies(slot):
        def copy(src, dst, n, device):
            return pltpu.make_async_remote_copy(
                src_ref=src, dst_ref=dst, send_sem=hs_sem.at[slot, n], recv_sem=hr_sem.at[slot, n],
                device_id=device, device_id_type=MESH)
        return (
            copy(field.at[slot, 0], halo_x.at[slot, 1], 1, xl),
            copy(field.at[slot, CX - 1], halo_x.at[slot, 0], 0, xr),
            copy(field.at[slot, :, 0], halo_y.at[slot, 1], 3, yl),
            copy(field.at[slot, :, CY - 1], halo_y.at[slot, 0], 2, yr),
        )

    def prepare():
        pot[...] = jnp.broadcast_to(
            (pot_ref[...] + (3.0 - CENTER))[:, None, :], (NXY, ORB, CZ)).reshape(CX, CY, ORB, CZ)
        for p in range(NPROJ):
            index = idx_ref[p:p + 1, :]
            value = val_ref[p:p + 1, :]
            v1 = value.astype(BF16).astype(F32)
            v2 = (value - v1).astype(BF16).astype(F32)
            v3 = value - v1 - v2
            high = lax.shift_right_logical(index, 7)
            low = lax.bitwise_and(index, 127)
            at_xy = lax.broadcasted_iota(jnp.int32, (NXY, 128), 0) == high
            at_z = lax.broadcasted_iota(jnp.int32, (CZ, 128), 0) == low
            left = jnp.concatenate([jnp.where(at_xy, v, 0.0) for v in (v1, v2, v3)], axis=0).astype(BF16)
            right = jnp.where(at_z, 1.0, 0.0).astype(BF16)
            got = lax.dot_general(left, right, (((1,), (1,)), ((), ())), preferred_element_type=F32)
            dense = got[0:NXY] + got[NXY:2 * NXY] + got[2 * NXY:]
            beta[p] = jnp.broadcast_to(dense[:, None, :], (NXY, ORB, CZ)).reshape(CX, CY, ORB, CZ)

    lane = lax.broadcasted_iota(jnp.int32, (CY, ORB, CZ), 2)

    def local(slot, scale, back):
        weights = []
        whole = field[slot]
        for p in range(NPROJ):
            acc = jnp.sum(whole * beta[p], axis=(0, 1))
            weights.append(jnp.sum(acc, axis=1, keepdims=True) * str_ref[p])
        zero = jnp.zeros((1, ORB, CZ), F32)
        for x in range(CX):
            cur = field[slot, x]
            near = jnp.concatenate([zero, cur[:-1]], axis=0) + jnp.concatenate([cur[1:], zero], axis=0)
            near = near + jnp.where(lane == 0, 0.0, pltpu.roll(cur, 1, 2))
            near = near + jnp.where(lane == CZ - 1, 0.0, pltpu.roll(cur, CZ - 1, 2))
            if x > 0:
                near = near + field[slot, x - 1]
            if x < CX - 1:
                near = near + field[slot, x + 1]
            total = pot[x] * cur - 0.5 * near
            for p in range(NPROJ):
                total = total + weights[p][None] * beta[p, x]
            field[1 - slot, x] = scale * total - back * field[1 - slot, x]

    def split_stored(k):
        load_stored(k).wait()
        first = pl.multiple_of(k * (NJ // DEGREE), NJ // DEGREE)
        base = k * rows

        def part(xy, carry):
            got = sraw[pl.ds(base + xy, NJ // DEGREE, stride=NXY), :]
            high = got.astype(BF16)
            cols = pl.ds(pl.multiple_of(xy * CZ, CZ), CZ)
            s_hi[pl.ds(first, NJ // DEGREE), cols] = high
            s_lo[pl.ds(first, NJ // DEGREE), cols] = (got - high.astype(F32)).astype(BF16)
            return carry

        lax.fori_loop(0, NXY, part, 0)

    def step(k, carry):
        slot = lax.rem(k, 2)
        copies = halo_copies(slot)
        for c in copies:
            c.start()

        @pl.when(k == 0)
        def _():
            prepare()

        @pl.when(k > 0)
        def _():
            for c in halo_copies(1 - slot):
                c.wait_send()

        scale = pick(k, SCALES)
        local(slot, scale, pick(k, BACKS))
        split_stored(k)
        for c in copies:
            c.wait_recv()
        factor = -0.5 * scale
        nxt = 1 - slot
        field[nxt, 0] = field[nxt, 0] + factor * halo_x[slot, 0]
        field[nxt, CX - 1] = field[nxt, CX - 1] + factor * halo_x[slot, 1]
        field[nxt, :, 0] = field[nxt, :, 0] + factor * halo_y[slot, 0]
        field[nxt, :, CY - 1] = field[nxt, :, CY - 1] + factor * halo_y[slot, 1]
        return carry

    lax.fori_loop(0, DEGREE, step, 0)
    for c in halo_copies((DEGREE - 1) % 2):
        c.wait_send()

    swap = pltpu.make_async_remote_copy(
        src_ref=field.at[0], dst_ref=other, send_sem=b_sem.at[0], recv_sem=b_sem.at[1],
        device_id=twin, device_id_type=MESH)
    swap.start()
    swap.wait()

    first_core = band == 0
    for xy in range(NXY):
        mine, theirs = field[0, xy // CY, xy % CY], other[xy // CY, xy % CY]
        both = jnp.concatenate(
            [jnp.where(first_core, mine, theirs), jnp.where(first_core, theirs, mine)], axis=0)
        high = both.astype(BF16)
        wmat[0:16, xy * CZ:(xy + 1) * CZ] = high
        wmat[16:32, xy * CZ:(xy + 1) * CZ] = (both - high.astype(F32)).astype(BF16)

    def send1(c):
        return pltpu.make_async_remote_copy(
            src_ref=pbuf.at[c], dst_ref=r1.at[mz], send_sem=p1s.at[c], recv_sem=p1r.at[mz],
            device_id=(gx, c * NG_Y + my, band), device_id_type=MESH)

    nt = (((1,), (1,)), ((), ()))
    for t in range(NJ // 128):
        weights = wmat[...]
        got = lax.dot_general(s_hi[t * 128:(t + 1) * 128, :], weights, nt, preferred_element_type=F32)
        got = got + lax.dot_general(s_lo[t * 128:(t + 1) * 128, :], weights, nt, preferred_element_type=F32)
        flat = got.T
        flat = flat[0:16] + flat[16:32]
        for h in range(2):
            c = 2 * t + h
            pbuf[c] = flat[8 * h:8 * h + 8]

            @pl.when(mz == c)
            def _(c=c):
                r1[c] = pbuf[c]

            @pl.when(mz != c)
            def _(c=c):
                send1(c).start()

    def recv1(i):
        at, device = z_peer(i)
        return pltpu.make_async_remote_copy(
            src_ref=pbuf.at[at], dst_ref=r1.at[at], send_sem=p1s.at[at], recv_sem=p1r.at[at],
            device_id=device, device_id_type=MESH)

    for i in range(1, NG_Z):
        recv1(i).wait_recv()
    g2[plane] = jnp.sum(r1[...], axis=0)

    def send2(i):
        return pltpu.make_async_remote_copy(
            src_ref=g2.at[plane], dst_ref=g2.at[plane], send_sem=p2s.at[i], recv_sem=p2r.at[plane],
            device_id=plane_peer(i)[1], device_id_type=MESH)

    def recv2(i):
        at, device = plane_peer(i)
        return pltpu.make_async_remote_copy(
            src_ref=g2.at[plane], dst_ref=g2.at[at], send_sem=p2s.at[i], recv_sem=p2r.at[at],
            device_id=device, device_id_type=MESH)

    for i in range(1, PLANE):
        send2(i).start()
    for i in range(1, NG_Z):
        recv1(i).wait_send()
    for i in range(1, PLANE):
        recv2(i).wait_recv()
    q3[mz] = jnp.sum(g2[...], axis=0)

    def send3(i):
        return pltpu.make_async_remote_copy(
            src_ref=q3.at[mz], dst_ref=q3.at[mz], send_sem=p3s.at[i], recv_sem=p3r.at[mz],
            device_id=z_peer(i)[1], device_id_type=MESH)

    def recv3(i):
        at, device = z_peer(i)
        return pltpu.make_async_remote_copy(
            src_ref=q3.at[mz], dst_ref=q3.at[at], send_sem=p3s.at[i], recv_sem=p3r.at[at],
            device_id=device, device_id_type=MESH)

    for i in range(1, NG_Z):
        send3(i).start()
    for i in range(1, PLANE):
        send2(i).wait_send()
    for i in range(1, NG_Z):
        recv3(i).wait_recv()

    whole = jnp.concatenate(
        [jnp.concatenate([q3[2 * t], q3[2 * t + 1]], axis=0) for t in range(NJ // 128)], axis=1)
    int_ref[...] = whole
    high = whole.astype(BF16)
    low = (whole - high.astype(F32)).astype(BF16)
    left = jnp.concatenate([high, low], axis=0)
    nn = (((1,), (0,)), ((), ()))

    def give(x):
        return pltpu.make_async_remote_copy(
            src_ref=csend.at[x], dst_ref=crecv.at[x], send_sem=cs_sem.at[x], recv_sem=cr_sem.at[x],
            device_id=twin, device_id_type=MESH)

    for x in range(CX):
        cols = slice(x * CY * CZ, (x + 1) * CY * CZ)
        got = lax.dot_general(left, s_hi[:, cols], nn, preferred_element_type=F32)
        more = lax.dot_general(high, s_lo[:, cols], nn, preferred_element_type=F32)
        got = got[0:16] + got[16:32] + more
        keep = jnp.where(first_core, got[0:8], got[8:16])
        send = jnp.where(first_core, got[8:16], got[0:8])
        for y in range(CY):
            csend[x, y] = send[:, y * CZ:(y + 1) * CZ]
            field[1, x, y] = field[0, x, y] - keep[:, y * CZ:(y + 1) * CZ]
        give(x).start()
    for i in range(1, NG_Z):
        send3(i).wait_send()
    for x in range(CX):
        give(x).wait_recv()
        for y in range(CY):
            out_ref[pl.ds(x * CY + y, ORB, stride=NXY), :] = field[1, x, y] - crecv[x, y]
    for x in range(CX):
        give(x).wait_send()


def on_device(block, potential, proj_index, proj_value, proj_strength, stored):
    vmem = pl.BlockSpec(memory_space=pltpu.VMEM)
    dma = pltpu.SemaphoreType.DMA
    projected, intersection = pl.pallas_call(
        kernel,
        out_shape=(
            jax.ShapeDtypeStruct((ORB * NXY, CZ), F32),
            jax.ShapeDtypeStruct((2 * ORB, NJ), F32),
        ),
        in_specs=[
            pl.BlockSpec(memory_space=pl.ANY), vmem, vmem, vmem,
            pl.BlockSpec(memory_space=pltpu.SMEM), pl.BlockSpec(memory_space=pl.ANY)],
        out_specs=(vmem, vmem),
        scratch_shapes=[
            pltpu.VMEM((2, CX, CY, ORB, CZ), F32),
            pltpu.VMEM((ORB * NXY, CZ), F32),
            pltpu.VMEM((2, 2, CY, ORB, CZ), F32),
            pltpu.VMEM((2, 2, CX, ORB, CZ), F32),
            pltpu.VMEM((NPROJ, CX, CY, ORB, CZ), F32),
            pltpu.VMEM((CX, CY, ORB, CZ), F32),
            pltpu.VMEM((NJ * NXY, CZ), F32),
            pltpu.VMEM((NJ, CELLS), BF16),
            pltpu.VMEM((NJ, CELLS), BF16),
            pltpu.VMEM((CX, CY, ORB, CZ), F32),
            pltpu.VMEM((4 * ORB, CELLS), BF16),
            pltpu.VMEM((NG_Z, ORB, CZ), F32),
            pltpu.VMEM((NG_Z, ORB, CZ), F32),
            pltpu.VMEM((PLANE, ORB, CZ), F32),
            pltpu.VMEM((NG_Z, ORB, CZ), F32),
            pltpu.VMEM((CX, CY, ORB, CZ), F32),
            pltpu.VMEM((CX, CY, ORB, CZ), F32),
            dma, dma((DEGREE,)), dma((2, 4)), dma((2, 4)), dma((2,)),
            dma((NG_Z,)), dma((NG_Z,)), dma((PLANE,)), dma((PLANE,)), dma((NG_Z,)), dma((NG_Z,)),
            dma((CX,)), dma((CX,)),
        ],
        compiler_params=pltpu.CompilerParams(
            collective_id=0, has_side_effects=True, vmem_limit_bytes=40 * 1024 * 1024),
        name="filter_project",
    )(
        block.reshape(ORB * NXY, CZ), potential.reshape(NXY, CZ), proj_index, proj_value,
        proj_strength, stored.reshape(NJ * NXY, CZ))
    return projected.reshape(block.shape), intersection.T


def solution(mesh):
    in_specs = (
        P("band", "gx", "gyz", None),
        P("gx", "gyz", None),
        P(("gx", "gyz"), None),
        P(("gx", "gyz"), None),
        P(("gx", "gyz")),
        P("band", "gx", "gyz", None),
    )
    out_specs = (P("band", "gx", "gyz", None), P("band", None))
    return jax.shard_map(
        on_device, mesh=mesh, in_specs=in_specs, out_specs=out_specs, check_vma=False
    )
```

```python
import functools

import jax
import jax.numpy as jnp
from jax import lax
from jax.experimental import pallas as pl
from jax.experimental.pallas import tpu as pltpu
from jax.sharding import PartitionSpec as P

DEGREE = 8
ROUNDS = DEGREE // 2
LOW_EDGE = 0.0
CUT_EDGE = 1.0
TOP_EDGE = 10.0
HALF = (TOP_EDGE - CUT_EDGE) / 2.0
CENTER = (TOP_EDGE + CUT_EDGE) / 2.0

MESH = pl.DeviceIdType.MESH
F32 = jnp.float32
BF16 = jnp.bfloat16

CX, CY, CZ = 4, 8, 128
NXY = CX * CY
CELLS = NXY * CZ
ORB = 8
NPROJ = 8
NJ = 512
NG_X, NG_Y, NG_Z = 4, 4, 8
PLANE = NG_X * NG_Y


def recurrence():
    x = (LOW_EDGE - CENTER) / HALF
    t = [1.0, x]
    while len(t) <= DEGREE:
        t.append(2.0 * x * t[-1] - t[-2])
    ups, stays, backs = [2.0 / t[2]], [-1.0 / t[2]], [0.0]
    for m in range(1, ROUNDS):
        after = t[2 * m + 2]
        ups.append(4.0 * t[2 * m] / after)
        stays.append(-2.0 * t[2 * m] / after)
        backs.append(t[2 * m - 2] / after)
    return ups, stays, backs


UPS, STAYS, BACKS = recurrence()


def pick(k, values):
    out = jnp.float32(values[-1])
    for i in range(len(values) - 2, -1, -1):
        out = jnp.where(k == i, jnp.float32(values[i]), out)
    return out


def kernel(
    block_ref, pot_ref, idx_ref, val_ref, str_ref, stored_ref,
    out_ref, int_ref,
    field, inner, raw, beta, dense, edge, side_x, side_y, beta_x, beta_y, coef, coef_in, sraw, s_hi, s_lo, other, wmat,
    pbuf, r1, g2, q3, csend, crecv,
    in_sem, st_sem, hs_sem, hr_sem, fs_sem, fr_sem, b_sem, p1s, p1r, p2s, p2r, p3s, p3r, cs_sem, cr_sem,
):
    gx = lax.axis_index("gx")
    gyz = lax.axis_index("gyz")
    band = lax.axis_index("band")
    mz = lax.div(gyz, NG_Y)
    my = lax.rem(gyz, NG_Y)
    plane = gx * NG_Y + my
    left, right = lax.rem(gx + NG_X - 1, NG_X), lax.rem(gx + 1, NG_X)
    down, up = lax.rem(gyz + NG_Y * NG_Z - 1, NG_Y * NG_Z), lax.rem(gyz + 1, NG_Y * NG_Z)
    xl, xr, yl, yr = (left, gyz, band), (right, gyz, band), (gx, down, band), (gx, up, band)
    diagonal = [(x, y, band) for x in (left, right) for y in (down, up)]
    twin = (gx, gyz, 1 - band)

    def plane_peer(i):
        at = lax.rem(plane + i, PLANE)
        return at, (lax.div(at, NG_Y), mz * NG_Y + lax.rem(at, NG_Y), band)

    def z_peer(i):
        at = lax.rem(mz + i, NG_Z)
        return at, (gx, at * NG_Y + my, band)

    barrier = pltpu.get_barrier_semaphore()

    def greet(device):
        pl.semaphore_signal(barrier, inc=1, device_id=device, device_id_type=MESH)

    for device in [yl, yr, twin] + diagonal:
        greet(device)
    for i in range(1, PLANE):
        greet(plane_peer(i)[1])
    for i in range(1, NG_Z):
        greet(z_peer(i)[1])

    load_block = pltpu.make_async_copy(block_ref, raw, in_sem)
    load_block.start()
    rows = NJ * NXY // DEGREE

    def load_stored(k):
        at = pl.ds(pl.multiple_of(k * rows, rows), rows)
        return pltpu.make_async_copy(stored_ref.at[at], sraw.at[at], st_sem.at[k])

    def prepare():
        low_edge = lax.broadcasted_iota(jnp.int32, (NXY, 128), 0)
        at_row = lax.broadcasted_iota(jnp.int32, (CZ, 128), 0)
        for p in range(NPROJ):
            index = idx_ref[p:p + 1, :]
            value = val_ref[p:p + 1, :]
            v1 = value.astype(BF16).astype(F32)
            v2 = (value - v1).astype(BF16).astype(F32)
            v3 = value - v1 - v2
            at_xy = low_edge == lax.shift_right_logical(index, 7)
            at_z = at_row == lax.bitwise_and(index, 127)
            picks = jnp.concatenate([jnp.where(at_xy, v, 0.0) for v in (v1, v2, v3)], axis=0).astype(BF16)
            places = jnp.where(at_z, 1.0, 0.0).astype(BF16)
            got = lax.dot_general(picks, places, (((1,), (1,)), ((), ())), preferred_element_type=F32)
            dense[p] = got[0:NXY] + got[NXY:2 * NXY] + got[2 * NXY:]
        dense[NPROJ] = (pot_ref[...] + (3.0 - CENTER)) * (1.0 / HALF)
        for p in range(NPROJ + 1):
            beta[p] = jnp.broadcast_to(dense[p][:, None, :], (NXY, ORB, CZ)).reshape(CX, CY, ORB, CZ)
            edge[p, 0:4] = dense[p, pl.ds(0, CX, stride=CY), :]
            edge[p, 4:8] = dense[p, pl.ds(CY - 1, CX, stride=CY), :]

    def side_copies():
        def copy(src, dst, n, device):
            return pltpu.make_async_remote_copy(
                src_ref=src, dst_ref=dst, send_sem=fs_sem.at[n], recv_sem=fr_sem.at[n],
                device_id=device, device_id_type=MESH)
        return (
            copy(dense.at[:, 0:CY], side_x.at[1], 1, xl),
            copy(dense.at[:, NXY - CY:NXY], side_x.at[0], 0, xr),
            copy(edge, side_y.at[1], 3, yl),
            copy(edge, side_y.at[0], 2, yr),
        )

    def spread_sides():
        for p in range(NPROJ + 1):
            for side in range(2):
                beta_x[side, p] = jnp.broadcast_to(side_x[side, p][:, None, :], (CY, ORB, CZ))
                rows_y = side_y[side, p, 4:8] if side == 0 else side_y[side, p, 0:4]
                beta_y[side, p] = jnp.broadcast_to(rows_y[:, None, :], (CX, ORB, CZ))

    load_block.wait()
    for k in range(DEGREE):
        load_stored(k).start()

    for xy in range(NXY):
        field[0, 2 + xy // CY, 2 + xy % CY] = raw[pl.ds(xy, ORB, stride=NXY), :]
    field[1, 2:6, 2:10] = jnp.zeros((CX, CY, ORB, CZ), F32)
    prepare()

    pl.semaphore_wait(barrier, 7 + PLANE - 1 + NG_Z - 1)

    def halo_copies(slot):
        def copy(src, dst, n, device):
            return pltpu.make_async_remote_copy(
                src_ref=field.at[(slot,) + src], dst_ref=field.at[(slot,) + dst],
                send_sem=hs_sem.at[slot, n], recv_sem=hr_sem.at[slot, n],
                device_id=device, device_id_type=MESH)
        own_x, own_y = slice(2, 6), slice(2, 10)
        return (
            copy((2, 2), (6, 10), 4, diagonal[0]),
            copy((2, 9), (6, 1), 5, diagonal[1]),
            copy((5, 2), (1, 10), 6, diagonal[2]),
            copy((5, 9), (1, 1), 7, diagonal[3]),
            copy((own_x, slice(2, 4)), (own_x, slice(10, 12)), 3, yl),
            copy((own_x, slice(8, 10)), (own_x, slice(0, 2)), 2, yr),
            copy((slice(2, 4), own_y), (slice(6, 8), own_y), 1, xl),
            copy((slice(4, 6), own_y), (slice(0, 2), own_y), 0, xr),
        )

    def coef_copies(slot):
        def copy(side, n, device):
            return pltpu.make_async_remote_copy(
                src_ref=coef.at[slot], dst_ref=coef_in.at[slot, side],
                send_sem=hs_sem.at[slot, 8 + n], recv_sem=hr_sem.at[slot, 8 + n],
                device_id=device, device_id_type=MESH)
        return copy(3, 3, yl), copy(2, 2, yr), copy(1, 1, xl), copy(0, 0, xr)

    lanes = lax.broadcasted_iota(jnp.int32, (1, ORB, CZ), 2)
    lane = lax.broadcasted_iota(jnp.int32, (ORB, CZ), 1)
    side_scale = 0.5 / HALF

    def along_z(cur):
        return (jnp.where(lanes == 0, 0.0, pltpu.roll(cur, 1, 2))
                + jnp.where(lanes == CZ - 1, 0.0, pltpu.roll(cur, CZ - 1, 2)))

    def coefficients(whole):
        out = []
        for p in range(NPROJ):
            acc = jnp.sum(whole * beta[p], axis=(0, 1))
            out.append(jnp.sum(acc, axis=1, keepdims=True) * (str_ref[p] * (1.0 / HALF)))
        return out

    def spread(weights, tiles):
        total = weights[0][None] * tiles(0)
        for p in range(1, NPROJ):
            total = total + weights[p][None] * tiles(p)
        return total

    def first_inside(slot, weights):
        zero = jnp.zeros((1, ORB, CZ), F32)
        for x in range(CX):
            cur = field[slot, 2 + x, 2:10]
            near = jnp.concatenate([zero, cur[:-1]], axis=0) + jnp.concatenate([cur[1:], zero], axis=0)
            near = near + along_z(cur)
            if x > 0:
                near = near + field[slot, 1 + x, 2:10]
            if x < CX - 1:
                near = near + field[slot, 3 + x, 2:10]
            inner[1 + x, 1:9] = (
                beta[NPROJ, x] * cur - side_scale * near + spread(weights, lambda p: beta[p, x]))

    def first_outside(slot):
        inner[1, 1:9] = inner[1, 1:9] - side_scale * field[slot, 1, 2:10]
        inner[4, 1:9] = inner[4, 1:9] - side_scale * field[slot, 6, 2:10]
        inner[1:5, 1] = inner[1:5, 1] - side_scale * field[slot, 2:6, 1]
        inner[1:5, 8] = inner[1:5, 8] - side_scale * field[slot, 2:6, 10]
        for side in range(2):
            at = 1 if side == 0 else 6
            got = coef_in[slot, side]
            weights = [got[:, p:p + 1] for p in range(NPROJ)]
            cur = field[slot, at, 2:10]
            near = field[slot, at - 1, 2:10] + field[slot, at + 1, 2:10]
            near = near + field[slot, at, 1:9] + field[slot, at, 3:11] + along_z(cur)
            inner[at - 1, 1:9] = (
                beta_x[side, NPROJ] * cur - side_scale * near
                + spread(weights, lambda p: beta_x[side, p]))
        for side in range(2):
            at = 1 if side == 0 else 10
            got = coef_in[slot, 2 + side]
            weights = [got[:, p:p + 1] for p in range(NPROJ)]
            cur = field[slot, 2:6, at]
            near = field[slot, 2:6, at - 1] + field[slot, 2:6, at + 1]
            near = near + field[slot, 1:5, at] + field[slot, 3:7, at] + along_z(cur)
            inner[1:5, at - 1] = (
                beta_y[side, NPROJ] * cur - side_scale * near
                + spread(weights, lambda p: beta_y[side, p]))

    def second(slot, ups, stays, backs):
        weights = coefficients(inner[1:5, 1:9])
        for x in range(CX):
            cur = inner[1 + x, 1:9]
            near = inner[x, 1:9] + inner[2 + x, 1:9] + inner[1 + x, 0:8] + inner[1 + x, 2:10]
            near = near + along_z(cur)
            twice = beta[NPROJ, x] * cur - side_scale * near + spread(weights, lambda p: beta[p, x])
            field[1 - slot, 2 + x, 2:10] = (
                ups * twice + stays * field[slot, 2 + x, 2:10] - backs * field[1 - slot, 2 + x, 2:10])

    def split_stored(k):
        load_stored(k).wait()
        first = pl.multiple_of(k * (NJ // DEGREE), NJ // DEGREE)
        base = k * rows

        def part(xy, carry):
            got = sraw[pl.ds(base + xy, NJ // DEGREE, stride=NXY), :]
            high = got.astype(BF16)
            cols = pl.ds(pl.multiple_of(xy * CZ, CZ), CZ)
            s_hi[pl.ds(first, NJ // DEGREE), cols] = high
            s_lo[pl.ds(first, NJ // DEGREE), cols] = (got - high.astype(F32)).astype(BF16)
            return carry

        lax.fori_loop(0, NXY, part, 0)

    def step(k, carry):
        slot = lax.rem(k, 2)
        copies = halo_copies(slot)
        for c in copies:
            c.start()

        @pl.when(k == 0)
        def _():
            for c in side_copies():
                c.start()

        weights = coefficients(field[slot, 2:6, 2:10])
        packed = jnp.zeros((ORB, CZ), F32)
        for p in range(NPROJ):
            packed = jnp.where(lane == p, weights[p], packed)
        coef[slot] = packed
        more = coef_copies(slot)
        for c in more:
            c.start()
        first_inside(slot, weights)
        split_stored(2 * k)
        split_stored(2 * k + 1)

        @pl.when(k > 0)
        def _():
            for c in halo_copies(1 - slot) + coef_copies(1 - slot):
                c.wait_send()

        @pl.when(k == 0)
        def _():
            for c in side_copies():
                c.wait()
            spread_sides()

        for c in copies + more:
            c.wait_recv()
        first_outside(slot)
        second(slot, pick(k, UPS), pick(k, STAYS), pick(k, BACKS))
        return carry

    lax.fori_loop(0, ROUNDS, step, 0)
    for c in halo_copies((ROUNDS - 1) % 2) + coef_copies((ROUNDS - 1) % 2):
        c.wait_send()

    swap = pltpu.make_async_remote_copy(
        src_ref=field.at[0, 2:6, 2:10], dst_ref=other, send_sem=b_sem.at[0], recv_sem=b_sem.at[1],
        device_id=twin, device_id_type=MESH)
    swap.start()
    swap.wait()

    first_core = band == 0
    for xy in range(NXY):
        mine, theirs = field[0, 2 + xy // CY, 2 + xy % CY], other[xy // CY, xy % CY]
        both = jnp.concatenate(
            [jnp.where(first_core, mine, theirs), jnp.where(first_core, theirs, mine)], axis=0)
        high = both.astype(BF16)
        wmat[0:16, xy * CZ:(xy + 1) * CZ] = high
        wmat[16:32, xy * CZ:(xy + 1) * CZ] = (both - high.astype(F32)).astype(BF16)

    def send1(c):
        return pltpu.make_async_remote_copy(
            src_ref=pbuf.at[c], dst_ref=r1.at[mz], send_sem=p1s.at[c], recv_sem=p1r.at[mz],
            device_id=(gx, c * NG_Y + my, band), device_id_type=MESH)

    nt = (((1,), (1,)), ((), ()))
    for t in range(NJ // 128):
        weights = wmat[...]
        got = lax.dot_general(s_hi[t * 128:(t + 1) * 128, :], weights, nt, preferred_element_type=F32)
        got = got + lax.dot_general(s_lo[t * 128:(t + 1) * 128, :], weights, nt, preferred_element_type=F32)
        flat = got.T
        flat = flat[0:16] + flat[16:32]
        for h in range(2):
            c = 2 * t + h
            pbuf[c] = flat[8 * h:8 * h + 8]

            @pl.when(mz == c)
            def _(c=c):
                r1[c] = pbuf[c]

            @pl.when(mz != c)
            def _(c=c):
                send1(c).start()

    def recv1(i):
        at, device = z_peer(i)
        return pltpu.make_async_remote_copy(
            src_ref=pbuf.at[at], dst_ref=r1.at[at], send_sem=p1s.at[at], recv_sem=p1r.at[at],
            device_id=device, device_id_type=MESH)

    for i in range(1, NG_Z):
        recv1(i).wait_recv()
    g2[plane] = jnp.sum(r1[...], axis=0)

    def send2(i):
        return pltpu.make_async_remote_copy(
            src_ref=g2.at[plane], dst_ref=g2.at[plane], send_sem=p2s.at[i], recv_sem=p2r.at[plane],
            device_id=plane_peer(i)[1], device_id_type=MESH)

    def recv2(i):
        at, device = plane_peer(i)
        return pltpu.make_async_remote_copy(
            src_ref=g2.at[plane], dst_ref=g2.at[at], send_sem=p2s.at[i], recv_sem=p2r.at[at],
            device_id=device, device_id_type=MESH)

    for i in range(1, PLANE):
        send2(i).start()
    for i in range(1, NG_Z):
        recv1(i).wait_send()
    for i in range(1, PLANE):
        recv2(i).wait_recv()
    q3[mz] = jnp.sum(g2[...], axis=0)

    def send3(i):
        return pltpu.make_async_remote_copy(
            src_ref=q3.at[mz], dst_ref=q3.at[mz], send_sem=p3s.at[i], recv_sem=p3r.at[mz],
            device_id=z_peer(i)[1], device_id_type=MESH)

    def recv3(i):
        at, device = z_peer(i)
        return pltpu.make_async_remote_copy(
            src_ref=q3.at[mz], dst_ref=q3.at[at], send_sem=p3s.at[i], recv_sem=p3r.at[at],
            device_id=device, device_id_type=MESH)

    for i in range(1, NG_Z):
        send3(i).start()
    for i in range(1, PLANE):
        send2(i).wait_send()
    for i in range(1, NG_Z):
        recv3(i).wait_recv()

    whole = jnp.concatenate(
        [jnp.concatenate([q3[2 * t], q3[2 * t + 1]], axis=0) for t in range(NJ // 128)], axis=1)
    int_ref[...] = whole
    high = whole.astype(BF16)
    low = (whole - high.astype(F32)).astype(BF16)
    left = jnp.concatenate([high, low], axis=0)
    nn = (((1,), (0,)), ((), ()))

    def give(x):
        return pltpu.make_async_remote_copy(
            src_ref=csend.at[x], dst_ref=crecv.at[x], send_sem=cs_sem.at[x], recv_sem=cr_sem.at[x],
            device_id=twin, device_id_type=MESH)

    for x in range(CX):
        cols = slice(x * CY * CZ, (x + 1) * CY * CZ)
        got = lax.dot_general(left, s_hi[:, cols], nn, preferred_element_type=F32)
        more = lax.dot_general(high, s_lo[:, cols], nn, preferred_element_type=F32)
        got = got[0:16] + got[16:32] + more
        keep = jnp.where(first_core, got[0:8], got[8:16])
        send = jnp.where(first_core, got[8:16], got[0:8])
        for y in range(CY):
            csend[x, y] = send[:, y * CZ:(y + 1) * CZ]
            field[1, 2 + x, 2 + y] = field[0, 2 + x, 2 + y] - keep[:, y * CZ:(y + 1) * CZ]
        give(x).start()
    for i in range(1, NG_Z):
        send3(i).wait_send()
    for x in range(CX):
        give(x).wait_recv()
        for y in range(CY):
            out_ref[pl.ds(x * CY + y, ORB, stride=NXY), :] = field[1, 2 + x, 2 + y] - crecv[x, y]
    for x in range(CX):
        give(x).wait_send()


def on_device(block, potential, proj_index, proj_value, proj_strength, stored):
    vmem = pl.BlockSpec(memory_space=pltpu.VMEM)
    dma = pltpu.SemaphoreType.DMA
    projected, intersection = pl.pallas_call(
        kernel,
        out_shape=(
            jax.ShapeDtypeStruct((ORB * NXY, CZ), F32),
            jax.ShapeDtypeStruct((2 * ORB, NJ), F32),
        ),
        in_specs=[
            pl.BlockSpec(memory_space=pl.ANY), vmem, vmem, vmem,
            pl.BlockSpec(memory_space=pltpu.SMEM), pl.BlockSpec(memory_space=pl.ANY)],
        out_specs=(vmem, vmem),
        scratch_shapes=[
            pltpu.VMEM((2, CX + 4, CY + 4, ORB, CZ), F32),
            pltpu.VMEM((CX + 2, CY + 2, ORB, CZ), F32),
            pltpu.VMEM((ORB * NXY, CZ), F32),
            pltpu.VMEM((NPROJ + 1, CX, CY, ORB, CZ), F32),
            pltpu.VMEM((NPROJ + 1, NXY, CZ), F32),
            pltpu.VMEM((NPROJ + 1, 2 * CX, CZ), F32),
            pltpu.VMEM((2, NPROJ + 1, CY, CZ), F32),
            pltpu.VMEM((2, NPROJ + 1, 2 * CX, CZ), F32),
            pltpu.VMEM((2, NPROJ + 1, CY, ORB, CZ), F32),
            pltpu.VMEM((2, NPROJ + 1, CX, ORB, CZ), F32),
            pltpu.VMEM((2, ORB, CZ), F32),
            pltpu.VMEM((2, 4, ORB, CZ), F32),
            pltpu.VMEM((NJ * NXY, CZ), F32),
            pltpu.VMEM((NJ, CELLS), BF16),
            pltpu.VMEM((NJ, CELLS), BF16),
            pltpu.VMEM((CX, CY, ORB, CZ), F32),
            pltpu.VMEM((4 * ORB, CELLS), BF16),
            pltpu.VMEM((NG_Z, ORB, CZ), F32),
            pltpu.VMEM((NG_Z, ORB, CZ), F32),
            pltpu.VMEM((PLANE, ORB, CZ), F32),
            pltpu.VMEM((NG_Z, ORB, CZ), F32),
            pltpu.VMEM((CX, CY, ORB, CZ), F32),
            pltpu.VMEM((CX, CY, ORB, CZ), F32),
            dma, dma((DEGREE,)), dma((2, 12)), dma((2, 12)), dma((4,)), dma((4,)), dma((2,)),
            dma((NG_Z,)), dma((NG_Z,)), dma((PLANE,)), dma((PLANE,)), dma((NG_Z,)), dma((NG_Z,)),
            dma((CX,)), dma((CX,)),
        ],
        compiler_params=pltpu.CompilerParams(
            collective_id=0, has_side_effects=True, vmem_limit_bytes=60 * 1024 * 1024),
        name="filter_project",
    )(
        block.reshape(ORB * NXY, CZ), potential.reshape(NXY, CZ), proj_index, proj_value,
        proj_strength, stored.reshape(NJ * NXY, CZ))
    return projected.reshape(block.shape), intersection.T


def solution(mesh):
    in_specs = (
        P("band", "gx", "gyz", None),
        P("gx", "gyz", None),
        P(("gx", "gyz"), None),
        P(("gx", "gyz"), None),
        P(("gx", "gyz")),
        P("band", "gx", "gyz", None),
    )
    out_specs = (P("band", "gx", "gyz", None), P("band", None))
    return jax.shard_map(
        on_device, mesh=mesh, in_specs=in_specs, out_specs=out_specs, check_vma=False
    )
```

```python
import functools

import jax
import jax.numpy as jnp
from jax import lax
from jax.experimental import pallas as pl
from jax.experimental.pallas import tpu as pltpu
from jax.sharding import PartitionSpec as P

DEGREE = 8
ROUNDS = DEGREE // 2
LOW_EDGE = 0.0
CUT_EDGE = 1.0
TOP_EDGE = 10.0
HALF = (TOP_EDGE - CUT_EDGE) / 2.0
CENTER = (TOP_EDGE + CUT_EDGE) / 2.0

MESH = pl.DeviceIdType.MESH
F32 = jnp.float32
BF16 = jnp.bfloat16

CX, CY, CZ = 4, 8, 128
NXY = CX * CY
CELLS = NXY * CZ
ORB = 8
NPROJ = 8
NJ = 512
NG_X, NG_Y, NG_Z = 4, 4, 8
PLANE = NG_X * NG_Y


def recurrence():
    x = (LOW_EDGE - CENTER) / HALF
    t = [1.0, x]
    while len(t) <= DEGREE:
        t.append(2.0 * x * t[-1] - t[-2])
    ups, stays, backs = [2.0 / t[2]], [-1.0 / t[2]], [0.0]
    for m in range(1, ROUNDS):
        after = t[2 * m + 2]
        ups.append(4.0 * t[2 * m] / after)
        stays.append(-2.0 * t[2 * m] / after)
        backs.append(t[2 * m - 2] / after)
    return ups, stays, backs


UPS, STAYS, BACKS = recurrence()


def pick(k, values):
    out = jnp.float32(values[-1])
    for i in range(len(values) - 2, -1, -1):
        out = jnp.where(k == i, jnp.float32(values[i]), out)
    return out


def kernel(
    block_ref, pot_in, idx_in, val_in, str_ref, stored_ref,
    out_ref, int_ref,
    field, inner, raw, pot_ref, idx_ref, val_ref, beta, dense, edge, side_x, side_y, beta_x, beta_y, coef, coef_in, sraw, s_hi, s_lo, other, wmat, total,
    pbuf, r1, g2, q3, csend, crecv,
    in_sem, st_sem, hs_sem, hr_sem, fs_sem, fr_sem, bs_sem, br_sem, p1s, p1r, p2s, p2r, p3s, p3r, cs_sem, cr_sem,
):
    gx = lax.axis_index("gx")
    gyz = lax.axis_index("gyz")
    band = lax.axis_index("band")
    mz = lax.div(gyz, NG_Y)
    my = lax.rem(gyz, NG_Y)
    plane = gx * NG_Y + my
    left, right = lax.rem(gx + NG_X - 1, NG_X), lax.rem(gx + 1, NG_X)
    down, up = lax.rem(gyz + NG_Y * NG_Z - 1, NG_Y * NG_Z), lax.rem(gyz + 1, NG_Y * NG_Z)
    xl, xr, yl, yr = (left, gyz, band), (right, gyz, band), (gx, down, band), (gx, up, band)
    diagonal = [(x, y, band) for x in (left, right) for y in (down, up)]
    twin = (gx, gyz, 1 - band)

    def plane_peer(i):
        at = lax.rem(plane + i, PLANE)
        return at, (lax.div(at, NG_Y), mz * NG_Y + lax.rem(at, NG_Y), band)

    def z_peer(i):
        at = lax.rem(mz + i, NG_Z)
        return at, (gx, at * NG_Y + my, band)

    barrier = pltpu.get_barrier_semaphore()

    def greet(device):
        pl.semaphore_signal(barrier, inc=1, device_id=device, device_id_type=MESH)

    for device in [yl, yr, twin] + diagonal:
        greet(device)
    for i in range(1, PLANE):
        greet(plane_peer(i)[1])
    for i in range(1, NG_Z):
        greet(z_peer(i)[1])

    loads = [
        pltpu.make_async_copy(src, dst, in_sem.at[n])
        for n, (src, dst) in enumerate(
            ((idx_in, idx_ref), (val_in, val_ref), (pot_in, pot_ref), (block_ref, raw)))]
    for load in loads:
        load.start()
    rows = NJ * NXY // DEGREE

    def load_stored(k):
        at = pl.ds(pl.multiple_of(k * rows, rows), rows)
        return pltpu.make_async_copy(stored_ref.at[at], sraw.at[at], st_sem.at[k])

    def prepare():
        low_edge = lax.broadcasted_iota(jnp.int32, (NXY, 128), 0)
        at_row = lax.broadcasted_iota(jnp.int32, (CZ, 128), 0)
        for p in range(NPROJ):
            index = idx_ref[p:p + 1, :]
            value = val_ref[p:p + 1, :]
            v1 = value.astype(BF16).astype(F32)
            v2 = (value - v1).astype(BF16).astype(F32)
            v3 = value - v1 - v2
            at_xy = low_edge == lax.shift_right_logical(index, 7)
            at_z = at_row == lax.bitwise_and(index, 127)
            picks = jnp.concatenate([jnp.where(at_xy, v, 0.0) for v in (v1, v2, v3)], axis=0).astype(BF16)
            places = jnp.where(at_z, 1.0, 0.0).astype(BF16)
            got = lax.dot_general(picks, places, (((1,), (1,)), ((), ())), preferred_element_type=F32)
            dense[p] = got[0:NXY] + got[NXY:2 * NXY] + got[2 * NXY:]
        dense[NPROJ] = (pot_ref[...] + (3.0 - CENTER)) * (1.0 / HALF)
        for p in range(NPROJ + 1):
            beta[p] = jnp.broadcast_to(dense[p][:, None, :], (NXY, ORB, CZ)).reshape(CX, CY, ORB, CZ)
            edge[p, 0:4] = dense[p, pl.ds(0, CX, stride=CY), :]
            edge[p, 4:8] = dense[p, pl.ds(CY - 1, CX, stride=CY), :]

    def side_copies():
        def copy(src, dst, n, device):
            return pltpu.make_async_remote_copy(
                src_ref=src, dst_ref=dst, send_sem=fs_sem.at[n], recv_sem=fr_sem.at[n],
                device_id=device, device_id_type=MESH)
        return (
            copy(dense.at[:, 0:CY], side_x.at[1], 1, xl),
            copy(dense.at[:, NXY - CY:NXY], side_x.at[0], 0, xr),
            copy(edge, side_y.at[1], 3, yl),
            copy(edge, side_y.at[0], 2, yr),
        )

    def spread_sides():
        for p in range(NPROJ + 1):
            for side in range(2):
                beta_x[side, p] = jnp.broadcast_to(side_x[side, p][:, None, :], (CY, ORB, CZ))
                rows_y = side_y[side, p, 4:8] if side == 0 else side_y[side, p, 0:4]
                beta_y[side, p] = jnp.broadcast_to(rows_y[:, None, :], (CX, ORB, CZ))

    for load in loads[:3]:
        load.wait()
    prepare()
    loads[3].wait()
    for k in range(DEGREE):
        load_stored(k).start()

    for xy in range(NXY):
        field[0, 2 + xy // CY, 2 + xy % CY] = raw[pl.ds(xy, ORB, stride=NXY), :]
    field[1, 2:6, 2:10] = jnp.zeros((CX, CY, ORB, CZ), F32)

    pl.semaphore_wait(barrier, 7 + PLANE - 1 + NG_Z - 1)

    def halo_copies(slot):
        def copy(src, dst, n, device):
            return pltpu.make_async_remote_copy(
                src_ref=field.at[(slot,) + src], dst_ref=field.at[(slot,) + dst],
                send_sem=hs_sem.at[slot, n], recv_sem=hr_sem.at[slot, n],
                device_id=device, device_id_type=MESH)
        own_x, own_y = slice(2, 6), slice(2, 10)
        corners = (
            copy((2, 2), (6, 10), 4, diagonal[0]),
            copy((2, 9), (6, 1), 5, diagonal[1]),
            copy((5, 2), (1, 10), 6, diagonal[2]),
            copy((5, 9), (1, 1), 7, diagonal[3]),
        )
        faces = (
            copy((own_x, slice(2, 4)), (own_x, slice(10, 12)), 3, yl),
            copy((own_x, slice(8, 10)), (own_x, slice(0, 2)), 2, yr),
            copy((slice(2, 4), own_y), (slice(6, 8), own_y), 1, xl),
            copy((slice(4, 6), own_y), (slice(0, 2), own_y), 0, xr),
        )
        return corners, faces

    def coef_copies(slot):
        def copy(side, n, device):
            return pltpu.make_async_remote_copy(
                src_ref=coef.at[slot], dst_ref=coef_in.at[slot, side],
                send_sem=hs_sem.at[slot, 8 + n], recv_sem=hr_sem.at[slot, 8 + n],
                device_id=device, device_id_type=MESH)
        return copy(3, 3, yl), copy(2, 2, yr), copy(1, 1, xl), copy(0, 0, xr)

    def wait_sent(slot):
        corners, faces = halo_copies(slot)
        for c in corners + faces + coef_copies(slot):
            c.wait_send()

    lanes = lax.broadcasted_iota(jnp.int32, (1, ORB, CZ), 2)
    lane = lax.broadcasted_iota(jnp.int32, (ORB, CZ), 1)
    side_scale = 0.5 / HALF

    def along(cur):
        zero = jnp.zeros((1, ORB, CZ), F32)
        return jnp.concatenate([zero, cur[:-1]], axis=0) + jnp.concatenate([cur[1:], zero], axis=0)

    def along_z(cur):
        return (jnp.where(lanes == 0, 0.0, pltpu.roll(cur, 1, 2))
                + jnp.where(lanes == CZ - 1, 0.0, pltpu.roll(cur, CZ - 1, 2)))

    def coefficients(whole):
        out = []
        for p in range(NPROJ):
            acc = jnp.sum(whole * beta[p], axis=(0, 1))
            out.append(jnp.sum(acc, axis=1, keepdims=True) * (str_ref[p] * (1.0 / HALF)))
        return out

    def spread(weights, tiles):
        total = weights[0][None] * tiles(0)
        for p in range(1, NPROJ):
            total = total + weights[p][None] * tiles(p)
        return total

    def first_inside(slot, weights):
        for x in range(CX):
            cur = field[slot, 2 + x, 2:10]
            near = along(cur) + along_z(cur)
            if x > 0:
                near = near + field[slot, 1 + x, 2:10]
            if x < CX - 1:
                near = near + field[slot, 3 + x, 2:10]
            inner[1 + x, 1:9] = (
                beta[NPROJ, x] * cur - side_scale * near + spread(weights, lambda p: beta[p, x]))

    def first_outside(slot):
        inner[1, 1:9] = inner[1, 1:9] - side_scale * field[slot, 1, 2:10]
        inner[4, 1:9] = inner[4, 1:9] - side_scale * field[slot, 6, 2:10]
        inner[1:5, 1] = inner[1:5, 1] - side_scale * field[slot, 2:6, 1]
        inner[1:5, 8] = inner[1:5, 8] - side_scale * field[slot, 2:6, 10]
        for side in range(2):
            at = 1 if side == 0 else 6
            got = coef_in[slot, side]
            weights = [got[:, p:p + 1] for p in range(NPROJ)]
            cur = field[slot, at, 2:10]
            near = field[slot, at - 1, 2:10] + field[slot, at + 1, 2:10]
            near = near + along(cur) + along_z(cur)
            inner[at - 1, 1:9] = (
                beta_x[side, NPROJ] * cur - side_scale * near
                + spread(weights, lambda p: beta_x[side, p]))
        for side in range(2):
            at = 1 if side == 0 else 10
            got = coef_in[slot, 2 + side]
            weights = [got[:, p:p + 1] for p in range(NPROJ)]
            cur = field[slot, 2:6, at]
            near = field[slot, 2:6, at - 1] + field[slot, 2:6, at + 1]
            near = near + along(cur) + along_z(cur)
            inner[1:5, at - 1] = (
                beta_y[side, NPROJ] * cur - side_scale * near
                + spread(weights, lambda p: beta_y[side, p]))

    def swap(x):
        return pltpu.make_async_remote_copy(
            src_ref=field.at[0, 2 + x, 2:10], dst_ref=other.at[x], send_sem=bs_sem.at[x], recv_sem=br_sem.at[x],
            device_id=twin, device_id_type=MESH)

    def second(slot, ups, stays, backs, last):
        weights = coefficients(inner[1:5, 1:9])
        for x in range(CX):
            cur = inner[1 + x, 1:9]
            near = inner[x, 1:9] + inner[2 + x, 1:9] + inner[1 + x, 0:8] + inner[1 + x, 2:10]
            near = near + along_z(cur)
            twice = beta[NPROJ, x] * cur - side_scale * near + spread(weights, lambda p: beta[p, x])
            field[1 - slot, 2 + x, 2:10] = (
                ups * twice + stays * field[slot, 2 + x, 2:10] - backs * field[1 - slot, 2 + x, 2:10])

            if 0 < x < CX - 1:
                @pl.when(last)
                def _(x=x):
                    swap(x).start()

    def split_stored(k):
        load_stored(k).wait()
        first = pl.multiple_of(k * (NJ // DEGREE), NJ // DEGREE)
        base = k * rows

        def part(xy, carry):
            got = sraw[pl.ds(base + xy, NJ // DEGREE, stride=NXY), :]
            high = got.astype(BF16)
            cols = pl.ds(pl.multiple_of(xy * CZ, CZ), CZ)
            s_hi[pl.ds(first, NJ // DEGREE), cols] = high
            s_lo[pl.ds(first, NJ // DEGREE), cols] = (got - high.astype(F32)).astype(BF16)
            return carry

        lax.fori_loop(0, NXY, part, 0)

    def step(k, carry):
        slot = lax.rem(k, 2)
        corners, faces = halo_copies(slot)
        for c in corners + faces:
            c.start()

        @pl.when(k == 0)
        def _():
            for c in side_copies():
                c.start()

        weights = coefficients(field[slot, 2:6, 2:10])
        packed = jnp.zeros((ORB, CZ), F32)
        for p in range(NPROJ):
            packed = jnp.where(lane == p, weights[p], packed)
        coef[slot] = packed
        more = coef_copies(slot)
        for c in more:
            c.start()
        first_inside(slot, weights)
        split_stored(2 * k)
        split_stored(2 * k + 1)

        @pl.when(k > 0)
        def _():
            wait_sent(1 - slot)

        @pl.when(k == 0)
        def _():
            for c in side_copies():
                c.wait()
            spread_sides()

        for c in faces + more:
            c.wait_recv()
        first_outside(slot)
        ups = pick(k, UPS)
        second(slot, ups, pick(k, STAYS), pick(k, BACKS), k == ROUNDS - 1)
        for c in corners:
            c.wait_recv()
        twice = ups * (2.0 * side_scale * side_scale)
        for x, y, at_x, at_y in ((2, 2, 1, 1), (2, 9, 1, 10), (5, 2, 6, 1), (5, 9, 6, 10)):
            field[1 - slot, x, y] = field[1 - slot, x, y] + twice * field[slot, at_x, at_y]

        @pl.when(k == ROUNDS - 1)
        def _():
            swap(0).start()
            swap(CX - 1).start()

        return carry

    lax.fori_loop(0, ROUNDS, step, 0)
    wait_sent((ROUNDS - 1) % 2)

    first_core = band == 0
    def send1(c):
        return pltpu.make_async_remote_copy(
            src_ref=pbuf.at[c], dst_ref=r1.at[mz], send_sem=p1s.at[c], recv_sem=p1r.at[mz],
            device_id=(gx, c * NG_Y + my, band), device_id_type=MESH)

    nt = (((1,), (1,)), ((), ()))
    for step_x, x in enumerate((1, 2, 0, 3)):
        swap(x).wait_recv()
        for y in range(CY):
            mine, theirs = field[0, 2 + x, 2 + y], other[x, y]
            both = jnp.concatenate(
                [jnp.where(first_core, mine, theirs), jnp.where(first_core, theirs, mine)], axis=0)
            high = both.astype(BF16)
            wmat[0:16, y * CZ:(y + 1) * CZ] = high
            wmat[16:32, y * CZ:(y + 1) * CZ] = (both - high.astype(F32)).astype(BF16)
        weights = wmat[...]
        cols = slice(x * CY * CZ, (x + 1) * CY * CZ)
        got = lax.dot_general(weights, s_hi[:, cols], nt, preferred_element_type=F32)
        got = got[0:16] + got[16:32]
        got = got + lax.dot_general(weights[0:16], s_lo[:, cols], nt, preferred_element_type=F32)
        total[...] = got if step_x == 0 else total[...] + got
    for t in range(NJ // 128):
        flat = total[:, t * 128:(t + 1) * 128]
        for h in range(2):
            c = 2 * t + h
            pbuf[c] = flat[8 * h:8 * h + 8]

            @pl.when(mz == c)
            def _(c=c):
                r1[c] = pbuf[c]

            @pl.when(mz != c)
            def _(c=c):
                send1(c).start()

    def recv1(i):
        at, device = z_peer(i)
        return pltpu.make_async_remote_copy(
            src_ref=pbuf.at[at], dst_ref=r1.at[at], send_sem=p1s.at[at], recv_sem=p1r.at[at],
            device_id=device, device_id_type=MESH)

    for x in range(CX):
        swap(x).wait_send()
    for i in range(1, NG_Z):
        recv1(i).wait_recv()
    g2[plane] = jnp.sum(r1[...], axis=0)

    def send2(i):
        return pltpu.make_async_remote_copy(
            src_ref=g2.at[plane], dst_ref=g2.at[plane], send_sem=p2s.at[i], recv_sem=p2r.at[plane],
            device_id=plane_peer(i)[1], device_id_type=MESH)

    def recv2(i):
        at, device = plane_peer(i)
        return pltpu.make_async_remote_copy(
            src_ref=g2.at[plane], dst_ref=g2.at[at], send_sem=p2s.at[i], recv_sem=p2r.at[at],
            device_id=device, device_id_type=MESH)

    for i in range(1, PLANE):
        send2(i).start()
    for i in range(1, NG_Z):
        recv1(i).wait_send()
    for i in range(1, PLANE):
        recv2(i).wait_recv()
    q3[mz] = jnp.sum(g2[...], axis=0)

    def send3(i):
        return pltpu.make_async_remote_copy(
            src_ref=q3.at[mz], dst_ref=q3.at[mz], send_sem=p3s.at[i], recv_sem=p3r.at[mz],
            device_id=z_peer(i)[1], device_id_type=MESH)

    def recv3(i):
        at, device = z_peer(i)
        return pltpu.make_async_remote_copy(
            src_ref=q3.at[mz], dst_ref=q3.at[at], send_sem=p3s.at[i], recv_sem=p3r.at[at],
            device_id=device, device_id_type=MESH)

    for i in range(1, NG_Z):
        send3(i).start()
    for i in range(1, PLANE):
        send2(i).wait_send()
    for i in range(1, NG_Z):
        recv3(i).wait_recv()

    whole = jnp.concatenate(
        [jnp.concatenate([q3[2 * t], q3[2 * t + 1]], axis=0) for t in range(NJ // 128)], axis=1)
    int_ref[...] = whole
    high = whole.astype(BF16)
    low = (whole - high.astype(F32)).astype(BF16)
    left = jnp.concatenate([high, low], axis=0)
    nn = (((1,), (0,)), ((), ()))

    def give(x):
        return pltpu.make_async_remote_copy(
            src_ref=csend.at[x], dst_ref=crecv.at[x], send_sem=cs_sem.at[x], recv_sem=cr_sem.at[x],
            device_id=twin, device_id_type=MESH)

    for x in range(CX):
        cols = slice(x * CY * CZ, (x + 1) * CY * CZ)
        got = lax.dot_general(left, s_hi[:, cols], nn, preferred_element_type=F32)
        more = lax.dot_general(high, s_lo[:, cols], nn, preferred_element_type=F32)
        got = got[0:16] + got[16:32] + more
        keep = jnp.where(first_core, got[0:8], got[8:16])
        send = jnp.where(first_core, got[8:16], got[0:8])
        for y in range(CY):
            csend[x, y] = send[:, y * CZ:(y + 1) * CZ]
            field[1, 2 + x, 2 + y] = field[0, 2 + x, 2 + y] - keep[:, y * CZ:(y + 1) * CZ]
        give(x).start()
    for i in range(1, NG_Z):
        send3(i).wait_send()
    for x in range(CX):
        give(x).wait_recv()
        for y in range(CY):
            out_ref[pl.ds(x * CY + y, ORB, stride=NXY), :] = field[1, 2 + x, 2 + y] - crecv[x, y]
    for x in range(CX):
        give(x).wait_send()


def finish(a_ref, b_ref, a_out, b_out):
    a_out[...] = a_ref[...]
    b_out[...] = b_ref[...]


def on_device(block, potential, proj_index, proj_value, proj_strength, stored):
    vmem = pl.BlockSpec(memory_space=pltpu.VMEM)
    hbm = pl.BlockSpec(memory_space=pltpu.HBM)
    dma = pltpu.SemaphoreType.DMA
    projected, intersection = pl.pallas_call(
        kernel,
        out_shape=(
            jax.ShapeDtypeStruct((ORB * NXY, CZ), F32),
            jax.ShapeDtypeStruct((2 * ORB, NJ), F32),
        ),
        in_specs=[
            hbm, hbm, hbm, hbm, pl.BlockSpec(memory_space=pltpu.SMEM), hbm],
        out_specs=(vmem, vmem),
        scratch_shapes=[
            pltpu.VMEM((2, CX + 4, CY + 4, ORB, CZ), F32),
            pltpu.VMEM((CX + 2, CY + 2, ORB, CZ), F32),
            pltpu.VMEM((ORB * NXY, CZ), F32),
            pltpu.VMEM((NXY, CZ), F32),
            pltpu.VMEM((NPROJ, 128), jnp.int32),
            pltpu.VMEM((NPROJ, 128), F32),
            pltpu.VMEM((NPROJ + 1, CX, CY, ORB, CZ), F32),
            pltpu.VMEM((NPROJ + 1, NXY, CZ), F32),
            pltpu.VMEM((NPROJ + 1, 2 * CX, CZ), F32),
            pltpu.VMEM((2, NPROJ + 1, CY, CZ), F32),
            pltpu.VMEM((2, NPROJ + 1, 2 * CX, CZ), F32),
            pltpu.VMEM((2, NPROJ + 1, CY, ORB, CZ), F32),
            pltpu.VMEM((2, NPROJ + 1, CX, ORB, CZ), F32),
            pltpu.VMEM((2, ORB, CZ), F32),
            pltpu.VMEM((2, 4, ORB, CZ), F32),
            pltpu.VMEM((NJ * NXY, CZ), F32),
            pltpu.VMEM((NJ, CELLS), BF16),
            pltpu.VMEM((NJ, CELLS), BF16),
            pltpu.VMEM((CX, CY, ORB, CZ), F32),
            pltpu.VMEM((4 * ORB, CY * CZ), BF16),
            pltpu.VMEM((2 * ORB, NJ), F32),
            pltpu.VMEM((NG_Z, ORB, CZ), F32),
            pltpu.VMEM((NG_Z, ORB, CZ), F32),
            pltpu.VMEM((PLANE, ORB, CZ), F32),
            pltpu.VMEM((NG_Z, ORB, CZ), F32),
            pltpu.VMEM((CX, CY, ORB, CZ), F32),
            pltpu.VMEM((CX, CY, ORB, CZ), F32),
            dma((4,)), dma((DEGREE,)), dma((2, 12)), dma((2, 12)), dma((4,)), dma((4,)), dma((CX,)), dma((CX,)),
            dma((NG_Z,)), dma((NG_Z,)), dma((PLANE,)), dma((PLANE,)), dma((NG_Z,)), dma((NG_Z,)),
            dma((CX,)), dma((CX,)),
        ],
        compiler_params=pltpu.CompilerParams(
            collective_id=0, has_side_effects=True, vmem_limit_bytes=60 * 1024 * 1024),
        name="filter_project",
    )(
        block.reshape(ORB * NXY, CZ), potential.reshape(NXY, CZ), proj_index, proj_value,
        proj_strength, stored.reshape(NJ * NXY, CZ))
    projected, intersection = pl.pallas_call(
        finish,
        out_shape=(jax.ShapeDtypeStruct(projected.shape, F32), jax.ShapeDtypeStruct(intersection.shape, F32)),
        in_specs=[vmem, vmem],
        out_specs=(vmem, vmem),
        name="finish",
    )(projected, intersection)
    return projected.reshape(block.shape), intersection.T


def solution(mesh):
    in_specs = (
        P("band", "gx", "gyz", None),
        P("gx", "gyz", None),
        P(("gx", "gyz"), None),
        P(("gx", "gyz"), None),
        P(("gx", "gyz")),
        P("band", "gx", "gyz", None),
    )
    out_specs = (P("band", "gx", "gyz", None), P("band", None))
    return jax.shard_map(
        on_device, mesh=mesh, in_specs=in_specs, out_specs=out_specs, check_vma=False
    )
```

```python
import functools

import jax
import jax.numpy as jnp
from jax import lax
from jax.experimental import pallas as pl
from jax.experimental.pallas import tpu as pltpu
from jax.sharding import PartitionSpec as P

DEGREE = 8
LOW_EDGE = 0.0
CUT_EDGE = 1.0
TOP_EDGE = 10.0
HALF = (TOP_EDGE - CUT_EDGE) / 2.0
CENTER = (TOP_EDGE + CUT_EDGE) / 2.0

MESH = pl.DeviceIdType.MESH
F32 = jnp.float32
BF16 = jnp.bfloat16

CX, CY, CZ = 4, 8, 128
NXY = CX * CY
CELLS = NXY * CZ
ORB = 8
NPROJ = 8
NJ = 512
NG_X, NG_Y, NG_Z = 4, 4, 8
PLANE = NG_X * NG_Y


def chebyshev_at_low():
    x = (LOW_EDGE - CENTER) / HALF
    t = [1.0, x]
    while len(t) <= DEGREE:
        t.append(2.0 * x * t[-1] - t[-2])
    return t


AT_LOW = chebyshev_at_low()


def kernel(
    block_ref, pot_in, idx_in, val_in, str_in, stored_ref,
    out_ref, int_ref,
    field, inner, inner2, raw, pot_ref, idx_ref, val_ref, str_ref, beta, dense, edge, nook, side_x, side_y, side_d,
    beta_x, beta_y, beta_d, coef, coef_in, part, part_in, sraw, s_hi, s_lo, other, wmat, total,
    pbuf, r1, g2, q3, fix, csend, crecv,
    in_sem, st_sem, hs_sem, hr_sem, fs_sem, fr_sem, bs_sem, br_sem, p1s, p1r, p2s, p2r, p3s, p3r, cs_sem, cr_sem,
):
    gx = lax.axis_index("gx")
    gyz = lax.axis_index("gyz")
    band = lax.axis_index("band")
    mz = lax.div(gyz, NG_Y)
    my = lax.rem(gyz, NG_Y)
    plane = gx * NG_Y + my
    left, right = lax.rem(gx + NG_X - 1, NG_X), lax.rem(gx + 1, NG_X)
    down, up = lax.rem(gyz + NG_Y * NG_Z - 1, NG_Y * NG_Z), lax.rem(gyz + 1, NG_Y * NG_Z)
    xl, xr, yl, yr = (left, gyz, band), (right, gyz, band), (gx, down, band), (gx, up, band)
    diagonal = [(x, y, band) for x in (left, right) for y in (down, up)]
    x2 = (lax.rem(gx + 2, NG_X), gyz, band)
    down2 = (gx, lax.rem(gyz + NG_Y * NG_Z - 2, NG_Y * NG_Z), band)
    up2 = (gx, lax.rem(gyz + 2, NG_Y * NG_Z), band)
    twin = (gx, gyz, 1 - band)

    def plane_peer(i):
        at = lax.rem(plane + i, PLANE)
        return at, (lax.div(at, NG_Y), mz * NG_Y + lax.rem(at, NG_Y), band)

    def z_peer(i):
        at = lax.rem(mz + i, NG_Z)
        return at, (gx, at * NG_Y + my, band)

    barrier = pltpu.get_barrier_semaphore()

    def greet(device):
        pl.semaphore_signal(barrier, inc=1, device_id=device, device_id_type=MESH)

    for device in diagonal + [yl, yr, down2, up2, twin]:
        greet(device)
    for i in range(1, PLANE):
        greet(plane_peer(i)[1])
    for i in range(1, NG_Z):
        greet(z_peer(i)[1])

    loads = [
        pltpu.make_async_copy(src, dst, in_sem.at[n])
        for n, (src, dst) in enumerate(
            ((idx_in, idx_ref), (val_in, val_ref), (pot_in, pot_ref), (str_in, str_ref), (block_ref, raw)))]
    for load in loads:
        load.start()
    def load_stored(xy):
        return pltpu.make_async_copy(stored_ref.at[:, xy], sraw.at[xy], st_sem.at[xy])


    def prepare():
        edge[...] = jnp.zeros(edge.shape, F32)
        nook[...] = jnp.zeros(nook.shape, F32)
        low_edge = lax.broadcasted_iota(jnp.int32, (NXY, 128), 0)
        at_row = lax.broadcasted_iota(jnp.int32, (CZ, 128), 0)
        for p in range(NPROJ):
            index = idx_ref[p:p + 1, :]
            value = val_ref[p:p + 1, :] * jnp.sqrt(jnp.full((1, 128), str_ref[p] * (1.0 / HALF), F32))
            v1 = value.astype(BF16).astype(F32)
            v2 = (value - v1).astype(BF16).astype(F32)
            v3 = value - v1 - v2
            at_xy = low_edge == lax.shift_right_logical(index, 7)
            at_z = at_row == lax.bitwise_and(index, 127)
            picks = jnp.concatenate([jnp.where(at_xy, v, 0.0) for v in (v1, v2, v3)], axis=0).astype(BF16)
            places = jnp.where(at_z, 1.0, 0.0).astype(BF16)
            got = lax.dot_general(picks, places, (((1,), (1,)), ((), ())), preferred_element_type=F32)
            dense[p] = got[0:NXY] + got[NXY:2 * NXY] + got[2 * NXY:]
        dense[NPROJ] = (pot_ref[...] + (3.0 - CENTER)) * (1.0 / HALF)
        for p in range(NPROJ + 1):
            beta[p] = jnp.broadcast_to(dense[p][:, None, :], (NXY, ORB, CZ)).reshape(CX, CY, ORB, CZ)
            for layer in range(2):
                for side, y in ((0, layer), (1, CY - 1 - layer)):
                    edge[layer, side, CX * p:CX * p + CX] = dense[p, pl.ds(y, CX, stride=CY), :]
            for n, row in enumerate((0, CY - 1, NXY - CY, NXY - 1)):
                nook[n, p:p + 1] = dense[p, row:row + 1]

    def side_copies(layer):
        def copy(src, dst, n, device):
            return pltpu.make_async_remote_copy(
                src_ref=src, dst_ref=dst, send_sem=fs_sem.at[4 * layer + n], recv_sem=fr_sem.at[4 * layer + n],
                device_id=device, device_id_type=MESH)

        def x_rows(plane):
            return slice(CY * plane, CY * plane + CY)

        return (
            copy(edge.at[layer, 0], side_y.at[1, layer], 3, yl),
            copy(edge.at[layer, 1], side_y.at[0, layer], 2, yr),
            copy(dense.at[:, x_rows(layer)], side_x.at[1, :, x_rows(layer)], 1, xl),
            copy(dense.at[:, x_rows(CX - 1 - layer)], side_x.at[0, :, x_rows(1 - layer)], 0, xr),
        )

    def diagonal_copies():
        def copy(n):
            return pltpu.make_async_remote_copy(
                src_ref=nook.at[n], dst_ref=side_d.at[3 - n], send_sem=fs_sem.at[8 + n], recv_sem=fr_sem.at[8 + n],
                device_id=diagonal[n], device_id_type=MESH)
        return copy(0), copy(1), copy(2), copy(3)

    def spread_sides(layer):
        for p in range(NPROJ + 1):
            for side in range(2):
                n = layer if side == 1 else 1 - layer
                got = side_x[side, p, CY * n:CY * n + CY]
                beta_x[side, p, n] = jnp.broadcast_to(got[:, None, :], (CY, ORB, CZ))
                got = side_y[side, layer, CX * p:CX * p + CX]
                beta_y[side, p, :, n] = jnp.broadcast_to(got[:, None, :], (CX, ORB, CZ))

    def spread_diagonals():
        for p in range(NPROJ + 1):
            for n in range(4):
                beta_d[n, p] = jnp.broadcast_to(side_d[n, p:p + 1], (ORB, CZ))

    for xy in range(NXY):
        load_stored(xy).start()
    for load in loads[:4]:
        load.wait()
    prepare()
    loads[4].wait()

    for xy in range(NXY):
        field[0, 3 + xy // CY, 3 + xy % CY] = raw[pl.ds(xy, ORB, stride=NXY), :]

    def split_stored(k):
        def part(n, carry):
            xy = 4 * k + n
            load_stored(xy).wait()
            got = sraw[xy]
            high = got.astype(BF16)
            cols = pl.ds(pl.multiple_of(xy * CZ, CZ), CZ)
            s_hi[:, cols] = high
            s_lo[:, cols] = (got - high.astype(F32)).astype(BF16)
            return carry

        lax.fori_loop(0, 4, part, 0)

    pl.semaphore_wait(barrier, 9 + PLANE - 1 + NG_Z - 1)

    def halo_copies(slot, depth):
        def copy(src, dst, n, device):
            return pltpu.make_async_remote_copy(
                src_ref=field.at[(slot,) + src], dst_ref=field.at[(slot,) + dst],
                send_sem=hs_sem.at[slot, n], recv_sem=hr_sem.at[slot, n],
                device_id=device, device_id_type=MESH)
        own_x, own_y = slice(3, 7), slice(3, 11)
        low, high, n = 3, 3 + CX, depth - 1
        low_y, high_y = 3, 3 + CY
        x_low, x_high, y_low, y_high = (
            slice(low, low + n), slice(high - n, high), slice(low_y, low_y + n), slice(high_y - n, high_y))
        x_over, x_under, y_over, y_under = (
            slice(high, high + n), slice(low - n, low), slice(high_y, high_y + n), slice(low_y - n, low_y))
        corners = (
            copy((x_low, y_low), (x_over, y_over), 4, diagonal[0]),
            copy((x_low, y_high), (x_over, y_under), 5, diagonal[1]),
            copy((x_high, y_low), (x_under, y_over), 6, diagonal[2]),
            copy((x_high, y_high), (x_under, y_under), 7, diagonal[3]),
        )
        faces_y = (
            copy((own_x, slice(3, 3 + depth)), (own_x, slice(11, 11 + depth)), 3, yl),
            copy((own_x, slice(11 - depth, 11)), (own_x, slice(3 - depth, 3)), 2, yr),
        )
        faces_x = (
            copy((slice(3, 3 + depth), own_y), (slice(7, 7 + depth), own_y), 1, xl),
            copy((slice(7 - depth, 7), own_y), (slice(3 - depth, 3), own_y), 0, xr),
        )
        return corners, faces_y, faces_x

    def coef_copies(slot, count):
        def copy(place, device):
            return pltpu.make_async_remote_copy(
                src_ref=coef.at[slot], dst_ref=coef_in.at[slot, place],
                send_sem=hs_sem.at[slot, 8 + place], recv_sem=hr_sem.at[slot, 8 + place],
                device_id=device, device_id_type=MESH)
        return [copy(place, device) for place, device in (
            (7, diagonal[0]), (6, diagonal[1]), (5, diagonal[2]), (4, diagonal[3]),
            (10, down2), (9, up2), (8, x2), (3, yl), (2, yr), (1, xl), (0, xr))[11 - count:]]

    def part_copies(slot):
        def copy(place, device):
            return pltpu.make_async_remote_copy(
                src_ref=part.at[slot], dst_ref=part_in.at[slot, place],
                send_sem=hs_sem.at[slot, 19 + place], recv_sem=hr_sem.at[slot, 19 + place],
                device_id=device, device_id_type=MESH)
        return [copy(place, device) for place, device in ((3, yl), (2, yr), (1, xl), (0, xr))]

    lanes = lax.broadcasted_iota(jnp.int32, (1, ORB, CZ), 2)
    lane = lax.broadcasted_iota(jnp.int32, (ORB, CZ), 1)
    side_scale = 0.5 / HALF

    def along(cur):
        zero = jnp.zeros((1, ORB, CZ), F32)
        return jnp.concatenate([zero, cur[:-1]], axis=0) + jnp.concatenate([cur[1:], zero], axis=0)

    def along_z(cur):
        return (jnp.where(lanes == 0, 0.0, pltpu.roll(cur, 1, cur.ndim - 1))
                + jnp.where(lanes == CZ - 1, 0.0, pltpu.roll(cur, CZ - 1, cur.ndim - 1)))

    def dot_tiles(values, tiles):
        return [jnp.sum(jnp.sum(values * tiles(p), axis=tuple(range(values.ndim - 2))), axis=1, keepdims=True)
                for p in range(NPROJ)]

    def pack(columns):
        packed = jnp.zeros((ORB, CZ), F32)
        for n, column in enumerate(columns):
            packed = jnp.where(lane == n, column, packed)
        return packed

    def unpack(tile):
        return [tile[:, p:p + 1] for p in range(NPROJ)]

    def spread(weights, tiles):
        total = weights[0] * tiles(0)
        for p in range(1, NPROJ):
            total = total + weights[p] * tiles(p)
        return total

    def own_coefficients(values):
        return dot_tiles(values, lambda p: beta[p])

    def inside(slot, weights, x):
        cur = field[slot, 3 + x, 3:11]
        near = along(cur) + along_z(cur)
        if x > 0:
            near = near + field[slot, 2 + x, 3:11]
        if x < CX - 1:
            near = near + field[slot, 4 + x, 3:11]
        return beta[NPROJ, x] * cur - side_scale * near + spread(weights, lambda p: beta[p, x])

    def add_halo(slot):
        inner[2, 2:10] = inner[2, 2:10] - side_scale * field[slot, 2, 3:11]
        inner[5, 2:10] = inner[5, 2:10] - side_scale * field[slot, 7, 3:11]
        inner[2:6, 2] = inner[2:6, 2] - side_scale * field[slot, 3:7, 2]
        inner[2:6, 9] = inner[2:6, 9] - side_scale * field[slot, 3:7, 11]

    def first_layer(slot):
        for side, at in ((0, 2), (1, 7)):
            cur = field[slot, at, 3:11]
            near = field[slot, at - 1, 3:11] + field[slot, at + 1, 3:11] + along(cur) + along_z(cur)
            inner[at - 1, 2:10] = (
                beta_x[side, NPROJ, 1 - side] * cur - side_scale * near
                + spread(unpack(coef_in[slot, side]), lambda p: beta_x[side, p, 1 - side]))
        for side, at in ((0, 2), (1, 11)):
            cur = field[slot, 3:7, at]
            near = field[slot, 3:7, at - 1] + field[slot, 3:7, at + 1] + along(cur) + along_z(cur)
            inner[2:6, at - 1] = (
                beta_y[side, NPROJ, :, 1 - side] * cur - side_scale * near
                + spread(unpack(coef_in[slot, 2 + side]), lambda p: beta_y[side, p, :, 1 - side]))

    def own_x_of_inner(x, weights):
        cur = inner[2 + x, 2:10]
        near = inner[1 + x, 2:10] + inner[3 + x, 2:10] + inner[2 + x, 1:9] + inner[2 + x, 3:11]
        near = near + along_z(cur)
        return beta[NPROJ, x] * cur - side_scale * near + spread(weights, lambda p: beta[p, x])

    def degree_two():
        weights = own_coefficients(inner[2:6, 2:10])
        for x in range(CX):
            field[1, 3 + x, 3:11] = (
                (2.0 / AT_LOW[2]) * own_x_of_inner(x, weights) - (1.0 / AT_LOW[2]) * field[0, 3 + x, 3:11])

    def outer_layers(slot):
        for side, at in ((0, 1), (1, 7)):
            cur = field[slot, at:at + 2, 3:11]
            near = field[slot, at - 1:at + 1, 3:11] + field[slot, at + 1:at + 3, 3:11] + along_z(cur)
            near = near + field[slot, at:at + 2, 2:10] + field[slot, at:at + 2, 4:12]
            inner[at - 1:at + 1, 2:10] = (
                beta_x[side, NPROJ] * cur - side_scale * near
                + spread(unpack(coef_in[slot, side]), lambda p: beta_x[side, p]))
        for side, at in ((0, 1), (1, 11)):
            cur = field[slot, 3:7, at:at + 2]
            near = field[slot, 3:7, at - 1:at + 1] + field[slot, 3:7, at + 1:at + 3] + along_z(cur)
            near = near + field[slot, 2:6, at:at + 2] + field[slot, 4:8, at:at + 2]
            inner[2:6, at - 1:at + 1] = (
                beta_y[side, NPROJ] * cur - side_scale * near
                + spread(unpack(coef_in[slot, 2 + side]), lambda p: beta_y[side, p]))
        for n, (x, y) in enumerate(((2, 2), (2, 11), (7, 2), (7, 11))):
            cur = field[slot, x, y]
            near = field[slot, x - 1, y] + field[slot, x + 1, y] + field[slot, x, y - 1] + field[slot, x, y + 1]
            near = near + along_z(cur[None])[0]
            inner[x - 1, y - 1] = (
                beta_d[n, NPROJ] * cur - side_scale * near
                + spread(unpack(coef_in[slot, 4 + n]), lambda p: beta_d[n, p]))

    XL, XR, YL, YR = 1, 2, 3, 4

    def group(tile, n):
        return pltpu.roll(tile, CZ - 8 * n, 1)

    def next_coefficients(slot):
        got = [coef_in[slot, place] for place in range(11)]
        mine = coef[slot]
        own = group(got[0], XR) + group(got[1], XL) + group(got[2], YR) + group(got[3], YL)
        low_x = group(mine, XL) + group(got[8], XR) + group(got[4], YR) + group(got[5], YL)
        high_x = group(mine, XR) + group(got[8], XL) + group(got[6], YR) + group(got[7], YL)
        low_y = group(mine, YL) + group(got[9], YR) + group(got[4], XR) + group(got[6], XL)
        high_y = group(mine, YR) + group(got[10], YL) + group(got[5], XR) + group(got[7], XL)
        out = [unpack(part[slot] - side_scale * own)]
        for place, terms in enumerate((low_x, high_x, low_y, high_y)):
            out.append(unpack(part_in[slot, place] - side_scale * terms))
        return out

    def middle(slot, weights):
        for x in range(CX):
            inner2[1 + x, 1:9] = 2.0 * own_x_of_inner(x, weights[0]) - field[slot, 3 + x, 3:11]
        for side, at in ((0, 1), (1, 6)):
            cur = inner[at, 2:10]
            near = inner[at - 1, 2:10] + inner[at + 1, 2:10] + inner[at, 1:9] + inner[at, 3:11] + along_z(cur)
            got = (beta_x[side, NPROJ, 1 - side] * cur - side_scale * near
                   + spread(weights[1 + side], lambda p: beta_x[side, p, 1 - side]))
            inner2[at - 1, 1:9] = 2.0 * got - field[slot, at + 1, 3:11]
        for side, at in ((0, 1), (1, 10)):
            cur = inner[2:6, at]
            near = inner[2:6, at - 1] + inner[2:6, at + 1] + inner[1:5, at] + inner[3:7, at] + along_z(cur)
            got = (beta_y[side, NPROJ, :, 1 - side] * cur - side_scale * near
                   + spread(weights[3 + side], lambda p: beta_y[side, p, :, 1 - side]))
            inner2[1:5, at - 1] = 2.0 * got - field[slot, 3:7, at + 1]

    def swap(x):
        return pltpu.make_async_remote_copy(
            src_ref=field.at[1, 3 + x, 3:11], dst_ref=other.at[x], send_sem=bs_sem.at[x], recv_sem=br_sem.at[x],
            device_id=twin, device_id_type=MESH)

    def degree_three(slot, scale, back, last):
        weights = own_coefficients(inner2[1:5, 1:9])
        for x in range(CX):
            cur = inner2[1 + x, 1:9]
            near = inner2[x, 1:9] + inner2[2 + x, 1:9] + inner2[1 + x, 0:8] + inner2[1 + x, 2:10]
            near = near + along_z(cur)
            got = beta[NPROJ, x] * cur - side_scale * near + spread(weights, lambda p: beta[p, x])
            got = 2.0 * got - inner[2 + x, 2:10]
            field[1 - slot, 3 + x, 3:11] = scale * got - back * field[1 - slot, 3 + x, 3:11]

            @pl.when(last)
            def _(x=x):
                swap(x).start()

    def wait_sent(slot):
        corners, faces_y, faces_x = halo_copies(slot, 3)
        for c in corners + faces_y + faces_x + tuple(coef_copies(slot, 11)) + tuple(part_copies(slot)):
            c.wait_send()

    def start(copies):
        for c in copies:
            c.start()

    corners, faces_y, faces_x = halo_copies(0, 2)
    start(corners + faces_y)
    weights = own_coefficients(field[0, 3:7, 3:11])
    coef[0] = pack(weights)
    tiles = coef_copies(0, 4)
    start(tiles)
    near_sides, next_sides, far_sides = side_copies(0), side_copies(1), diagonal_copies()
    start(near_sides[:2])
    start(faces_x)
    start(near_sides[2:])
    for x in range(CX):
        inner[2 + x, 2:10] = inside(0, weights, x)
    split_stored(0)
    start(next_sides + far_sides)
    split_stored(1)
    for c in near_sides:
        c.wait_recv()
    spread_sides(0)
    for c in faces_x + faces_y + tuple(tiles):
        c.wait_recv()
    add_halo(0)
    first_layer(0)
    degree_two()
    for c in corners:
        c.wait_recv()
    twice = (2.0 / AT_LOW[2]) * (2.0 * side_scale * side_scale)
    for x, y, at_x, at_y in ((3, 3, 2, 2), (3, 10, 2, 11), (6, 3, 7, 2), (6, 10, 7, 11)):
        field[1, x, y] = field[1, x, y] + twice * field[0, at_x, at_y]

    def step(k, carry):
        slot = 1 - k
        corners, faces_y, faces_x = halo_copies(slot, 3)
        start(corners)
        weights = own_coefficients(field[slot, 3:7, 3:11])
        columns = list(weights)
        for side, at in ((0, 3), (1, 6)):
            columns += dot_tiles(field[slot, at, 3:11], lambda p: beta_x[side, p, 1 - side])
        for side, at in ((0, 3), (1, 10)):
            columns += dot_tiles(field[slot, 3:7, at], lambda p: beta_y[side, p, :, 1 - side])
        coef[slot] = pack(columns)
        tiles = coef_copies(slot, 11)
        start(tiles)
        start(faces_y)

        @pl.when(k == 0)
        def _():
            corners, faces_y, faces_x = halo_copies(0, 2)
            for c in corners + faces_y + faces_x + tuple(coef_copies(0, 4)):
                c.wait_send()
            field[0, 3:7, 3:11] = inner[2:6, 2:10]

        for x in range(CX):
            inner[2 + x, 2:10] = inside(slot, weights, x)
        part[slot] = pack(own_coefficients(inner[2:6, 2:10]))
        parts = part_copies(slot)
        start(parts[:2])
        start(faces_x)
        start(parts[2:])

        @pl.when(k == 0)
        def _():
            for c in near_sides + next_sides + far_sides:
                c.wait_send()
            for c in next_sides + far_sides:
                c.wait_recv()
            spread_sides(1)
            spread_diagonals()

        for n in range(3):
            split_stored(2 + 3 * k + n)

        @pl.when(k == 1)
        def _():
            wait_sent(1)

        for c in faces_x + faces_y + tuple(tiles) + tuple(parts) + corners:
            c.wait_recv()
        add_halo(slot)
        outer_layers(slot)
        middle(slot, next_coefficients(slot))
        scale = jnp.where(k == 0, 2.0 * AT_LOW[2] / AT_LOW[5], 2.0 * AT_LOW[5] / AT_LOW[8])
        back = jnp.where(k == 0, 1.0 / AT_LOW[5], AT_LOW[2] / AT_LOW[8])
        degree_three(slot, scale, back, k == 1)
        return carry

    lax.fori_loop(0, 2, step, 0)
    wait_sent(0)

    first_core = band == 0
    def send1(c):
        return pltpu.make_async_remote_copy(
            src_ref=pbuf.at[c], dst_ref=r1.at[mz], send_sem=p1s.at[c], recv_sem=p1r.at[mz],
            device_id=(gx, c * NG_Y + my, band), device_id_type=MESH)

    nt = (((1,), (1,)), ((), ()))
    for x in range(CX):
        swap(x).wait_recv()
        for y in range(CY):
            mine, theirs = field[1, 3 + x, 3 + y], other[x, y]
            both = jnp.concatenate(
                [jnp.where(first_core, mine, theirs), jnp.where(first_core, theirs, mine)], axis=0)
            high = both.astype(BF16)
            wmat[0:16, y * CZ:(y + 1) * CZ] = high
            wmat[16:32, y * CZ:(y + 1) * CZ] = (both - high.astype(F32)).astype(BF16)
        weights = wmat[...]
        cols = slice(x * CY * CZ, (x + 1) * CY * CZ)
        got = lax.dot_general(weights, s_hi[:, cols], nt, preferred_element_type=F32)
        got = got[0:16] + got[16:32]
        got = got + lax.dot_general(weights[0:16], s_lo[:, cols], nt, preferred_element_type=F32)
        total[...] = got if x == 0 else total[...] + got
    for t in range(NJ // 128):
        flat = total[:, t * 128:(t + 1) * 128]
        for h in range(2):
            c = 2 * t + h
            pbuf[c] = flat[8 * h:8 * h + 8]

            @pl.when(mz == c)
            def _(c=c):
                r1[c] = pbuf[c]

            @pl.when(mz != c)
            def _(c=c):
                send1(c).start()

    def recv1(i):
        at, device = z_peer(i)
        return pltpu.make_async_remote_copy(
            src_ref=pbuf.at[at], dst_ref=r1.at[at], send_sem=p1s.at[at], recv_sem=p1r.at[at],
            device_id=device, device_id_type=MESH)

    for x in range(CX):
        swap(x).wait_send()
    for i in range(1, NG_Z):
        recv1(i).wait_recv()
    g2[plane] = jnp.sum(r1[...], axis=0)

    def send2(i):
        return pltpu.make_async_remote_copy(
            src_ref=g2.at[plane], dst_ref=g2.at[plane], send_sem=p2s.at[i], recv_sem=p2r.at[plane],
            device_id=plane_peer(i)[1], device_id_type=MESH)

    def recv2(i):
        at, device = plane_peer(i)
        return pltpu.make_async_remote_copy(
            src_ref=g2.at[plane], dst_ref=g2.at[at], send_sem=p2s.at[i], recv_sem=p2r.at[at],
            device_id=device, device_id_type=MESH)

    for i in range(1, PLANE):
        send2(i).start()
    for i in range(1, NG_Z):
        recv1(i).wait_send()
    for i in range(1, PLANE):
        recv2(i).wait_recv()
    q3[mz] = jnp.sum(g2[...], axis=0)

    def send3(i):
        return pltpu.make_async_remote_copy(
            src_ref=q3.at[mz], dst_ref=q3.at[mz], send_sem=p3s.at[i], recv_sem=p3r.at[mz],
            device_id=z_peer(i)[1], device_id_type=MESH)

    for i in range(1, NG_Z):
        send3(i).start()
    for i in range(1, PLANE):
        send2(i).wait_send()
    nn = (((1,), (0,)), ((), ()))

    def arrived(c):
        pltpu.make_async_remote_copy(
            src_ref=q3.at[mz], dst_ref=q3.at[c], send_sem=p3s.at[0], recv_sem=p3r.at[c],
            device_id=(gx, c * NG_Y + my, band), device_id_type=MESH).wait_recv()

    def give(x):
        return pltpu.make_async_remote_copy(
            src_ref=csend.at[x], dst_ref=crecv.at[x], send_sem=cs_sem.at[x], recv_sem=cr_sem.at[x],
            device_id=twin, device_id_type=MESH)

    pairs = NG_Z // 2
    for n, ahead in enumerate((0, 1, 3, 2)):
        pair = lax.rem(lax.div(mz, 2) + ahead, pairs)
        for h in range(2):
            @pl.when(2 * pair + h != mz)
            def _(h=h):
                arrived(2 * pair + h)

        whole = jnp.concatenate([q3[2 * pair], q3[2 * pair + 1]], axis=0)
        rows_j = pl.ds(pl.multiple_of(pair * 128, 128), 128)
        int_ref[:, rows_j] = whole
        high = whole.astype(BF16)
        low = (whole - high.astype(F32)).astype(BF16)
        left_side = jnp.concatenate([high, low], axis=0)
        for x in range(CX):
            cols = slice(x * CY * CZ, (x + 1) * CY * CZ)
            got = lax.dot_general(left_side, s_hi[rows_j, cols], nn, preferred_element_type=F32)
            more = lax.dot_general(high, s_lo[rows_j, cols], nn, preferred_element_type=F32)
            got = got[0:16] + got[16:32] + more
            if n > 0:
                got = got + fix[:, cols]
            if n < pairs - 1:
                fix[:, cols] = got
                continue
            keep = jnp.where(first_core, got[0:8], got[8:16])
            send = jnp.where(first_core, got[8:16], got[0:8])
            for y in range(CY):
                csend[x, y] = send[:, y * CZ:(y + 1) * CZ]
                field[0, 3 + x, 3 + y] = field[1, 3 + x, 3 + y] - keep[:, y * CZ:(y + 1) * CZ]
            give(x).start()
    for i in range(1, NG_Z):
        send3(i).wait_send()
    for x in range(CX):
        give(x).wait_recv()
        for y in range(CY):
            out_ref[pl.ds(x * CY + y, ORB, stride=NXY), :] = field[0, 3 + x, 3 + y] - crecv[x, y]
    for x in range(CX):
        give(x).wait_send()


def finish(a_ref, b_ref, a_out, b_out):
    a_out[...] = a_ref[...]
    b_out[...] = b_ref[...]


def on_device(block, potential, proj_index, proj_value, proj_strength, stored):
    vmem = pl.BlockSpec(memory_space=pltpu.VMEM)
    hbm = pl.BlockSpec(memory_space=pltpu.HBM)
    dma = pltpu.SemaphoreType.DMA
    projected, intersection = pl.pallas_call(
        kernel,
        out_shape=(
            jax.ShapeDtypeStruct((ORB * NXY, CZ), F32),
            jax.ShapeDtypeStruct((2 * ORB, NJ), F32),
        ),
        in_specs=[
            hbm, hbm, hbm, hbm, hbm, hbm],
        out_specs=(vmem, vmem),
        scratch_shapes=[
            pltpu.VMEM((2, CX + 6, CY + 6, ORB, CZ), F32),
            pltpu.VMEM((CX + 4, CY + 4, ORB, CZ), F32),
            pltpu.VMEM((CX + 2, CY + 2, ORB, CZ), F32),
            pltpu.VMEM((ORB * NXY, CZ), F32),
            pltpu.VMEM((NXY, CZ), F32),
            pltpu.VMEM((NPROJ, 128), jnp.int32),
            pltpu.VMEM((NPROJ, 128), F32),
            pltpu.SMEM((NPROJ,), F32),
            pltpu.VMEM((NPROJ + 1, CX, CY, ORB, CZ), F32),
            pltpu.VMEM((NPROJ + 1, NXY, CZ), F32),
            pltpu.VMEM((2, 2, 40, CZ), F32),
            pltpu.VMEM((4, 16, CZ), F32),
            pltpu.VMEM((2, NPROJ + 1, 2 * CY, CZ), F32),
            pltpu.VMEM((2, 2, 40, CZ), F32),
            pltpu.VMEM((4, 16, CZ), F32),
            pltpu.VMEM((2, NPROJ + 1, 2, CY, ORB, CZ), F32),
            pltpu.VMEM((2, NPROJ + 1, CX, 2, ORB, CZ), F32),
            pltpu.VMEM((4, NPROJ + 1, ORB, CZ), F32),
            pltpu.VMEM((2, ORB, CZ), F32),
            pltpu.VMEM((2, 11, ORB, CZ), F32),
            pltpu.VMEM((2, ORB, CZ), F32),
            pltpu.VMEM((2, 4, ORB, CZ), F32),
            pltpu.VMEM((NXY, NJ, CZ), F32),
            pltpu.VMEM((NJ, CELLS), BF16),
            pltpu.VMEM((NJ, CELLS), BF16),
            pltpu.VMEM((CX, CY, ORB, CZ), F32),
            pltpu.VMEM((4 * ORB, CY * CZ), BF16),
            pltpu.VMEM((2 * ORB, NJ), F32),
            pltpu.VMEM((NG_Z, ORB, CZ), F32),
            pltpu.VMEM((NG_Z, ORB, CZ), F32),
            pltpu.VMEM((PLANE, ORB, CZ), F32),
            pltpu.VMEM((NG_Z, ORB, CZ), F32),
            pltpu.VMEM((2 * ORB, CELLS), F32),
            pltpu.VMEM((CX, CY, ORB, CZ), F32),
            pltpu.VMEM((CX, CY, ORB, CZ), F32),
            dma((5,)), dma((NXY,)), dma((2, 23)), dma((2, 23)), dma((12,)), dma((12,)), dma((CX,)), dma((CX,)),
            dma((NG_Z,)), dma((NG_Z,)), dma((PLANE,)), dma((PLANE,)), dma((NG_Z,)), dma((NG_Z,)),
            dma((CX,)), dma((CX,)),
        ],
        compiler_params=pltpu.CompilerParams(
            collective_id=0, has_side_effects=True, vmem_limit_bytes=60 * 1024 * 1024),
        name="filter_project",
    )(
        block.reshape(ORB * NXY, CZ), potential.reshape(NXY, CZ), proj_index, proj_value,
        proj_strength, stored.reshape(NJ, NXY, CZ))
    projected, intersection = pl.pallas_call(
        finish,
        out_shape=(jax.ShapeDtypeStruct(projected.shape, F32), jax.ShapeDtypeStruct(intersection.shape, F32)),
        in_specs=[vmem, vmem],
        out_specs=(vmem, vmem),
        name="finish",
    )(projected, intersection)
    return projected.reshape(block.shape), intersection.T


def solution(mesh):
    in_specs = (
        P("band", "gx", "gyz", None),
        P("gx", "gyz", None),
        P(("gx", "gyz"), None),
        P(("gx", "gyz"), None),
        P(("gx", "gyz")),
        P("band", "gx", "gyz", None),
    )
    out_specs = (P("band", "gx", "gyz", None), P("band", None))
    return jax.shard_map(
        on_device, mesh=mesh, in_specs=in_specs, out_specs=out_specs, check_vma=False
    )
```

```python
import functools

import jax
import jax.numpy as jnp
from jax import lax
from jax.experimental import pallas as pl
from jax.experimental.pallas import tpu as pltpu
from jax.sharding import PartitionSpec as P

DEGREE = 8
LOW_EDGE = 0.0
CUT_EDGE = 1.0
TOP_EDGE = 10.0
HALF = (TOP_EDGE - CUT_EDGE) / 2.0
CENTER = (TOP_EDGE + CUT_EDGE) / 2.0

MESH = pl.DeviceIdType.MESH
F32 = jnp.float32
BF16 = jnp.bfloat16

CX, CY, CZ = 4, 8, 128
NXY = CX * CY
CELLS = NXY * CZ
ORB = 8
NPROJ = 8
NJ = 512
NG_X, NG_Y, NG_Z = 4, 4, 8
PLANE = NG_X * NG_Y


def chebyshev_at_low():
    x = (LOW_EDGE - CENTER) / HALF
    t = [1.0, x]
    while len(t) <= DEGREE:
        t.append(2.0 * x * t[-1] - t[-2])
    return t


AT_LOW = chebyshev_at_low()


def kernel(
    block_ref, pot_in, idx_in, val_in, str_in, stored_ref,
    out_ref, int_ref,
    field, inner, inner2, raw, pot_ref, idx_ref, val_ref, str_ref, beta, dense, edge, nook, side_x, side_y, side_d,
    beta_x, beta_y, beta_d, coef, coef_in, part, part_in, sraw, s_hi, s_lo, other, wmat, total,
    pbuf, r1, g2, q3, fix, csend, crecv,
    in_sem, st_sem, hs_sem, hr_sem, fs_sem, fr_sem, bs_sem, br_sem, p1s, p1r, p2s, p2r, p3s, p3r, cs_sem, cr_sem,
):
    gx = lax.axis_index("gx")
    gyz = lax.axis_index("gyz")
    band = lax.axis_index("band")
    mz = lax.div(gyz, NG_Y)
    my = lax.rem(gyz, NG_Y)
    plane = gx * NG_Y + my
    left, right = lax.rem(gx + NG_X - 1, NG_X), lax.rem(gx + 1, NG_X)
    down, up = lax.rem(gyz + NG_Y * NG_Z - 1, NG_Y * NG_Z), lax.rem(gyz + 1, NG_Y * NG_Z)
    xl, xr, yl, yr = (left, gyz, band), (right, gyz, band), (gx, down, band), (gx, up, band)
    diagonal = [(x, y, band) for x in (left, right) for y in (down, up)]
    x2 = (lax.rem(gx + 2, NG_X), gyz, band)
    down2 = (gx, lax.rem(gyz + NG_Y * NG_Z - 2, NG_Y * NG_Z), band)
    up2 = (gx, lax.rem(gyz + 2, NG_Y * NG_Z), band)
    twin = (gx, gyz, 1 - band)

    def plane_peer(i):
        at = lax.rem(plane + i, PLANE)
        return at, (lax.div(at, NG_Y), mz * NG_Y + lax.rem(at, NG_Y), band)

    def z_peer(i):
        at = lax.rem(mz + i, NG_Z)
        return at, (gx, at * NG_Y + my, band)

    barrier = pltpu.get_barrier_semaphore()

    def greet(device):
        pl.semaphore_signal(barrier, inc=1, device_id=device, device_id_type=MESH)

    for device in diagonal + [yl, yr, down2, up2, twin]:
        greet(device)
    for i in range(1, PLANE):
        greet(plane_peer(i)[1])
    for i in range(1, NG_Z):
        greet(z_peer(i)[1])

    loads = [
        pltpu.make_async_copy(src, dst, in_sem.at[n])
        for n, (src, dst) in enumerate(
            ((idx_in, idx_ref), (val_in, val_ref), (pot_in, pot_ref), (str_in, str_ref), (block_ref, raw)))]
    for load in loads:
        load.start()
    def load_stored(xy):
        return pltpu.make_async_copy(stored_ref.at[:, xy], sraw.at[xy], st_sem.at[xy])


    def prepare():
        edge[...] = jnp.zeros(edge.shape, F32)
        nook[...] = jnp.zeros(nook.shape, F32)
        low_edge = lax.broadcasted_iota(jnp.int32, (NXY, 128), 0)
        at_row = lax.broadcasted_iota(jnp.int32, (CZ, 128), 0)
        for p in range(NPROJ):
            index = idx_ref[p:p + 1, :]
            value = val_ref[p:p + 1, :] * jnp.sqrt(jnp.full((1, 128), str_ref[p] * (1.0 / HALF), F32))
            v1 = value.astype(BF16).astype(F32)
            v2 = (value - v1).astype(BF16).astype(F32)
            v3 = value - v1 - v2
            at_xy = low_edge == lax.shift_right_logical(index, 7)
            at_z = at_row == lax.bitwise_and(index, 127)
            picks = jnp.concatenate([jnp.where(at_xy, v, 0.0) for v in (v1, v2, v3)], axis=0).astype(BF16)
            places = jnp.where(at_z, 1.0, 0.0).astype(BF16)
            got = lax.dot_general(picks, places, (((1,), (1,)), ((), ())), preferred_element_type=F32)
            dense[p] = got[0:NXY] + got[NXY:2 * NXY] + got[2 * NXY:]
        dense[NPROJ] = (pot_ref[...] + (3.0 - CENTER)) * (1.0 / HALF)
        for p in range(NPROJ + 1):
            beta[p] = jnp.broadcast_to(dense[p][:, None, :], (NXY, ORB, CZ)).reshape(CX, CY, ORB, CZ)
            for layer in range(2):
                for side, y in ((0, layer), (1, CY - 1 - layer)):
                    edge[layer, side, CX * p:CX * p + CX] = dense[p, pl.ds(y, CX, stride=CY), :]
            for n, row in enumerate((0, CY - 1, NXY - CY, NXY - 1)):
                nook[n, p:p + 1] = dense[p, row:row + 1]

    def side_copies(layer):
        def copy(src, dst, n, device):
            return pltpu.make_async_remote_copy(
                src_ref=src, dst_ref=dst, send_sem=fs_sem.at[4 * layer + n], recv_sem=fr_sem.at[4 * layer + n],
                device_id=device, device_id_type=MESH)

        def x_rows(plane):
            return slice(CY * plane, CY * plane + CY)

        return (
            copy(edge.at[layer, 0], side_y.at[1, layer], 3, yl),
            copy(edge.at[layer, 1], side_y.at[0, layer], 2, yr),
            copy(dense.at[:, x_rows(layer)], side_x.at[1, :, x_rows(layer)], 1, xl),
            copy(dense.at[:, x_rows(CX - 1 - layer)], side_x.at[0, :, x_rows(1 - layer)], 0, xr),
        )

    def diagonal_copies():
        def copy(n):
            return pltpu.make_async_remote_copy(
                src_ref=nook.at[n], dst_ref=side_d.at[3 - n], send_sem=fs_sem.at[8 + n], recv_sem=fr_sem.at[8 + n],
                device_id=diagonal[n], device_id_type=MESH)
        return copy(0), copy(1), copy(2), copy(3)

    def spread_sides(layer):
        for p in range(NPROJ + 1):
            for side in range(2):
                n = layer if side == 1 else 1 - layer
                got = side_x[side, p, CY * n:CY * n + CY]
                beta_x[side, p, n] = jnp.broadcast_to(got[:, None, :], (CY, ORB, CZ))
                got = side_y[side, layer, CX * p:CX * p + CX]
                beta_y[side, p, :, n] = jnp.broadcast_to(got[:, None, :], (CX, ORB, CZ))

    def spread_diagonals():
        for p in range(NPROJ + 1):
            for n in range(4):
                beta_d[n, p] = jnp.broadcast_to(side_d[n, p:p + 1], (ORB, CZ))

    for xy in range(NXY):
        load_stored(xy).start()
    for load in loads[:4]:
        load.wait()
    prepare()
    loads[4].wait()

    for xy in range(NXY):
        field[0, 3 + xy // CY, 3 + xy % CY] = raw[pl.ds(xy, ORB, stride=NXY), :]

    def split_stored(k):
        def part(n, carry):
            xy = 4 * k + n
            load_stored(xy).wait()
            got = sraw[xy]
            high = got.astype(BF16)
            cols = pl.ds(pl.multiple_of(xy * CZ, CZ), CZ)
            s_hi[:, cols] = high
            s_lo[:, cols] = (got - high.astype(F32)).astype(BF16)
            return carry

        lax.fori_loop(0, 4, part, 0)

    pl.semaphore_wait(barrier, 9 + PLANE - 1 + NG_Z - 1)

    def halo_copies(slot, depth):
        def copy(src, dst, n, device):
            return pltpu.make_async_remote_copy(
                src_ref=field.at[(slot,) + src], dst_ref=field.at[(slot,) + dst],
                send_sem=hs_sem.at[slot, n], recv_sem=hr_sem.at[slot, n],
                device_id=device, device_id_type=MESH)
        own_x, own_y = slice(3, 7), slice(3, 11)
        low, high, n = 3, 3 + CX, depth - 1
        low_y, high_y = 3, 3 + CY
        x_low, x_high, y_low, y_high = (
            slice(low, low + n), slice(high - n, high), slice(low_y, low_y + n), slice(high_y - n, high_y))
        x_over, x_under, y_over, y_under = (
            slice(high, high + n), slice(low - n, low), slice(high_y, high_y + n), slice(low_y - n, low_y))
        corners = (
            copy((x_low, y_low), (x_over, y_over), 4, diagonal[0]),
            copy((x_low, y_high), (x_over, y_under), 5, diagonal[1]),
            copy((x_high, y_low), (x_under, y_over), 6, diagonal[2]),
            copy((x_high, y_high), (x_under, y_under), 7, diagonal[3]),
        )
        faces_y = (
            copy((own_x, slice(3, 3 + depth)), (own_x, slice(11, 11 + depth)), 3, yl),
            copy((own_x, slice(11 - depth, 11)), (own_x, slice(3 - depth, 3)), 2, yr),
        )
        faces_x = (
            copy((slice(3, 3 + depth), own_y), (slice(7, 7 + depth), own_y), 1, xl),
            copy((slice(7 - depth, 7), own_y), (slice(3 - depth, 3), own_y), 0, xr),
        )
        return corners, faces_y, faces_x

    def coef_copies(slot, count):
        def copy(place, device):
            return pltpu.make_async_remote_copy(
                src_ref=coef.at[slot], dst_ref=coef_in.at[slot, place],
                send_sem=hs_sem.at[slot, 8 + place], recv_sem=hr_sem.at[slot, 8 + place],
                device_id=device, device_id_type=MESH)
        return [copy(place, device) for place, device in (
            (7, diagonal[0]), (6, diagonal[1]), (5, diagonal[2]), (4, diagonal[3]),
            (10, down2), (9, up2), (8, x2), (3, yl), (2, yr), (1, xl), (0, xr))[11 - count:]]

    def part_copies(slot):
        def copy(place, device):
            return pltpu.make_async_remote_copy(
                src_ref=part.at[slot], dst_ref=part_in.at[slot, place],
                send_sem=hs_sem.at[slot, 19 + place], recv_sem=hr_sem.at[slot, 19 + place],
                device_id=device, device_id_type=MESH)
        return [copy(place, device) for place, device in ((3, yl), (2, yr), (1, xl), (0, xr))]

    lanes = lax.broadcasted_iota(jnp.int32, (1, ORB, CZ), 2)
    lane = lax.broadcasted_iota(jnp.int32, (ORB, CZ), 1)
    side_scale = 0.5 / HALF

    def along(cur):
        zero = jnp.zeros((1,) + cur.shape[1:], F32)
        return jnp.concatenate([zero, cur[:-1]], axis=0) + jnp.concatenate([cur[1:], zero], axis=0)

    def along_z(cur):
        return (jnp.where(lanes == 0, 0.0, pltpu.roll(cur, 1, cur.ndim - 1))
                + jnp.where(lanes == CZ - 1, 0.0, pltpu.roll(cur, CZ - 1, cur.ndim - 1)))

    def dot_tiles(values, tiles):
        return [jnp.sum(jnp.sum(values * tiles(p), axis=tuple(range(values.ndim - 2))), axis=1, keepdims=True)
                for p in range(NPROJ)]

    def pack(columns):
        packed = jnp.zeros((ORB, CZ), F32)
        for n, column in enumerate(columns):
            packed = jnp.where(lane == n, column, packed)
        return packed

    def unpack(tile):
        return [tile[:, p:p + 1] for p in range(NPROJ)]

    def spread(weights, tiles):
        total = weights[0] * tiles(0)
        for p in range(1, NPROJ):
            total = total + weights[p] * tiles(p)
        return total

    def own_coefficients(values):
        return dot_tiles(values, lambda p: beta[p])

    def inside(slot, weights, x):
        cur = field[slot, 3 + x, 3:11]
        near = along(cur) + along_z(cur)
        if x > 0:
            near = near + field[slot, 2 + x, 3:11]
        if x < CX - 1:
            near = near + field[slot, 4 + x, 3:11]
        return beta[NPROJ, x] * cur - side_scale * near + spread(weights, lambda p: beta[p, x])

    def add_halo(slot):
        inner[2, 2:10] = inner[2, 2:10] - side_scale * field[slot, 2, 3:11]
        inner[5, 2:10] = inner[5, 2:10] - side_scale * field[slot, 7, 3:11]
        inner[2:6, 2] = inner[2:6, 2] - side_scale * field[slot, 3:7, 2]
        inner[2:6, 9] = inner[2:6, 9] - side_scale * field[slot, 3:7, 11]

    def first_layer(slot):
        for side, at in ((0, 2), (1, 7)):
            cur = field[slot, at, 3:11]
            near = field[slot, at - 1, 3:11] + field[slot, at + 1, 3:11] + along(cur) + along_z(cur)
            inner[at - 1, 2:10] = (
                beta_x[side, NPROJ, 1 - side] * cur - side_scale * near
                + spread(unpack(coef_in[slot, side]), lambda p: beta_x[side, p, 1 - side]))
        for side, at in ((0, 2), (1, 11)):
            cur = field[slot, 3:7, at]
            near = field[slot, 3:7, at - 1] + field[slot, 3:7, at + 1] + along(cur) + along_z(cur)
            inner[2:6, at - 1] = (
                beta_y[side, NPROJ, :, 1 - side] * cur - side_scale * near
                + spread(unpack(coef_in[slot, 2 + side]), lambda p: beta_y[side, p, :, 1 - side]))

    def own_x_of_inner(x, weights):
        cur = inner[2 + x, 2:10]
        near = inner[1 + x, 2:10] + inner[3 + x, 2:10] + inner[2 + x, 1:9] + inner[2 + x, 3:11]
        near = near + along_z(cur)
        return beta[NPROJ, x] * cur - side_scale * near + spread(weights, lambda p: beta[p, x])

    def degree_two():
        weights = own_coefficients(inner[2:6, 2:10])
        for x in range(CX):
            field[1, 3 + x, 3:11] = (
                (2.0 / AT_LOW[2]) * own_x_of_inner(x, weights) - (1.0 / AT_LOW[2]) * field[0, 3 + x, 3:11])

    def outer_layers(slot):
        for side, at in ((0, 1), (1, 7)):
            cur = field[slot, at:at + 2, 3:11]
            near = field[slot, at - 1:at + 1, 3:11] + field[slot, at + 1:at + 3, 3:11] + along_z(cur)
            near = near + jnp.stack([along(cur[0]), along(cur[1])])
            inner[at - 1:at + 1, 2:10] = (
                beta_x[side, NPROJ] * cur - side_scale * near
                + spread(unpack(coef_in[slot, side]), lambda p: beta_x[side, p]))
        for side, at in ((0, 1), (1, 11)):
            cur = field[slot, 3:7, at:at + 2]
            near = field[slot, 3:7, at - 1:at + 1] + field[slot, 3:7, at + 1:at + 3] + along_z(cur)
            near = near + along(cur)
            inner[2:6, at - 1:at + 1] = (
                beta_y[side, NPROJ] * cur - side_scale * near
                + spread(unpack(coef_in[slot, 2 + side]), lambda p: beta_y[side, p]))
    def corner_cells(slot, weights):
        added, tiles = [], []
        for x, y, own_x, own_y, out in ((2, 2, 3, 3, -1), (2, 11, 3, 10, 1), (7, 2, 6, 3, -1), (7, 11, 6, 10, 1)):
            far_x, far_y = 2 * x - own_x, y + out
            for here_x, here_y, got in ((x, own_y, (x, y)), (far_x, own_y, (far_x, y)),
                                        (own_x, y, (x, y)), (own_x, far_y, (x, far_y))):
                inner[here_x - 1, here_y - 1] = (
                    inner[here_x - 1, here_y - 1] - side_scale * field[(slot,) + got])
            more = (4.0 * side_scale * side_scale) * field[slot, x, y]
            inner2[own_x - 2, own_y - 2] = inner2[own_x - 2, own_y - 2] + more
            added.append(more)
            tiles.append((own_x - 3, own_y - 3))
        out = []
        for p in range(NPROJ):
            acc = sum(more * beta[p, x, y] for more, (x, y) in zip(added, tiles))
            out.append(weights[p] + jnp.sum(acc, axis=1, keepdims=True))
        for n, (x, y) in enumerate(((2, 2), (2, 11), (7, 2), (7, 11))):
            cur = field[slot, x, y]
            near = field[slot, x - 1, y] + field[slot, x + 1, y] + field[slot, x, y - 1] + field[slot, x, y + 1]
            near = near + along_z(cur[None])[0]
            inner[x - 1, y - 1] = (
                beta_d[n, NPROJ] * cur - side_scale * near
                + spread(unpack(coef_in[slot, 4 + n]), lambda p: beta_d[n, p]))
        return out

    XL, XR, YL, YR = 1, 2, 3, 4

    def group(tile, n):
        return pltpu.roll(tile, CZ - 8 * n, 1)

    def next_own(slot):
        near = [coef_in[slot, place] for place in range(4)]
        own = group(near[0], XR) + group(near[1], XL) + group(near[2], YR) + group(near[3], YL)
        return unpack(part[slot] - side_scale * own)

    def next_around(slot):
        got = [coef_in[slot, place] for place in range(11)]
        mine = coef[slot]
        low_x = group(mine, XL) + group(got[8], XR) + group(got[4], YR) + group(got[5], YL)
        high_x = group(mine, XR) + group(got[8], XL) + group(got[6], YR) + group(got[7], YL)
        low_y = group(mine, YL) + group(got[9], YR) + group(got[4], XR) + group(got[6], XL)
        high_y = group(mine, YR) + group(got[10], YL) + group(got[5], XR) + group(got[7], XL)
        return [unpack(part_in[slot, place] - side_scale * terms)
                for place, terms in enumerate((low_x, high_x, low_y, high_y))]

    def middle_own(slot, weights):
        for x in range(CX):
            inner2[1 + x, 1:9] = 2.0 * own_x_of_inner(x, weights) - field[slot, 3 + x, 3:11]

    def middle_around(slot, weights):
        for side, at in ((0, 1), (1, 6)):
            cur = inner[at, 2:10]
            near = inner[at - 1, 2:10] + inner[at + 1, 2:10] + inner[at, 1:9] + inner[at, 3:11] + along_z(cur)
            got = (beta_x[side, NPROJ, 1 - side] * cur - side_scale * near
                   + spread(weights[side], lambda p: beta_x[side, p, 1 - side]))
            inner2[at - 1, 1:9] = 2.0 * got - field[slot, at + 1, 3:11]
        for side, at in ((0, 1), (1, 10)):
            cur = inner[2:6, at]
            near = inner[2:6, at - 1] + inner[2:6, at + 1] + inner[1:5, at] + inner[3:7, at] + along_z(cur)
            got = (beta_y[side, NPROJ, :, 1 - side] * cur - side_scale * near
                   + spread(weights[2 + side], lambda p: beta_y[side, p, :, 1 - side]))
            inner2[1:5, at - 1] = 2.0 * got - field[slot, 3:7, at + 1]

    def swap(x):
        return pltpu.make_async_remote_copy(
            src_ref=field.at[1, 3 + x, 3:11], dst_ref=other.at[x], send_sem=bs_sem.at[x], recv_sem=br_sem.at[x],
            device_id=twin, device_id_type=MESH)

    def degree_three(slot, weights, scale, back, last):
        for x in range(CX):
            cur = inner2[1 + x, 1:9]
            near = inner2[x, 1:9] + inner2[2 + x, 1:9] + inner2[1 + x, 0:8] + inner2[1 + x, 2:10]
            near = near + along_z(cur)
            got = beta[NPROJ, x] * cur - side_scale * near + spread(weights, lambda p: beta[p, x])
            got = 2.0 * got - inner[2 + x, 2:10]
            field[1 - slot, 3 + x, 3:11] = scale * got - back * field[1 - slot, 3 + x, 3:11]

            @pl.when(last)
            def _(x=x):
                swap(x).start()

    def wait_sent(slot):
        corners, faces_y, faces_x = halo_copies(slot, 3)
        for c in corners + faces_y + faces_x + tuple(coef_copies(slot, 11)) + tuple(part_copies(slot)):
            c.wait_send()

    def start(copies):
        for c in copies:
            c.start()

    corners, faces_y, faces_x = halo_copies(0, 2)
    start(corners + faces_y)
    weights = own_coefficients(field[0, 3:7, 3:11])
    coef[0] = pack(weights)
    tiles = coef_copies(0, 4)
    start(tiles)
    near_sides, next_sides, far_sides = side_copies(0), side_copies(1), diagonal_copies()
    start(near_sides[:2])
    start(faces_x)
    start(near_sides[2:])
    for x in range(CX):
        inner[2 + x, 2:10] = inside(0, weights, x)
    split_stored(0)
    start(next_sides + far_sides)
    split_stored(1)
    for c in near_sides:
        c.wait_recv()
    spread_sides(0)
    for c in faces_x + faces_y + tuple(tiles):
        c.wait_recv()
    add_halo(0)
    first_layer(0)
    degree_two()
    for c in corners:
        c.wait_recv()
    twice = (2.0 / AT_LOW[2]) * (2.0 * side_scale * side_scale)
    for x, y, at_x, at_y in ((3, 3, 2, 2), (3, 10, 2, 11), (6, 3, 7, 2), (6, 10, 7, 11)):
        field[1, x, y] = field[1, x, y] + twice * field[0, at_x, at_y]

    def step(k, carry):
        slot = 1 - k
        corners, faces_y, faces_x = halo_copies(slot, 3)
        start(corners)
        weights = own_coefficients(field[slot, 3:7, 3:11])
        columns = list(weights)
        for side, at in ((0, 3), (1, 6)):
            columns += dot_tiles(field[slot, at, 3:11], lambda p: beta_x[side, p, 1 - side])
        for side, at in ((0, 3), (1, 10)):
            columns += dot_tiles(field[slot, 3:7, at], lambda p: beta_y[side, p, :, 1 - side])
        coef[slot] = pack(columns)
        tiles = coef_copies(slot, 11)
        start(tiles)
        start(faces_y)
        start(faces_x)

        @pl.when(k == 0)
        def _():
            corners, faces_y, faces_x = halo_copies(0, 2)
            for c in corners + faces_y + faces_x + tuple(coef_copies(0, 4)):
                c.wait_send()
            field[0, 3:7, 3:11] = inner[2:6, 2:10]

        for x in range(CX):
            inner[2 + x, 2:10] = inside(slot, weights, x)
        part[slot] = pack(own_coefficients(inner[2:6, 2:10]))
        parts = part_copies(slot)
        start(parts)

        @pl.when(k == 0)
        def _():
            for c in near_sides + next_sides + far_sides:
                c.wait_send()
            for c in next_sides + far_sides:
                c.wait_recv()
            spread_sides(1)
            spread_diagonals()

        for n in range(3):
            split_stored(2 + 3 * k + n)

        @pl.when(k == 1)
        def _():
            wait_sent(1)

        for c in faces_x + faces_y + tuple(tiles[7:]):
            c.wait_recv()
        add_halo(slot)
        outer_layers(slot)
        middle_own(slot, next_own(slot))
        weights = own_coefficients(inner2[1:5, 1:9])
        for c in corners + tuple(tiles[:7]) + tuple(parts):
            c.wait_recv()
        weights = corner_cells(slot, weights)
        middle_around(slot, next_around(slot))
        scale = jnp.where(k == 0, 2.0 * AT_LOW[2] / AT_LOW[5], 2.0 * AT_LOW[5] / AT_LOW[8])
        back = jnp.where(k == 0, 1.0 / AT_LOW[5], AT_LOW[2] / AT_LOW[8])
        degree_three(slot, weights, scale, back, k == 1)
        return carry

    lax.fori_loop(0, 2, step, 0)
    wait_sent(0)

    first_core = band == 0
    def send1(c):
        return pltpu.make_async_remote_copy(
            src_ref=pbuf.at[c], dst_ref=r1.at[mz], send_sem=p1s.at[c], recv_sem=p1r.at[mz],
            device_id=(gx, c * NG_Y + my, band), device_id_type=MESH)

    nt = (((1,), (1,)), ((), ()))
    for x in range(CX):
        swap(x).wait_recv()
        for y in range(CY):
            mine, theirs = field[1, 3 + x, 3 + y], other[x, y]
            both = jnp.concatenate(
                [jnp.where(first_core, mine, theirs), jnp.where(first_core, theirs, mine)], axis=0)
            high = both.astype(BF16)
            wmat[0:16, y * CZ:(y + 1) * CZ] = high
            wmat[16:32, y * CZ:(y + 1) * CZ] = (both - high.astype(F32)).astype(BF16)
        weights = wmat[...]
        cols = slice(x * CY * CZ, (x + 1) * CY * CZ)
        got = lax.dot_general(weights, s_hi[:, cols], nt, preferred_element_type=F32)
        got = got[0:16] + got[16:32]
        got = got + lax.dot_general(weights[0:16], s_lo[:, cols], nt, preferred_element_type=F32)
        total[...] = got if x == 0 else total[...] + got
    for t in range(NJ // 128):
        flat = total[:, t * 128:(t + 1) * 128]
        for h in range(2):
            c = 2 * t + h
            pbuf[c] = flat[8 * h:8 * h + 8]

            @pl.when(mz == c)
            def _(c=c):
                r1[c] = pbuf[c]

            @pl.when(mz != c)
            def _(c=c):
                send1(c).start()

    def recv1(i):
        at, device = z_peer(i)
        return pltpu.make_async_remote_copy(
            src_ref=pbuf.at[at], dst_ref=r1.at[at], send_sem=p1s.at[at], recv_sem=p1r.at[at],
            device_id=device, device_id_type=MESH)

    for x in range(CX):
        swap(x).wait_send()
    for i in range(1, NG_Z):
        recv1(i).wait_recv()
    g2[plane] = jnp.sum(r1[...], axis=0)

    def send2(i):
        return pltpu.make_async_remote_copy(
            src_ref=g2.at[plane], dst_ref=g2.at[plane], send_sem=p2s.at[i], recv_sem=p2r.at[plane],
            device_id=plane_peer(i)[1], device_id_type=MESH)

    def recv2(i):
        at, device = plane_peer(i)
        return pltpu.make_async_remote_copy(
            src_ref=g2.at[plane], dst_ref=g2.at[at], send_sem=p2s.at[i], recv_sem=p2r.at[at],
            device_id=device, device_id_type=MESH)

    for i in (10, 9, 11, 6, 14, 5, 7, 13, 15, 2, 8, 1, 3, 4, 12):
        send2(i).start()
    for i in range(1, NG_Z):
        recv1(i).wait_send()
    for i in range(1, PLANE):
        recv2(i).wait_recv()
    q3[mz] = jnp.sum(g2[...], axis=0)

    def send3(i):
        return pltpu.make_async_remote_copy(
            src_ref=q3.at[mz], dst_ref=q3.at[mz], send_sem=p3s.at[i], recv_sem=p3r.at[mz],
            device_id=z_peer(i)[1], device_id_type=MESH)

    for i in (4, 3, 5, 2, 6, 1, 7):
        send3(i).start()
    for i in range(1, PLANE):
        send2(i).wait_send()
    nn = (((1,), (0,)), ((), ()))

    def arrived(c):
        pltpu.make_async_remote_copy(
            src_ref=q3.at[mz], dst_ref=q3.at[c], send_sem=p3s.at[0], recv_sem=p3r.at[c],
            device_id=(gx, c * NG_Y + my, band), device_id_type=MESH).wait_recv()

    def give(x):
        return pltpu.make_async_remote_copy(
            src_ref=csend.at[x], dst_ref=crecv.at[x], send_sem=cs_sem.at[x], recv_sem=cr_sem.at[x],
            device_id=twin, device_id_type=MESH)

    pairs = NG_Z // 2
    for n, ahead in enumerate((0, 1, 3, 2)):
        pair = lax.rem(lax.div(mz, 2) + ahead, pairs)
        for h in range(2):
            @pl.when(2 * pair + h != mz)
            def _(h=h):
                arrived(2 * pair + h)

        whole = jnp.concatenate([q3[2 * pair], q3[2 * pair + 1]], axis=0)
        rows_j = pl.ds(pl.multiple_of(pair * 128, 128), 128)
        int_ref[:, rows_j] = whole
        high = whole.astype(BF16)
        low = (whole - high.astype(F32)).astype(BF16)
        left_side = jnp.concatenate([high, low], axis=0)
        for x in range(CX):
            cols = slice(x * CY * CZ, (x + 1) * CY * CZ)
            got = lax.dot_general(left_side, s_hi[rows_j, cols], nn, preferred_element_type=F32)
            more = lax.dot_general(high, s_lo[rows_j, cols], nn, preferred_element_type=F32)
            got = got[0:16] + got[16:32] + more
            if n > 0:
                got = got + fix[:, cols]
            if n < pairs - 1:
                fix[:, cols] = got
                continue
            keep = jnp.where(first_core, got[0:8], got[8:16])
            send = jnp.where(first_core, got[8:16], got[0:8])
            for y in range(CY):
                csend[x, y] = send[:, y * CZ:(y + 1) * CZ]
                field[0, 3 + x, 3 + y] = field[1, 3 + x, 3 + y] - keep[:, y * CZ:(y + 1) * CZ]
            give(x).start()
    for i in range(1, NG_Z):
        send3(i).wait_send()
    for x in range(CX):
        give(x).wait_recv()
        for y in range(CY):
            out_ref[pl.ds(x * CY + y, ORB, stride=NXY), :] = field[0, 3 + x, 3 + y] - crecv[x, y]
    for x in range(CX):
        give(x).wait_send()


def finish(a_ref, b_ref, a_out, b_out):
    a_out[...] = a_ref[...]
    b_out[...] = b_ref[...]


def on_device(block, potential, proj_index, proj_value, proj_strength, stored):
    vmem = pl.BlockSpec(memory_space=pltpu.VMEM)
    hbm = pl.BlockSpec(memory_space=pltpu.HBM)
    dma = pltpu.SemaphoreType.DMA
    projected, intersection = pl.pallas_call(
        kernel,
        out_shape=(
            jax.ShapeDtypeStruct((ORB * NXY, CZ), F32),
            jax.ShapeDtypeStruct((2 * ORB, NJ), F32),
        ),
        in_specs=[
            hbm, hbm, hbm, hbm, hbm, hbm],
        out_specs=(vmem, vmem),
        scratch_shapes=[
            pltpu.VMEM((2, CX + 6, CY + 6, ORB, CZ), F32),
            pltpu.VMEM((CX + 4, CY + 4, ORB, CZ), F32),
            pltpu.VMEM((CX + 2, CY + 2, ORB, CZ), F32),
            pltpu.VMEM((ORB * NXY, CZ), F32),
            pltpu.VMEM((NXY, CZ), F32),
            pltpu.VMEM((NPROJ, 128), jnp.int32),
            pltpu.VMEM((NPROJ, 128), F32),
            pltpu.SMEM((NPROJ,), F32),
            pltpu.VMEM((NPROJ + 1, CX, CY, ORB, CZ), F32),
            pltpu.VMEM((NPROJ + 1, NXY, CZ), F32),
            pltpu.VMEM((2, 2, 40, CZ), F32),
            pltpu.VMEM((4, 16, CZ), F32),
            pltpu.VMEM((2, NPROJ + 1, 2 * CY, CZ), F32),
            pltpu.VMEM((2, 2, 40, CZ), F32),
            pltpu.VMEM((4, 16, CZ), F32),
            pltpu.VMEM((2, NPROJ + 1, 2, CY, ORB, CZ), F32),
            pltpu.VMEM((2, NPROJ + 1, CX, 2, ORB, CZ), F32),
            pltpu.VMEM((4, NPROJ + 1, ORB, CZ), F32),
            pltpu.VMEM((2, ORB, CZ), F32),
            pltpu.VMEM((2, 11, ORB, CZ), F32),
            pltpu.VMEM((2, ORB, CZ), F32),
            pltpu.VMEM((2, 4, ORB, CZ), F32),
            pltpu.VMEM((NXY, NJ, CZ), F32),
            pltpu.VMEM((NJ, CELLS), BF16),
            pltpu.VMEM((NJ, CELLS), BF16),
            pltpu.VMEM((CX, CY, ORB, CZ), F32),
            pltpu.VMEM((4 * ORB, CY * CZ), BF16),
            pltpu.VMEM((2 * ORB, NJ), F32),
            pltpu.VMEM((NG_Z, ORB, CZ), F32),
            pltpu.VMEM((NG_Z, ORB, CZ), F32),
            pltpu.VMEM((PLANE, ORB, CZ), F32),
            pltpu.VMEM((NG_Z, ORB, CZ), F32),
            pltpu.VMEM((2 * ORB, CELLS), F32),
            pltpu.VMEM((CX, CY, ORB, CZ), F32),
            pltpu.VMEM((CX, CY, ORB, CZ), F32),
            dma((5,)), dma((NXY,)), dma((2, 23)), dma((2, 23)), dma((12,)), dma((12,)), dma((CX,)), dma((CX,)),
            dma((NG_Z,)), dma((NG_Z,)), dma((PLANE,)), dma((PLANE,)), dma((NG_Z,)), dma((NG_Z,)),
            dma((CX,)), dma((CX,)),
        ],
        compiler_params=pltpu.CompilerParams(
            collective_id=0, has_side_effects=True, vmem_limit_bytes=60 * 1024 * 1024),
        name="filter_project",
    )(
        block.reshape(ORB * NXY, CZ), potential.reshape(NXY, CZ), proj_index, proj_value,
        proj_strength, stored.reshape(NJ, NXY, CZ))
    projected, intersection = pl.pallas_call(
        finish,
        out_shape=(jax.ShapeDtypeStruct(projected.shape, F32), jax.ShapeDtypeStruct(intersection.shape, F32)),
        in_specs=[vmem, vmem],
        out_specs=(vmem, vmem),
        name="finish",
    )(projected, intersection)
    return projected.reshape(block.shape), intersection.T


def solution(mesh):
    in_specs = (
        P("band", "gx", "gyz", None),
        P("gx", "gyz", None),
        P(("gx", "gyz"), None),
        P(("gx", "gyz"), None),
        P(("gx", "gyz")),
        P("band", "gx", "gyz", None),
    )
    out_specs = (P("band", "gx", "gyz", None), P("band", None))
    return jax.shard_map(
        on_device, mesh=mesh, in_specs=in_specs, out_specs=out_specs, check_vma=False
    )
```

```python
import functools

import jax
import jax.numpy as jnp
from jax import lax
from jax.experimental import pallas as pl
from jax.experimental.pallas import tpu as pltpu
from jax.sharding import PartitionSpec as P

DEGREE = 8
LOW_EDGE = 0.0
CUT_EDGE = 1.0
TOP_EDGE = 10.0
HALF = (TOP_EDGE - CUT_EDGE) / 2.0
CENTER = (TOP_EDGE + CUT_EDGE) / 2.0

MESH = pl.DeviceIdType.MESH
F32 = jnp.float32
BF16 = jnp.bfloat16

CX, CY, CZ = 4, 8, 128
NXY = CX * CY
CELLS = NXY * CZ
ORB = 8
NPROJ = 8
NJ = 512
NG_X, NG_Y, NG_Z = 4, 4, 8
PLANE = NG_X * NG_Y


def chebyshev_at_low():
    x = (LOW_EDGE - CENTER) / HALF
    t = [1.0, x]
    while len(t) <= DEGREE:
        t.append(2.0 * x * t[-1] - t[-2])
    return t


AT_LOW = chebyshev_at_low()


def kernel(
    block_ref, pot_in, idx_in, val_in, str_in, stored_ref,
    out_ref, int_ref,
    field, inner, inner2, raw, pot_ref, idx_ref, val_ref, str_ref, beta, dense, edge, nook, side_x, side_y, side_d,
    beta_x, beta_y, beta_d, coef, coef_in, part, part_in, sraw, s_hi, s_lo, other, wmat, total,
    pbuf, r1, g2, q3, fix, csend, crecv,
    in_sem, st_sem, hs_sem, hr_sem, fs_sem, fr_sem, bs_sem, br_sem, p1s, p1r, p2s, p2r, p3s, p3r, cs_sem, cr_sem,
):
    gx = lax.axis_index("gx")
    gyz = lax.axis_index("gyz")
    band = lax.axis_index("band")
    mz = lax.div(gyz, NG_Y)
    my = lax.rem(gyz, NG_Y)
    plane = gx * NG_Y + my
    left, right = lax.rem(gx + NG_X - 1, NG_X), lax.rem(gx + 1, NG_X)
    down, up = lax.rem(gyz + NG_Y * NG_Z - 1, NG_Y * NG_Z), lax.rem(gyz + 1, NG_Y * NG_Z)
    xl, xr, yl, yr = (left, gyz, band), (right, gyz, band), (gx, down, band), (gx, up, band)
    diagonal = [(x, y, band) for x in (left, right) for y in (down, up)]
    x2 = (lax.rem(gx + 2, NG_X), gyz, band)
    down2 = (gx, lax.rem(gyz + NG_Y * NG_Z - 2, NG_Y * NG_Z), band)
    up2 = (gx, lax.rem(gyz + 2, NG_Y * NG_Z), band)
    twin = (gx, gyz, 1 - band)

    def plane_peer(i):
        at = lax.rem(plane + i, PLANE)
        return at, (lax.div(at, NG_Y), mz * NG_Y + lax.rem(at, NG_Y), band)

    def z_peer(i):
        at = lax.rem(mz + i, NG_Z)
        return at, (gx, at * NG_Y + my, band)

    barrier = pltpu.get_barrier_semaphore()

    def greet(device):
        pl.semaphore_signal(barrier, inc=1, device_id=device, device_id_type=MESH)

    for device in diagonal + [yl, yr, down2, up2, twin]:
        greet(device)
    for i in range(1, PLANE):
        greet(plane_peer(i)[1])
    for i in range(1, NG_Z):
        greet(z_peer(i)[1])

    loads = [
        pltpu.make_async_copy(src, dst, in_sem.at[n])
        for n, (src, dst) in enumerate(
            ((idx_in, idx_ref), (val_in, val_ref), (pot_in, pot_ref), (str_in, str_ref), (block_ref, raw)))]
    for load in loads:
        load.start()
    def load_stored(xy):
        return pltpu.make_async_copy(stored_ref.at[:, xy], sraw.at[xy], st_sem.at[xy])


    def prepare():
        edge[...] = jnp.zeros(edge.shape, F32)
        nook[...] = jnp.zeros(nook.shape, F32)
        low_edge = lax.broadcasted_iota(jnp.int32, (NXY, 128), 0)
        at_row = lax.broadcasted_iota(jnp.int32, (CZ, 128), 0)
        for p in range(NPROJ):
            index = idx_ref[p:p + 1, :]
            value = val_ref[p:p + 1, :] * jnp.sqrt(jnp.full((1, 128), str_ref[p] * (1.0 / HALF), F32))
            v1 = value.astype(BF16).astype(F32)
            v2 = (value - v1).astype(BF16).astype(F32)
            v3 = value - v1 - v2
            at_xy = low_edge == lax.shift_right_logical(index, 7)
            at_z = at_row == lax.bitwise_and(index, 127)
            picks = jnp.concatenate([jnp.where(at_xy, v, 0.0) for v in (v1, v2, v3)], axis=0).astype(BF16)
            places = jnp.where(at_z, 1.0, 0.0).astype(BF16)
            got = lax.dot_general(picks, places, (((1,), (1,)), ((), ())), preferred_element_type=F32)
            dense[p] = got[0:NXY] + got[NXY:2 * NXY] + got[2 * NXY:]
        dense[NPROJ] = (pot_ref[...] + (3.0 - CENTER)) * (1.0 / HALF)
        for p in range(NPROJ + 1):
            beta[p] = jnp.broadcast_to(dense[p][:, None, :], (NXY, ORB, CZ)).reshape(CX, CY, ORB, CZ)
            for layer in range(2):
                for side, y in ((0, layer), (1, CY - 1 - layer)):
                    edge[layer, side, CX * p:CX * p + CX] = dense[p, pl.ds(y, CX, stride=CY), :]
            for n, row in enumerate((0, CY - 1, NXY - CY, NXY - 1)):
                nook[n, p:p + 1] = dense[p, row:row + 1]

    def side_copies(layer):
        def copy(src, dst, n, device):
            return pltpu.make_async_remote_copy(
                src_ref=src, dst_ref=dst, send_sem=fs_sem.at[4 * layer + n], recv_sem=fr_sem.at[4 * layer + n],
                device_id=device, device_id_type=MESH)

        def x_rows(plane):
            return slice(CY * plane, CY * plane + CY)

        return (
            copy(edge.at[layer, 0], side_y.at[1, layer], 3, yl),
            copy(edge.at[layer, 1], side_y.at[0, layer], 2, yr),
            copy(dense.at[:, x_rows(layer)], side_x.at[1, :, x_rows(layer)], 1, xl),
            copy(dense.at[:, x_rows(CX - 1 - layer)], side_x.at[0, :, x_rows(1 - layer)], 0, xr),
        )

    def diagonal_copies():
        def copy(n):
            return pltpu.make_async_remote_copy(
                src_ref=nook.at[n], dst_ref=side_d.at[3 - n], send_sem=fs_sem.at[8 + n], recv_sem=fr_sem.at[8 + n],
                device_id=diagonal[n], device_id_type=MESH)
        return copy(0), copy(1), copy(2), copy(3)

    def spread_sides(layer):
        for p in range(NPROJ + 1):
            for side in range(2):
                n = layer if side == 1 else 1 - layer
                got = side_x[side, p, CY * n:CY * n + CY]
                beta_x[side, p, n] = jnp.broadcast_to(got[:, None, :], (CY, ORB, CZ))
                got = side_y[side, layer, CX * p:CX * p + CX]
                beta_y[side, p, :, n] = jnp.broadcast_to(got[:, None, :], (CX, ORB, CZ))

    def spread_diagonals():
        for p in range(NPROJ + 1):
            for n in range(4):
                beta_d[n, p] = jnp.broadcast_to(side_d[n, p:p + 1], (ORB, CZ))

    for xy in range(NXY):
        load_stored(xy).start()
    for load in loads[:4]:
        load.wait()
    prepare()
    loads[4].wait()

    for xy in range(NXY):
        field[0, 3 + xy // CY, 3 + xy % CY] = raw[pl.ds(xy, ORB, stride=NXY), :]

    def split_stored(k):
        def part(n, carry):
            xy = 4 * k + n
            load_stored(xy).wait()
            got = sraw[xy]
            high = got.astype(BF16)
            cols = pl.ds(pl.multiple_of(xy * CZ, CZ), CZ)
            s_hi[:, cols] = high
            s_lo[:, cols] = (got - high.astype(F32)).astype(BF16)
            return carry

        lax.fori_loop(0, 4, part, 0)

    pl.semaphore_wait(barrier, 9 + PLANE - 1 + NG_Z - 1)

    def halo_copies(slot, depth):
        def copy(src, dst, n, device):
            return pltpu.make_async_remote_copy(
                src_ref=field.at[(slot,) + src], dst_ref=field.at[(slot,) + dst],
                send_sem=hs_sem.at[slot, n], recv_sem=hr_sem.at[slot, n],
                device_id=device, device_id_type=MESH)
        own_x, own_y = slice(3, 7), slice(3, 11)
        low, high, n = 3, 3 + CX, depth - 1
        low_y, high_y = 3, 3 + CY
        x_low, x_high, y_low, y_high = (
            slice(low, low + n), slice(high - n, high), slice(low_y, low_y + n), slice(high_y - n, high_y))
        x_over, x_under, y_over, y_under = (
            slice(high, high + n), slice(low - n, low), slice(high_y, high_y + n), slice(low_y - n, low_y))
        corners = (
            copy((x_low, y_low), (x_over, y_over), 4, diagonal[0]),
            copy((x_low, y_high), (x_over, y_under), 5, diagonal[1]),
            copy((x_high, y_low), (x_under, y_over), 6, diagonal[2]),
            copy((x_high, y_high), (x_under, y_under), 7, diagonal[3]),
        )
        faces_y = (
            copy((own_x, slice(3, 3 + depth)), (own_x, slice(11, 11 + depth)), 3, yl),
            copy((own_x, slice(11 - depth, 11)), (own_x, slice(3 - depth, 3)), 2, yr),
        )
        faces_x = (
            copy((slice(3, 3 + depth), own_y), (slice(7, 7 + depth), own_y), 1, xl),
            copy((slice(7 - depth, 7), own_y), (slice(3 - depth, 3), own_y), 0, xr),
        )
        return corners, faces_y, faces_x

    def coef_copies(slot, count):
        def copy(place, device):
            return pltpu.make_async_remote_copy(
                src_ref=coef.at[slot], dst_ref=coef_in.at[slot, place],
                send_sem=hs_sem.at[slot, 8 + place], recv_sem=hr_sem.at[slot, 8 + place],
                device_id=device, device_id_type=MESH)
        return [copy(place, device) for place, device in (
            (7, diagonal[0]), (6, diagonal[1]), (5, diagonal[2]), (4, diagonal[3]),
            (10, down2), (9, up2), (8, x2), (3, yl), (2, yr), (1, xl), (0, xr))[11 - count:]]

    def part_copies(slot):
        def copy(place, device):
            return pltpu.make_async_remote_copy(
                src_ref=part.at[slot], dst_ref=part_in.at[slot, place],
                send_sem=hs_sem.at[slot, 19 + place], recv_sem=hr_sem.at[slot, 19 + place],
                device_id=device, device_id_type=MESH)
        return [copy(place, device) for place, device in ((3, yl), (2, yr), (1, xl), (0, xr))]

    lanes = lax.broadcasted_iota(jnp.int32, (1, ORB, CZ), 2)
    lane = lax.broadcasted_iota(jnp.int32, (ORB, CZ), 1)
    side_scale = 0.5 / HALF

    def along(cur):
        zero = jnp.zeros((1,) + cur.shape[1:], F32)
        return jnp.concatenate([zero, cur[:-1]], axis=0) + jnp.concatenate([cur[1:], zero], axis=0)

    def along_z(cur):
        return (jnp.where(lanes == 0, 0.0, pltpu.roll(cur, 1, cur.ndim - 1))
                + jnp.where(lanes == CZ - 1, 0.0, pltpu.roll(cur, CZ - 1, cur.ndim - 1)))

    def dot_tiles(values, tiles):
        return [jnp.sum(jnp.sum(values * tiles(p), axis=tuple(range(values.ndim - 2))), axis=1, keepdims=True)
                for p in range(NPROJ)]

    def pack(columns):
        packed = jnp.zeros((ORB, CZ), F32)
        for n, column in enumerate(columns):
            packed = jnp.where(lane == n, column, packed)
        return packed

    def unpack(tile):
        return [tile[:, p:p + 1] for p in range(NPROJ)]

    def spread(weights, tiles):
        total = weights[0] * tiles(0)
        for p in range(1, NPROJ):
            total = total + weights[p] * tiles(p)
        return total

    def own_coefficients(values):
        return dot_tiles(values, lambda p: beta[p])

    def inside(slot, weights, x):
        cur = field[slot, 3 + x, 3:11]
        near = along(cur) + along_z(cur)
        if x > 0:
            near = near + field[slot, 2 + x, 3:11]
        if x < CX - 1:
            near = near + field[slot, 4 + x, 3:11]
        return beta[NPROJ, x] * cur - side_scale * near + spread(weights, lambda p: beta[p, x])

    def add_halo(slot):
        inner[2, 2:10] = inner[2, 2:10] - side_scale * field[slot, 2, 3:11]
        inner[5, 2:10] = inner[5, 2:10] - side_scale * field[slot, 7, 3:11]
        inner[2:6, 2] = inner[2:6, 2] - side_scale * field[slot, 3:7, 2]
        inner[2:6, 9] = inner[2:6, 9] - side_scale * field[slot, 3:7, 11]

    def first_layer(slot):
        for side, at in ((0, 2), (1, 7)):
            cur = field[slot, at, 3:11]
            near = field[slot, at - 1, 3:11] + field[slot, at + 1, 3:11] + along(cur) + along_z(cur)
            inner[at - 1, 2:10] = (
                beta_x[side, NPROJ, 1 - side] * cur - side_scale * near
                + spread(unpack(coef_in[slot, side]), lambda p: beta_x[side, p, 1 - side]))
        for side, at in ((0, 2), (1, 11)):
            cur = field[slot, 3:7, at]
            near = field[slot, 3:7, at - 1] + field[slot, 3:7, at + 1] + along(cur) + along_z(cur)
            inner[2:6, at - 1] = (
                beta_y[side, NPROJ, :, 1 - side] * cur - side_scale * near
                + spread(unpack(coef_in[slot, 2 + side]), lambda p: beta_y[side, p, :, 1 - side]))

    def own_x_of_inner(x, weights):
        cur = inner[2 + x, 2:10]
        near = inner[1 + x, 2:10] + inner[3 + x, 2:10] + inner[2 + x, 1:9] + inner[2 + x, 3:11]
        near = near + along_z(cur)
        return beta[NPROJ, x] * cur - side_scale * near + spread(weights, lambda p: beta[p, x])

    def degree_two():
        weights = own_coefficients(inner[2:6, 2:10])
        for x in range(CX):
            field[1, 3 + x, 3:11] = (
                (2.0 / AT_LOW[2]) * own_x_of_inner(x, weights) - (1.0 / AT_LOW[2]) * field[0, 3 + x, 3:11])

    def outer_layers(slot):
        for side, at in ((0, 1), (1, 7)):
            cur = field[slot, at:at + 2, 3:11]
            near = field[slot, at - 1:at + 1, 3:11] + field[slot, at + 1:at + 3, 3:11] + along_z(cur)
            near = near + jnp.stack([along(cur[0]), along(cur[1])])
            inner[at - 1:at + 1, 2:10] = (
                beta_x[side, NPROJ] * cur - side_scale * near
                + spread(unpack(coef_in[slot, side]), lambda p: beta_x[side, p]))
        for side, at in ((0, 1), (1, 11)):
            cur = field[slot, 3:7, at:at + 2]
            near = field[slot, 3:7, at - 1:at + 1] + field[slot, 3:7, at + 1:at + 3] + along_z(cur)
            near = near + along(cur)
            inner[2:6, at - 1:at + 1] = (
                beta_y[side, NPROJ] * cur - side_scale * near
                + spread(unpack(coef_in[slot, 2 + side]), lambda p: beta_y[side, p]))
    def corner_cells(slot, weights):
        added, tiles = [], []
        for x, y, own_x, own_y, out in ((2, 2, 3, 3, -1), (2, 11, 3, 10, 1), (7, 2, 6, 3, -1), (7, 11, 6, 10, 1)):
            far_x, far_y = 2 * x - own_x, y + out
            for here_x, here_y, got in ((x, own_y, (x, y)), (far_x, own_y, (far_x, y)),
                                        (own_x, y, (x, y)), (own_x, far_y, (x, far_y))):
                inner[here_x - 1, here_y - 1] = (
                    inner[here_x - 1, here_y - 1] - side_scale * field[(slot,) + got])
            more = (4.0 * side_scale * side_scale) * field[slot, x, y]
            inner2[own_x - 2, own_y - 2] = inner2[own_x - 2, own_y - 2] + more
            added.append(more)
            tiles.append((own_x - 3, own_y - 3))
        out = []
        for p in range(NPROJ):
            acc = sum(more * beta[p, x, y] for more, (x, y) in zip(added, tiles))
            out.append(weights[p] + jnp.sum(acc, axis=1, keepdims=True))
        for n, (x, y) in enumerate(((2, 2), (2, 11), (7, 2), (7, 11))):
            cur = field[slot, x, y]
            near = field[slot, x - 1, y] + field[slot, x + 1, y] + field[slot, x, y - 1] + field[slot, x, y + 1]
            near = near + along_z(cur[None])[0]
            inner[x - 1, y - 1] = (
                beta_d[n, NPROJ] * cur - side_scale * near
                + spread(unpack(coef_in[slot, 4 + n]), lambda p: beta_d[n, p]))
        return out

    XL, XR, YL, YR = 1, 2, 3, 4

    def group(tile, n):
        return pltpu.roll(tile, CZ - 8 * n, 1)

    def next_own(slot):
        near = [coef_in[slot, place] for place in range(4)]
        own = group(near[0], XR) + group(near[1], XL) + group(near[2], YR) + group(near[3], YL)
        return unpack(part[slot] - side_scale * own)

    def next_around(slot):
        got = [coef_in[slot, place] for place in range(11)]
        mine = coef[slot]
        low_x = group(mine, XL) + group(got[8], XR) + group(got[4], YR) + group(got[5], YL)
        high_x = group(mine, XR) + group(got[8], XL) + group(got[6], YR) + group(got[7], YL)
        low_y = group(mine, YL) + group(got[9], YR) + group(got[4], XR) + group(got[6], XL)
        high_y = group(mine, YR) + group(got[10], YL) + group(got[5], XR) + group(got[7], XL)
        return [unpack(part_in[slot, place] - side_scale * terms)
                for place, terms in enumerate((low_x, high_x, low_y, high_y))]

    def middle_own(slot, weights):
        for x in range(CX):
            inner2[1 + x, 1:9] = 2.0 * own_x_of_inner(x, weights) - field[slot, 3 + x, 3:11]

    def middle_around(slot, weights):
        for side, at in ((0, 1), (1, 6)):
            cur = inner[at, 2:10]
            near = inner[at - 1, 2:10] + inner[at + 1, 2:10] + inner[at, 1:9] + inner[at, 3:11] + along_z(cur)
            got = (beta_x[side, NPROJ, 1 - side] * cur - side_scale * near
                   + spread(weights[side], lambda p: beta_x[side, p, 1 - side]))
            inner2[at - 1, 1:9] = 2.0 * got - field[slot, at + 1, 3:11]
        for side, at in ((0, 1), (1, 10)):
            cur = inner[2:6, at]
            near = inner[2:6, at - 1] + inner[2:6, at + 1] + inner[1:5, at] + inner[3:7, at] + along_z(cur)
            got = (beta_y[side, NPROJ, :, 1 - side] * cur - side_scale * near
                   + spread(weights[2 + side], lambda p: beta_y[side, p, :, 1 - side]))
            inner2[1:5, at - 1] = 2.0 * got - field[slot, 3:7, at + 1]

    def swap(x):
        return pltpu.make_async_remote_copy(
            src_ref=field.at[1, 3 + x, 3:11], dst_ref=other.at[x], send_sem=bs_sem.at[x], recv_sem=br_sem.at[x],
            device_id=twin, device_id_type=MESH)

    def degree_three(slot, weights, scale, back, last):
        for x in range(CX):
            cur = inner2[1 + x, 1:9]
            near = inner2[x, 1:9] + inner2[2 + x, 1:9] + inner2[1 + x, 0:8] + inner2[1 + x, 2:10]
            near = near + along_z(cur)
            got = beta[NPROJ, x] * cur - side_scale * near + spread(weights, lambda p: beta[p, x])
            got = 2.0 * got - inner[2 + x, 2:10]
            field[1 - slot, 3 + x, 3:11] = scale * got - back * field[1 - slot, 3 + x, 3:11]

            @pl.when(last)
            def _(x=x):
                swap(x).start()

    def wait_sent(slot):
        corners, faces_y, faces_x = halo_copies(slot, 3)
        for c in corners + faces_y + faces_x + tuple(coef_copies(slot, 11)) + tuple(part_copies(slot)):
            c.wait_send()

    def start(copies):
        for c in copies:
            c.start()

    corners, faces_y, faces_x = halo_copies(0, 2)
    start(corners + faces_y)
    weights = own_coefficients(field[0, 3:7, 3:11])
    coef[0] = pack(weights)
    tiles = coef_copies(0, 4)
    start(tiles)
    near_sides, next_sides, far_sides = side_copies(0), side_copies(1), diagonal_copies()
    start(near_sides[:2])
    start(faces_x)
    start(near_sides[2:])
    for x in range(CX):
        inner[2 + x, 2:10] = inside(0, weights, x)
    split_stored(0)
    start(next_sides + far_sides)
    split_stored(1)
    for c in near_sides:
        c.wait_recv()
    spread_sides(0)
    for c in faces_x + faces_y + tuple(tiles):
        c.wait_recv()
    add_halo(0)
    first_layer(0)
    degree_two()
    for c in corners:
        c.wait_recv()
    twice = (2.0 / AT_LOW[2]) * (2.0 * side_scale * side_scale)
    for x, y, at_x, at_y in ((3, 3, 2, 2), (3, 10, 2, 11), (6, 3, 7, 2), (6, 10, 7, 11)):
        field[1, x, y] = field[1, x, y] + twice * field[0, at_x, at_y]

    def step(k, carry):
        slot = 1 - k
        corners, faces_y, faces_x = halo_copies(slot, 3)
        start(corners)
        weights = own_coefficients(field[slot, 3:7, 3:11])
        columns = list(weights)
        for side, at in ((0, 3), (1, 6)):
            columns += dot_tiles(field[slot, at, 3:11], lambda p: beta_x[side, p, 1 - side])
        for side, at in ((0, 3), (1, 10)):
            columns += dot_tiles(field[slot, 3:7, at], lambda p: beta_y[side, p, :, 1 - side])
        coef[slot] = pack(columns)
        tiles = coef_copies(slot, 11)
        start(tiles)
        start(faces_y)
        start(faces_x)

        @pl.when(k == 0)
        def _():
            corners, faces_y, faces_x = halo_copies(0, 2)
            for c in corners + faces_y + faces_x + tuple(coef_copies(0, 4)):
                c.wait_send()
            field[0, 3:7, 3:11] = inner[2:6, 2:10]

        for x in range(CX):
            inner[2 + x, 2:10] = inside(slot, weights, x)
        part[slot] = pack(own_coefficients(inner[2:6, 2:10]))
        parts = part_copies(slot)
        start(parts)

        @pl.when(k == 0)
        def _():
            for c in near_sides + next_sides + far_sides:
                c.wait_send()
            for c in next_sides + far_sides:
                c.wait_recv()
            spread_sides(1)
            spread_diagonals()

        for n in range(3):
            split_stored(2 + 3 * k + n)

        @pl.when(k == 1)
        def _():
            wait_sent(1)

        for c in faces_x + faces_y + tuple(tiles[7:]):
            c.wait_recv()
        add_halo(slot)
        outer_layers(slot)
        middle_own(slot, next_own(slot))
        weights = own_coefficients(inner2[1:5, 1:9])
        for c in corners + tuple(tiles[:7]) + tuple(parts):
            c.wait_recv()
        weights = corner_cells(slot, weights)
        middle_around(slot, next_around(slot))
        scale = jnp.where(k == 0, 2.0 * AT_LOW[2] / AT_LOW[5], 2.0 * AT_LOW[5] / AT_LOW[8])
        back = jnp.where(k == 0, 1.0 / AT_LOW[5], AT_LOW[2] / AT_LOW[8])
        degree_three(slot, weights, scale, back, k == 1)
        return carry

    lax.fori_loop(0, 2, step, 0)

    first_core = band == 0
    def send1(i):
        at, device = z_peer(i)
        return pltpu.make_async_remote_copy(
            src_ref=pbuf.at[at], dst_ref=r1.at[mz], send_sem=p1s.at[at], recv_sem=p1r.at[mz],
            device_id=device, device_id_type=MESH)

    nt = (((1,), (1,)), ((), ()))
    for x in range(CX):
        swap(x).wait_recv()
        for y in range(CY):
            mine, theirs = field[1, 3 + x, 3 + y], other[x, y]
            both = jnp.concatenate(
                [jnp.where(first_core, mine, theirs), jnp.where(first_core, theirs, mine)], axis=0)
            high = both.astype(BF16)
            wmat[0:16, y * CZ:(y + 1) * CZ] = high
            wmat[16:32, y * CZ:(y + 1) * CZ] = (both - high.astype(F32)).astype(BF16)
        weights = wmat[...]
        cols = slice(x * CY * CZ, (x + 1) * CY * CZ)
        got = lax.dot_general(weights, s_hi[:, cols], nt, preferred_element_type=F32)
        got = got[0:16] + got[16:32]
        got = got + lax.dot_general(weights[0:16], s_lo[:, cols], nt, preferred_element_type=F32)
        total[...] = got if x == 0 else total[...] + got
    for t in range(NJ // 128):
        flat = total[:, t * 128:(t + 1) * 128]
        pbuf[2 * t], pbuf[2 * t + 1] = flat[0:8], flat[8:16]
    for i in (4, 3, 5, 2, 6, 1, 7):
        send1(i).start()
    r1[mz] = pbuf[mz]
    wait_sent(0)

    def recv1(i):
        at, device = z_peer(i)
        return pltpu.make_async_remote_copy(
            src_ref=pbuf.at[at], dst_ref=r1.at[at], send_sem=p1s.at[at], recv_sem=p1r.at[at],
            device_id=device, device_id_type=MESH)

    for x in range(CX):
        swap(x).wait_send()
    for i in range(1, NG_Z):
        recv1(i).wait_recv()
    g2[plane] = jnp.sum(r1[...], axis=0)

    def send2(i):
        return pltpu.make_async_remote_copy(
            src_ref=g2.at[plane], dst_ref=g2.at[plane], send_sem=p2s.at[i], recv_sem=p2r.at[plane],
            device_id=plane_peer(i)[1], device_id_type=MESH)

    def recv2(i):
        at, device = plane_peer(i)
        return pltpu.make_async_remote_copy(
            src_ref=g2.at[plane], dst_ref=g2.at[at], send_sem=p2s.at[i], recv_sem=p2r.at[at],
            device_id=device, device_id_type=MESH)

    for i in (10, 9, 11, 6, 14, 5, 7, 13, 15, 2, 8, 1, 3, 4, 12):
        send2(i).start()
    for i in range(1, NG_Z):
        recv1(i).wait_send()
    for i in range(1, PLANE):
        recv2(i).wait_recv()
    q3[mz] = jnp.sum(g2[...], axis=0)

    def send3(i):
        return pltpu.make_async_remote_copy(
            src_ref=q3.at[mz], dst_ref=q3.at[mz], send_sem=p3s.at[i], recv_sem=p3r.at[mz],
            device_id=z_peer(i)[1], device_id_type=MESH)

    for i in (4, 3, 5, 2, 6, 1, 7):
        send3(i).start()
    for i in range(1, PLANE):
        send2(i).wait_send()
    nn = (((1,), (0,)), ((), ()))

    def arrived(c):
        pltpu.make_async_remote_copy(
            src_ref=q3.at[mz], dst_ref=q3.at[c], send_sem=p3s.at[0], recv_sem=p3r.at[c],
            device_id=(gx, c * NG_Y + my, band), device_id_type=MESH).wait_recv()

    def give(x):
        return pltpu.make_async_remote_copy(
            src_ref=csend.at[x], dst_ref=crecv.at[x], send_sem=cs_sem.at[x], recv_sem=cr_sem.at[x],
            device_id=twin, device_id_type=MESH)

    pairs = NG_Z // 2
    for n, ahead in enumerate((0, 1, 3, 2)):
        pair = lax.rem(lax.div(mz, 2) + ahead, pairs)
        for h in range(2):
            @pl.when(2 * pair + h != mz)
            def _(h=h):
                arrived(2 * pair + h)

        whole = jnp.concatenate([q3[2 * pair], q3[2 * pair + 1]], axis=0)
        rows_j = pl.ds(pl.multiple_of(pair * 128, 128), 128)
        int_ref[:, rows_j] = whole
        high = whole.astype(BF16)
        low = (whole - high.astype(F32)).astype(BF16)
        left_side = jnp.concatenate([high, low], axis=0)
        for x in range(CX):
            cols = slice(x * CY * CZ, (x + 1) * CY * CZ)
            got = lax.dot_general(left_side, s_hi[rows_j, cols], nn, preferred_element_type=F32)
            more = lax.dot_general(high, s_lo[rows_j, cols], nn, preferred_element_type=F32)
            got = got[0:16] + got[16:32] + more
            if n > 0:
                got = got + fix[:, cols]
            if n < pairs - 1:
                fix[:, cols] = got
                continue
            keep = jnp.where(first_core, got[0:8], got[8:16])
            send = jnp.where(first_core, got[8:16], got[0:8])
            for y in range(CY):
                csend[x, y] = send[:, y * CZ:(y + 1) * CZ]
                field[0, 3 + x, 3 + y] = field[1, 3 + x, 3 + y] - keep[:, y * CZ:(y + 1) * CZ]
            give(x).start()
    for i in range(1, NG_Z):
        send3(i).wait_send()
    for x in range(CX):
        give(x).wait_recv()
        for y in range(CY):
            out_ref[pl.ds(x * CY + y, ORB, stride=NXY), :] = field[0, 3 + x, 3 + y] - crecv[x, y]
    for x in range(CX):
        give(x).wait_send()


def finish(a_ref, b_ref, a_out, b_out):
    a_out[...] = a_ref[...]
    b_out[...] = b_ref[...]


def on_device(block, potential, proj_index, proj_value, proj_strength, stored):
    vmem = pl.BlockSpec(memory_space=pltpu.VMEM)
    hbm = pl.BlockSpec(memory_space=pltpu.HBM)
    dma = pltpu.SemaphoreType.DMA
    projected, intersection = pl.pallas_call(
        kernel,
        out_shape=(
            jax.ShapeDtypeStruct((ORB * NXY, CZ), F32),
            jax.ShapeDtypeStruct((2 * ORB, NJ), F32),
        ),
        in_specs=[
            hbm, hbm, hbm, hbm, hbm, hbm],
        out_specs=(vmem, vmem),
        scratch_shapes=[
            pltpu.VMEM((2, CX + 6, CY + 6, ORB, CZ), F32),
            pltpu.VMEM((CX + 4, CY + 4, ORB, CZ), F32),
            pltpu.VMEM((CX + 2, CY + 2, ORB, CZ), F32),
            pltpu.VMEM((ORB * NXY, CZ), F32),
            pltpu.VMEM((NXY, CZ), F32),
            pltpu.VMEM((NPROJ, 128), jnp.int32),
            pltpu.VMEM((NPROJ, 128), F32),
            pltpu.SMEM((NPROJ,), F32),
            pltpu.VMEM((NPROJ + 1, CX, CY, ORB, CZ), F32),
            pltpu.VMEM((NPROJ + 1, NXY, CZ), F32),
            pltpu.VMEM((2, 2, 40, CZ), F32),
            pltpu.VMEM((4, 16, CZ), F32),
            pltpu.VMEM((2, NPROJ + 1, 2 * CY, CZ), F32),
            pltpu.VMEM((2, 2, 40, CZ), F32),
            pltpu.VMEM((4, 16, CZ), F32),
            pltpu.VMEM((2, NPROJ + 1, 2, CY, ORB, CZ), F32),
            pltpu.VMEM((2, NPROJ + 1, CX, 2, ORB, CZ), F32),
            pltpu.VMEM((4, NPROJ + 1, ORB, CZ), F32),
            pltpu.VMEM((2, ORB, CZ), F32),
            pltpu.VMEM((2, 11, ORB, CZ), F32),
            pltpu.VMEM((2, ORB, CZ), F32),
            pltpu.VMEM((2, 4, ORB, CZ), F32),
            pltpu.VMEM((NXY, NJ, CZ), F32),
            pltpu.VMEM((NJ, CELLS), BF16),
            pltpu.VMEM((NJ, CELLS), BF16),
            pltpu.VMEM((CX, CY, ORB, CZ), F32),
            pltpu.VMEM((4 * ORB, CY * CZ), BF16),
            pltpu.VMEM((2 * ORB, NJ), F32),
            pltpu.VMEM((NG_Z, ORB, CZ), F32),
            pltpu.VMEM((NG_Z, ORB, CZ), F32),
            pltpu.VMEM((PLANE, ORB, CZ), F32),
            pltpu.VMEM((NG_Z, ORB, CZ), F32),
            pltpu.VMEM((2 * ORB, CELLS), F32),
            pltpu.VMEM((CX, CY, ORB, CZ), F32),
            pltpu.VMEM((CX, CY, ORB, CZ), F32),
            dma((5,)), dma((NXY,)), dma((2, 23)), dma((2, 23)), dma((12,)), dma((12,)), dma((CX,)), dma((CX,)),
            dma((NG_Z,)), dma((NG_Z,)), dma((PLANE,)), dma((PLANE,)), dma((NG_Z,)), dma((NG_Z,)),
            dma((CX,)), dma((CX,)),
        ],
        compiler_params=pltpu.CompilerParams(
            collective_id=0, has_side_effects=True, vmem_limit_bytes=60 * 1024 * 1024),
        name="filter_project",
    )(
        block.reshape(ORB * NXY, CZ), potential.reshape(NXY, CZ), proj_index, proj_value,
        proj_strength, stored.reshape(NJ, NXY, CZ))
    projected, intersection = pl.pallas_call(
        finish,
        out_shape=(jax.ShapeDtypeStruct(projected.shape, F32), jax.ShapeDtypeStruct(intersection.shape, F32)),
        in_specs=[vmem, vmem],
        out_specs=(vmem, vmem),
        name="finish",
    )(projected, intersection)
    return projected.reshape(block.shape), intersection.T


def solution(mesh):
    in_specs = (
        P("band", "gx", "gyz", None),
        P("gx", "gyz", None),
        P(("gx", "gyz"), None),
        P(("gx", "gyz"), None),
        P(("gx", "gyz")),
        P("band", "gx", "gyz", None),
    )
    out_specs = (P("band", "gx", "gyz", None), P("band", None))
    return jax.shard_map(
        on_device, mesh=mesh, in_specs=in_specs, out_specs=out_specs, check_vma=False
    )
```

```python
import functools

import jax
import jax.numpy as jnp
from jax import lax
from jax.experimental import pallas as pl
from jax.experimental.pallas import tpu as pltpu
from jax.sharding import PartitionSpec as P

DEGREE = 8
LOW_EDGE = 0.0
CUT_EDGE = 1.0
TOP_EDGE = 10.0
HALF = (TOP_EDGE - CUT_EDGE) / 2.0
CENTER = (TOP_EDGE + CUT_EDGE) / 2.0

MESH = pl.DeviceIdType.MESH
F32 = jnp.float32
BF16 = jnp.bfloat16

CX, CY, CZ = 4, 8, 128
NXY = CX * CY
CELLS = NXY * CZ
ORB = 8
NPROJ = 8
NJ = 512
NG_X, NG_Y, NG_Z = 4, 4, 8
PLANE = NG_X * NG_Y


def chebyshev_at_low():
    x = (LOW_EDGE - CENTER) / HALF
    t = [1.0, x]
    while len(t) <= DEGREE:
        t.append(2.0 * x * t[-1] - t[-2])
    return t


AT_LOW = chebyshev_at_low()


def kernel(
    block_ref, pot_in, idx_in, val_in, str_in, stored_ref,
    out_ref, int_ref,
    field, inner, inner2, raw, pot_ref, idx_ref, val_ref, str_ref, beta, dense, edge, nook, side_x, side_y, side_d,
    beta_x, beta_y, beta_d, coef, coef_in, part, part_in, sraw, s_hi, s_lo, other, wmat, total,
    pbuf, r1, g2, q3, fix, csend, crecv,
    in_sem, st_sem, hs_sem, hr_sem, fs_sem, fr_sem, bs_sem, br_sem, p1s, p1r, p2s, p2r, p3s, p3r, cs_sem, cr_sem,
):
    gx = lax.axis_index("gx")
    gyz = lax.axis_index("gyz")
    band = lax.axis_index("band")
    mz = lax.div(gyz, NG_Y)
    my = lax.rem(gyz, NG_Y)
    plane = gx * NG_Y + my
    left, right = lax.rem(gx + NG_X - 1, NG_X), lax.rem(gx + 1, NG_X)
    down, up = lax.rem(gyz + NG_Y * NG_Z - 1, NG_Y * NG_Z), lax.rem(gyz + 1, NG_Y * NG_Z)
    xl, xr, yl, yr = (left, gyz, band), (right, gyz, band), (gx, down, band), (gx, up, band)
    diagonal = [(x, y, band) for x in (left, right) for y in (down, up)]
    x2 = (lax.rem(gx + 2, NG_X), gyz, band)
    down2 = (gx, lax.rem(gyz + NG_Y * NG_Z - 2, NG_Y * NG_Z), band)
    up2 = (gx, lax.rem(gyz + 2, NG_Y * NG_Z), band)
    twin = (gx, gyz, 1 - band)

    def plane_peer(i):
        at = lax.rem(plane + i, PLANE)
        return at, (lax.div(at, NG_Y), mz * NG_Y + lax.rem(at, NG_Y), band)

    def z_peer(i):
        at = lax.rem(mz + i, NG_Z)
        return at, (gx, at * NG_Y + my, band)

    barrier = pltpu.get_barrier_semaphore()

    def greet(device):
        pl.semaphore_signal(barrier, inc=1, device_id=device, device_id_type=MESH)

    for device in diagonal + [yl, yr, down2, up2, twin]:
        greet(device)
    for i in range(1, PLANE):
        greet(plane_peer(i)[1])
    for i in range(1, NG_Z):
        greet(z_peer(i)[1])

    loads = [
        pltpu.make_async_copy(src, dst, in_sem.at[n])
        for n, (src, dst) in enumerate(
            ((idx_in, idx_ref), (val_in, val_ref), (pot_in, pot_ref), (str_in, str_ref), (block_ref, raw)))]
    for load in loads:
        load.start()
    def load_stored(xy):
        return pltpu.make_async_copy(stored_ref.at[:, xy], sraw.at[xy], st_sem.at[xy])


    def prepare():
        edge[...] = jnp.zeros(edge.shape, F32)
        nook[...] = jnp.zeros(nook.shape, F32)
        low_edge = lax.broadcasted_iota(jnp.int32, (NXY, 128), 0)
        at_row = lax.broadcasted_iota(jnp.int32, (CZ, 128), 0)
        for p in range(NPROJ):
            index = idx_ref[p:p + 1, :]
            value = val_ref[p:p + 1, :] * jnp.sqrt(jnp.full((1, 128), str_ref[p] * (1.0 / HALF), F32))
            v1 = value.astype(BF16).astype(F32)
            v2 = (value - v1).astype(BF16).astype(F32)
            v3 = value - v1 - v2
            at_xy = low_edge == lax.shift_right_logical(index, 7)
            at_z = at_row == lax.bitwise_and(index, 127)
            picks = jnp.concatenate([jnp.where(at_xy, v, 0.0) for v in (v1, v2, v3)], axis=0).astype(BF16)
            places = jnp.where(at_z, 1.0, 0.0).astype(BF16)
            got = lax.dot_general(picks, places, (((1,), (1,)), ((), ())), preferred_element_type=F32)
            dense[p] = got[0:NXY] + got[NXY:2 * NXY] + got[2 * NXY:]
        dense[NPROJ] = (pot_ref[...] + (3.0 - CENTER)) * (1.0 / HALF)
        for p in range(NPROJ + 1):
            beta[p] = jnp.broadcast_to(dense[p][:, None, :], (NXY, ORB, CZ)).reshape(CX, CY, ORB, CZ)
            for layer in range(2):
                for side, y in ((0, layer), (1, CY - 1 - layer)):
                    edge[layer, side, CX * p:CX * p + CX] = dense[p, pl.ds(y, CX, stride=CY), :]
            for n, row in enumerate((0, CY - 1, NXY - CY, NXY - 1)):
                nook[n, p:p + 1] = dense[p, row:row + 1]

    def side_copies(layer):
        def copy(src, dst, n, device):
            return pltpu.make_async_remote_copy(
                src_ref=src, dst_ref=dst, send_sem=fs_sem.at[4 * layer + n], recv_sem=fr_sem.at[4 * layer + n],
                device_id=device, device_id_type=MESH)

        def x_rows(plane):
            return slice(CY * plane, CY * plane + CY)

        return (
            copy(edge.at[layer, 0], side_y.at[1, layer], 3, yl),
            copy(edge.at[layer, 1], side_y.at[0, layer], 2, yr),
            copy(dense.at[:, x_rows(layer)], side_x.at[1, :, x_rows(layer)], 1, xl),
            copy(dense.at[:, x_rows(CX - 1 - layer)], side_x.at[0, :, x_rows(1 - layer)], 0, xr),
        )

    def diagonal_copies():
        def copy(n):
            return pltpu.make_async_remote_copy(
                src_ref=nook.at[n], dst_ref=side_d.at[3 - n], send_sem=fs_sem.at[8 + n], recv_sem=fr_sem.at[8 + n],
                device_id=diagonal[n], device_id_type=MESH)
        return copy(0), copy(1), copy(2), copy(3)

    def spread_sides(layer):
        for p in range(NPROJ + 1):
            for side in range(2):
                n = layer if side == 1 else 1 - layer
                got = side_x[side, p, CY * n:CY * n + CY]
                beta_x[side, p, n] = jnp.broadcast_to(got[:, None, :], (CY, ORB, CZ))
                got = side_y[side, layer, CX * p:CX * p + CX]
                beta_y[side, p, :, n] = jnp.broadcast_to(got[:, None, :], (CX, ORB, CZ))

    def spread_diagonals():
        for p in range(NPROJ + 1):
            for n in range(4):
                beta_d[n, p] = jnp.broadcast_to(side_d[n, p:p + 1], (ORB, CZ))

    for xy in range(NXY):
        load_stored(xy).start()
    for load in loads[:4]:
        load.wait()
    prepare()
    loads[4].wait()

    for xy in range(NXY):
        field[0, 3 + xy // CY, 3 + xy % CY] = raw[pl.ds(xy, ORB, stride=NXY), :]

    def split_stored(k):
        def part(n, carry):
            xy = 4 * k + n
            load_stored(xy).wait()
            got = sraw[xy]
            high = got.astype(BF16)
            cols = pl.ds(pl.multiple_of(xy * CZ, CZ), CZ)
            s_hi[:, cols] = high
            s_lo[:, cols] = (got - high.astype(F32)).astype(BF16)
            return carry

        lax.fori_loop(0, 4, part, 0)

    pl.semaphore_wait(barrier, 9 + PLANE - 1 + NG_Z - 1)

    def halo_copies(slot, depth):
        def copy(src, dst, n, device):
            return pltpu.make_async_remote_copy(
                src_ref=field.at[(slot,) + src], dst_ref=field.at[(slot,) + dst],
                send_sem=hs_sem.at[slot, n], recv_sem=hr_sem.at[slot, n],
                device_id=device, device_id_type=MESH)
        own_x, own_y = slice(3, 7), slice(3, 11)
        low, high, n = 3, 3 + CX, depth - 1
        low_y, high_y = 3, 3 + CY
        x_low, x_high, y_low, y_high = (
            slice(low, low + n), slice(high - n, high), slice(low_y, low_y + n), slice(high_y - n, high_y))
        x_over, x_under, y_over, y_under = (
            slice(high, high + n), slice(low - n, low), slice(high_y, high_y + n), slice(low_y - n, low_y))
        corners = (
            copy((x_low, y_low), (x_over, y_over), 4, diagonal[0]),
            copy((x_low, y_high), (x_over, y_under), 5, diagonal[1]),
            copy((x_high, y_low), (x_under, y_over), 6, diagonal[2]),
            copy((x_high, y_high), (x_under, y_under), 7, diagonal[3]),
        )
        faces_y = (
            copy((own_x, slice(3, 3 + depth)), (own_x, slice(11, 11 + depth)), 3, yl),
            copy((own_x, slice(11 - depth, 11)), (own_x, slice(3 - depth, 3)), 2, yr),
        )
        faces_x = (
            copy((slice(3, 3 + depth), own_y), (slice(7, 7 + depth), own_y), 1, xl),
            copy((slice(7 - depth, 7), own_y), (slice(3 - depth, 3), own_y), 0, xr),
        )
        return corners, faces_y, faces_x

    def coef_copies(slot, count):
        def copy(place, device):
            return pltpu.make_async_remote_copy(
                src_ref=coef.at[slot], dst_ref=coef_in.at[slot, place],
                send_sem=hs_sem.at[slot, 8 + place], recv_sem=hr_sem.at[slot, 8 + place],
                device_id=device, device_id_type=MESH)
        return [copy(place, device) for place, device in (
            (7, diagonal[0]), (6, diagonal[1]), (5, diagonal[2]), (4, diagonal[3]),
            (10, down2), (9, up2), (8, x2), (3, yl), (2, yr), (1, xl), (0, xr))[11 - count:]]

    def part_copies(slot):
        def copy(place, device):
            return pltpu.make_async_remote_copy(
                src_ref=part.at[slot], dst_ref=part_in.at[slot, place],
                send_sem=hs_sem.at[slot, 19 + place], recv_sem=hr_sem.at[slot, 19 + place],
                device_id=device, device_id_type=MESH)
        return [copy(place, device) for place, device in ((3, yl), (2, yr), (1, xl), (0, xr))]

    lanes = lax.broadcasted_iota(jnp.int32, (1, ORB, CZ), 2)
    lane = lax.broadcasted_iota(jnp.int32, (ORB, CZ), 1)
    side_scale = 0.5 / HALF

    def along(cur):
        zero = jnp.zeros((1,) + cur.shape[1:], F32)
        return jnp.concatenate([zero, cur[:-1]], axis=0) + jnp.concatenate([cur[1:], zero], axis=0)

    def along_z(cur):
        return (jnp.where(lanes == 0, 0.0, pltpu.roll(cur, 1, cur.ndim - 1))
                + jnp.where(lanes == CZ - 1, 0.0, pltpu.roll(cur, CZ - 1, cur.ndim - 1)))

    def dot_tiles(values, tiles):
        return [jnp.sum(jnp.sum(values * tiles(p), axis=tuple(range(values.ndim - 2))), axis=1, keepdims=True)
                for p in range(NPROJ)]

    def pack(columns):
        packed = jnp.zeros((ORB, CZ), F32)
        for n, column in enumerate(columns):
            packed = jnp.where(lane == n, column, packed)
        return packed

    def unpack(tile):
        return [tile[:, p:p + 1] for p in range(NPROJ)]

    def spread(weights, tiles):
        total = weights[0] * tiles(0)
        for p in range(1, NPROJ):
            total = total + weights[p] * tiles(p)
        return total

    def own_coefficients(values):
        return dot_tiles(values, lambda p: beta[p])

    def inside(slot, weights, x):
        cur = field[slot, 3 + x, 3:11]
        near = along(cur) + along_z(cur)
        if x > 0:
            near = near + field[slot, 2 + x, 3:11]
        if x < CX - 1:
            near = near + field[slot, 4 + x, 3:11]
        return beta[NPROJ, x] * cur - side_scale * near + spread(weights, lambda p: beta[p, x])

    def add_halo(slot):
        inner[2, 2:10] = inner[2, 2:10] - side_scale * field[slot, 2, 3:11]
        inner[5, 2:10] = inner[5, 2:10] - side_scale * field[slot, 7, 3:11]
        inner[2:6, 2] = inner[2:6, 2] - side_scale * field[slot, 3:7, 2]
        inner[2:6, 9] = inner[2:6, 9] - side_scale * field[slot, 3:7, 11]

    def first_layer(slot):
        for side, at in ((0, 2), (1, 7)):
            cur = field[slot, at, 3:11]
            near = field[slot, at - 1, 3:11] + field[slot, at + 1, 3:11] + along(cur) + along_z(cur)
            inner[at - 1, 2:10] = (
                beta_x[side, NPROJ, 1 - side] * cur - side_scale * near
                + spread(unpack(coef_in[slot, side]), lambda p: beta_x[side, p, 1 - side]))
        for side, at in ((0, 2), (1, 11)):
            cur = field[slot, 3:7, at]
            near = field[slot, 3:7, at - 1] + field[slot, 3:7, at + 1] + along(cur) + along_z(cur)
            inner[2:6, at - 1] = (
                beta_y[side, NPROJ, :, 1 - side] * cur - side_scale * near
                + spread(unpack(coef_in[slot, 2 + side]), lambda p: beta_y[side, p, :, 1 - side]))

    def own_x_of_inner(x, weights):
        cur = inner[2 + x, 2:10]
        near = inner[1 + x, 2:10] + inner[3 + x, 2:10] + inner[2 + x, 1:9] + inner[2 + x, 3:11]
        near = near + along_z(cur)
        return beta[NPROJ, x] * cur - side_scale * near + spread(weights, lambda p: beta[p, x])

    def degree_two():
        weights = own_coefficients(inner[2:6, 2:10])
        for x in range(CX):
            field[1, 3 + x, 3:11] = (
                (2.0 / AT_LOW[2]) * own_x_of_inner(x, weights) - (1.0 / AT_LOW[2]) * field[0, 3 + x, 3:11])

    def outer_layers(slot):
        for side, at in ((0, 1), (1, 7)):
            cur = field[slot, at:at + 2, 3:11]
            near = field[slot, at - 1:at + 1, 3:11] + field[slot, at + 1:at + 3, 3:11] + along_z(cur)
            near = near + jnp.stack([along(cur[0]), along(cur[1])])
            inner[at - 1:at + 1, 2:10] = (
                beta_x[side, NPROJ] * cur - side_scale * near
                + spread(unpack(coef_in[slot, side]), lambda p: beta_x[side, p]))
        for side, at in ((0, 1), (1, 11)):
            cur = field[slot, 3:7, at:at + 2]
            near = field[slot, 3:7, at - 1:at + 1] + field[slot, 3:7, at + 1:at + 3] + along_z(cur)
            near = near + along(cur)
            inner[2:6, at - 1:at + 1] = (
                beta_y[side, NPROJ] * cur - side_scale * near
                + spread(unpack(coef_in[slot, 2 + side]), lambda p: beta_y[side, p]))
    def corner_cells(slot, weights):
        added, tiles = [], []
        for x, y, own_x, own_y, out in ((2, 2, 3, 3, -1), (2, 11, 3, 10, 1), (7, 2, 6, 3, -1), (7, 11, 6, 10, 1)):
            far_x, far_y = 2 * x - own_x, y + out
            for here_x, here_y, got in ((x, own_y, (x, y)), (far_x, own_y, (far_x, y)),
                                        (own_x, y, (x, y)), (own_x, far_y, (x, far_y))):
                inner[here_x - 1, here_y - 1] = (
                    inner[here_x - 1, here_y - 1] - side_scale * field[(slot,) + got])
            more = (4.0 * side_scale * side_scale) * field[slot, x, y]
            inner2[own_x - 2, own_y - 2] = inner2[own_x - 2, own_y - 2] + more
            added.append(more)
            tiles.append((own_x - 3, own_y - 3))
        out = []
        for p in range(NPROJ):
            acc = sum(more * beta[p, x, y] for more, (x, y) in zip(added, tiles))
            out.append(weights[p] + jnp.sum(acc, axis=1, keepdims=True))
        for n, (x, y) in enumerate(((2, 2), (2, 11), (7, 2), (7, 11))):
            cur = field[slot, x, y]
            near = field[slot, x - 1, y] + field[slot, x + 1, y] + field[slot, x, y - 1] + field[slot, x, y + 1]
            near = near + along_z(cur[None])[0]
            inner[x - 1, y - 1] = (
                beta_d[n, NPROJ] * cur - side_scale * near
                + spread(unpack(coef_in[slot, 4 + n]), lambda p: beta_d[n, p]))
        return out

    XL, XR, YL, YR = 1, 2, 3, 4

    def group(tile, n):
        return pltpu.roll(tile, CZ - 8 * n, 1)

    def next_own(slot):
        near = [coef_in[slot, place] for place in range(4)]
        own = group(near[0], XR) + group(near[1], XL) + group(near[2], YR) + group(near[3], YL)
        return unpack(part[slot] - side_scale * own)

    def next_around(slot):
        got = [coef_in[slot, place] for place in range(11)]
        mine = coef[slot]
        low_x = group(mine, XL) + group(got[8], XR) + group(got[4], YR) + group(got[5], YL)
        high_x = group(mine, XR) + group(got[8], XL) + group(got[6], YR) + group(got[7], YL)
        low_y = group(mine, YL) + group(got[9], YR) + group(got[4], XR) + group(got[6], XL)
        high_y = group(mine, YR) + group(got[10], YL) + group(got[5], XR) + group(got[7], XL)
        return [unpack(part_in[slot, place] - side_scale * terms)
                for place, terms in enumerate((low_x, high_x, low_y, high_y))]

    def middle_own(slot, weights):
        for x in range(CX):
            inner2[1 + x, 1:9] = 2.0 * own_x_of_inner(x, weights) - field[slot, 3 + x, 3:11]

    def middle_around(slot, weights):
        for side, at in ((0, 1), (1, 6)):
            cur = inner[at, 2:10]
            near = inner[at - 1, 2:10] + inner[at + 1, 2:10] + inner[at, 1:9] + inner[at, 3:11] + along_z(cur)
            got = (beta_x[side, NPROJ, 1 - side] * cur - side_scale * near
                   + spread(weights[side], lambda p: beta_x[side, p, 1 - side]))
            inner2[at - 1, 1:9] = 2.0 * got - field[slot, at + 1, 3:11]
        for side, at in ((0, 1), (1, 10)):
            cur = inner[2:6, at]
            near = inner[2:6, at - 1] + inner[2:6, at + 1] + inner[1:5, at] + inner[3:7, at] + along_z(cur)
            got = (beta_y[side, NPROJ, :, 1 - side] * cur - side_scale * near
                   + spread(weights[2 + side], lambda p: beta_y[side, p, :, 1 - side]))
            inner2[1:5, at - 1] = 2.0 * got - field[slot, 3:7, at + 1]

    def swap(x):
        return pltpu.make_async_remote_copy(
            src_ref=field.at[1, 3 + x, 3:11], dst_ref=other.at[x], send_sem=bs_sem.at[x], recv_sem=br_sem.at[x],
            device_id=twin, device_id_type=MESH)

    def degree_three(slot, weights, scale, back, last):
        for x in range(CX):
            cur = inner2[1 + x, 1:9]
            near = inner2[x, 1:9] + inner2[2 + x, 1:9] + inner2[1 + x, 0:8] + inner2[1 + x, 2:10]
            near = near + along_z(cur)
            got = beta[NPROJ, x] * cur - side_scale * near + spread(weights, lambda p: beta[p, x])
            got = 2.0 * got - inner[2 + x, 2:10]
            field[1 - slot, 3 + x, 3:11] = scale * got - back * field[1 - slot, 3 + x, 3:11]

            @pl.when(last)
            def _(x=x):
                swap(x).start()

    def wait_sent(slot):
        corners, faces_y, faces_x = halo_copies(slot, 3)
        for c in corners + faces_y + faces_x + tuple(coef_copies(slot, 11)) + tuple(part_copies(slot)):
            c.wait_send()

    def start(copies):
        for c in copies:
            c.start()

    corners, faces_y, faces_x = halo_copies(0, 2)
    near_sides, next_sides, far_sides = side_copies(0), side_copies(1), diagonal_copies()
    start(corners + near_sides[:2] + faces_y)
    weights = own_coefficients(field[0, 3:7, 3:11])
    coef[0] = pack(weights)
    tiles = coef_copies(0, 4)
    start(tiles)
    start(faces_x)
    start(near_sides[2:])
    for x in range(CX):
        inner[2 + x, 2:10] = inside(0, weights, x)
    split_stored(0)
    start(next_sides + far_sides)
    split_stored(1)
    for c in near_sides:
        c.wait_recv()
    spread_sides(0)
    for c in faces_x + faces_y + tuple(tiles):
        c.wait_recv()
    add_halo(0)
    first_layer(0)
    degree_two()
    for c in corners:
        c.wait_recv()
    twice = (2.0 / AT_LOW[2]) * (2.0 * side_scale * side_scale)
    for x, y, at_x, at_y in ((3, 3, 2, 2), (3, 10, 2, 11), (6, 3, 7, 2), (6, 10, 7, 11)):
        field[1, x, y] = field[1, x, y] + twice * field[0, at_x, at_y]

    def step(k, carry):
        slot = 1 - k
        corners, faces_y, faces_x = halo_copies(slot, 3)
        start(corners)
        weights = own_coefficients(field[slot, 3:7, 3:11])
        columns = list(weights)
        for side, at in ((0, 3), (1, 6)):
            columns += dot_tiles(field[slot, at, 3:11], lambda p: beta_x[side, p, 1 - side])
        for side, at in ((0, 3), (1, 10)):
            columns += dot_tiles(field[slot, 3:7, at], lambda p: beta_y[side, p, :, 1 - side])
        coef[slot] = pack(columns)
        tiles = coef_copies(slot, 11)
        start(tiles)
        start(faces_y)
        start(faces_x)

        @pl.when(k == 0)
        def _():
            corners, faces_y, faces_x = halo_copies(0, 2)
            for c in corners + faces_y + faces_x + tuple(coef_copies(0, 4)):
                c.wait_send()
            field[0, 3:7, 3:11] = inner[2:6, 2:10]

        for x in range(CX):
            inner[2 + x, 2:10] = inside(slot, weights, x)
        part[slot] = pack(own_coefficients(inner[2:6, 2:10]))
        parts = part_copies(slot)
        start(parts)

        @pl.when(k == 0)
        def _():
            for c in near_sides + next_sides + far_sides:
                c.wait_send()
            for c in next_sides + far_sides:
                c.wait_recv()
            spread_sides(1)
            spread_diagonals()

        for n in range(3):
            split_stored(2 + 3 * k + n)

        @pl.when(k == 1)
        def _():
            wait_sent(1)

        for c in faces_x + faces_y + tuple(tiles[7:]):
            c.wait_recv()
        add_halo(slot)
        outer_layers(slot)
        middle_own(slot, next_own(slot))
        weights = own_coefficients(inner2[1:5, 1:9])
        for c in corners + tuple(tiles[:7]) + tuple(parts):
            c.wait_recv()
        weights = corner_cells(slot, weights)
        middle_around(slot, next_around(slot))
        scale = jnp.where(k == 0, 2.0 * AT_LOW[2] / AT_LOW[5], 2.0 * AT_LOW[5] / AT_LOW[8])
        back = jnp.where(k == 0, 1.0 / AT_LOW[5], AT_LOW[2] / AT_LOW[8])
        degree_three(slot, weights, scale, back, k == 1)
        return carry

    lax.fori_loop(0, 2, step, 0)
    wait_sent(0)

    first_core = band == 0
    def send1(c):
        return pltpu.make_async_remote_copy(
            src_ref=pbuf.at[c], dst_ref=r1.at[mz], send_sem=p1s.at[c], recv_sem=p1r.at[mz],
            device_id=(gx, c * NG_Y + my, band), device_id_type=MESH)

    nt = (((1,), (1,)), ((), ()))
    for x in range(CX):
        swap(x).wait_recv()
        for y in range(CY):
            mine, theirs = field[1, 3 + x, 3 + y], other[x, y]
            both = jnp.concatenate(
                [jnp.where(first_core, mine, theirs), jnp.where(first_core, theirs, mine)], axis=0)
            high = both.astype(BF16)
            wmat[0:16, y * CZ:(y + 1) * CZ] = high
            wmat[16:32, y * CZ:(y + 1) * CZ] = (both - high.astype(F32)).astype(BF16)
        weights = wmat[...]
        cols = slice(x * CY * CZ, (x + 1) * CY * CZ)
        got = lax.dot_general(weights, s_hi[:, cols], nt, preferred_element_type=F32)
        got = got[0:16] + got[16:32]
        got = got + lax.dot_general(weights[0:16], s_lo[:, cols], nt, preferred_element_type=F32)
        total[...] = got if x == 0 else total[...] + got
    for t in range(NJ // 128):
        flat = total[:, t * 128:(t + 1) * 128]
        for h in range(2):
            c = 2 * t + h
            pbuf[c] = flat[8 * h:8 * h + 8]

            @pl.when(mz == c)
            def _(c=c):
                r1[c] = pbuf[c]

            @pl.when(mz != c)
            def _(c=c):
                send1(c).start()

    def recv1(i):
        at, device = z_peer(i)
        return pltpu.make_async_remote_copy(
            src_ref=pbuf.at[at], dst_ref=r1.at[at], send_sem=p1s.at[at], recv_sem=p1r.at[at],
            device_id=device, device_id_type=MESH)

    for x in range(CX):
        swap(x).wait_send()
    for i in range(1, NG_Z):
        recv1(i).wait_recv()
    g2[plane] = jnp.sum(r1[...], axis=0)

    def send2(i):
        return pltpu.make_async_remote_copy(
            src_ref=g2.at[plane], dst_ref=g2.at[plane], send_sem=p2s.at[i], recv_sem=p2r.at[plane],
            device_id=plane_peer(i)[1], device_id_type=MESH)

    def recv2(i):
        at, device = plane_peer(i)
        return pltpu.make_async_remote_copy(
            src_ref=g2.at[plane], dst_ref=g2.at[at], send_sem=p2s.at[i], recv_sem=p2r.at[at],
            device_id=device, device_id_type=MESH)

    for i in (10, 9, 11, 6, 14, 5, 7, 13, 15, 2, 8, 1, 3, 4, 12):
        send2(i).start()
    for i in range(1, NG_Z):
        recv1(i).wait_send()
    for i in range(1, PLANE):
        recv2(i).wait_recv()
    q3[mz] = jnp.sum(g2[...], axis=0)

    def send3(i):
        return pltpu.make_async_remote_copy(
            src_ref=q3.at[mz], dst_ref=q3.at[mz], send_sem=p3s.at[i], recv_sem=p3r.at[mz],
            device_id=z_peer(i)[1], device_id_type=MESH)

    for i in (4, 3, 5, 2, 6, 1, 7):
        send3(i).start()
    for i in range(1, PLANE):
        send2(i).wait_send()
    nn = (((1,), (0,)), ((), ()))

    def arrived(c):
        pltpu.make_async_remote_copy(
            src_ref=q3.at[mz], dst_ref=q3.at[c], send_sem=p3s.at[0], recv_sem=p3r.at[c],
            device_id=(gx, c * NG_Y + my, band), device_id_type=MESH).wait_recv()

    def give(x):
        return pltpu.make_async_remote_copy(
            src_ref=csend.at[x], dst_ref=crecv.at[x], send_sem=cs_sem.at[x], recv_sem=cr_sem.at[x],
            device_id=twin, device_id_type=MESH)

    pairs = NG_Z // 2
    for n, ahead in enumerate((0, 1, 3, 2)):
        pair = lax.rem(lax.div(mz, 2) + ahead, pairs)
        for h in range(2):
            @pl.when(2 * pair + h != mz)
            def _(h=h):
                arrived(2 * pair + h)

        whole = jnp.concatenate([q3[2 * pair], q3[2 * pair + 1]], axis=0)
        rows_j = pl.ds(pl.multiple_of(pair * 128, 128), 128)
        int_ref[:, rows_j] = whole
        high = whole.astype(BF16)
        low = (whole - high.astype(F32)).astype(BF16)
        left_side = jnp.concatenate([high, low], axis=0)
        for x in range(CX):
            cols = slice(x * CY * CZ, (x + 1) * CY * CZ)
            got = lax.dot_general(left_side, s_hi[rows_j, cols], nn, preferred_element_type=F32)
            more = lax.dot_general(high, s_lo[rows_j, cols], nn, preferred_element_type=F32)
            got = got[0:16] + got[16:32] + more
            if n > 0:
                got = got + fix[:, cols]
            if n < pairs - 1:
                fix[:, cols] = got
                continue
            keep = jnp.where(first_core, got[0:8], got[8:16])
            send = jnp.where(first_core, got[8:16], got[0:8])
            for y in range(CY):
                csend[x, y] = send[:, y * CZ:(y + 1) * CZ]
                field[0, 3 + x, 3 + y] = field[1, 3 + x, 3 + y] - keep[:, y * CZ:(y + 1) * CZ]
            give(x).start()
    for i in range(1, NG_Z):
        send3(i).wait_send()
    for x in range(CX):
        give(x).wait_recv()
        for y in range(CY):
            out_ref[pl.ds(x * CY + y, ORB, stride=NXY), :] = field[0, 3 + x, 3 + y] - crecv[x, y]
    for x in range(CX):
        give(x).wait_send()


def finish(a_ref, b_ref, a_out, b_out):
    a_out[...] = a_ref[...]
    b_out[...] = b_ref[...]


def on_device(block, potential, proj_index, proj_value, proj_strength, stored):
    vmem = pl.BlockSpec(memory_space=pltpu.VMEM)
    hbm = pl.BlockSpec(memory_space=pltpu.HBM)
    dma = pltpu.SemaphoreType.DMA
    projected, intersection = pl.pallas_call(
        kernel,
        out_shape=(
            jax.ShapeDtypeStruct((ORB * NXY, CZ), F32),
            jax.ShapeDtypeStruct((2 * ORB, NJ), F32),
        ),
        in_specs=[
            hbm, hbm, hbm, hbm, hbm, hbm],
        out_specs=(vmem, vmem),
        scratch_shapes=[
            pltpu.VMEM((2, CX + 6, CY + 6, ORB, CZ), F32),
            pltpu.VMEM((CX + 4, CY + 4, ORB, CZ), F32),
            pltpu.VMEM((CX + 2, CY + 2, ORB, CZ), F32),
            pltpu.VMEM((ORB * NXY, CZ), F32),
            pltpu.VMEM((NXY, CZ), F32),
            pltpu.VMEM((NPROJ, 128), jnp.int32),
            pltpu.VMEM((NPROJ, 128), F32),
            pltpu.SMEM((NPROJ,), F32),
            pltpu.VMEM((NPROJ + 1, CX, CY, ORB, CZ), F32),
            pltpu.VMEM((NPROJ + 1, NXY, CZ), F32),
            pltpu.VMEM((2, 2, 40, CZ), F32),
            pltpu.VMEM((4, 16, CZ), F32),
            pltpu.VMEM((2, NPROJ + 1, 2 * CY, CZ), F32),
            pltpu.VMEM((2, 2, 40, CZ), F32),
            pltpu.VMEM((4, 16, CZ), F32),
            pltpu.VMEM((2, NPROJ + 1, 2, CY, ORB, CZ), F32),
            pltpu.VMEM((2, NPROJ + 1, CX, 2, ORB, CZ), F32),
            pltpu.VMEM((4, NPROJ + 1, ORB, CZ), F32),
            pltpu.VMEM((2, ORB, CZ), F32),
            pltpu.VMEM((2, 11, ORB, CZ), F32),
            pltpu.VMEM((2, ORB, CZ), F32),
            pltpu.VMEM((2, 4, ORB, CZ), F32),
            pltpu.VMEM((NXY, NJ, CZ), F32),
            pltpu.VMEM((NJ, CELLS), BF16),
            pltpu.VMEM((NJ, CELLS), BF16),
            pltpu.VMEM((CX, CY, ORB, CZ), F32),
            pltpu.VMEM((4 * ORB, CY * CZ), BF16),
            pltpu.VMEM((2 * ORB, NJ), F32),
            pltpu.VMEM((NG_Z, ORB, CZ), F32),
            pltpu.VMEM((NG_Z, ORB, CZ), F32),
            pltpu.VMEM((PLANE, ORB, CZ), F32),
            pltpu.VMEM((NG_Z, ORB, CZ), F32),
            pltpu.VMEM((2 * ORB, CELLS), F32),
            pltpu.VMEM((CX, CY, ORB, CZ), F32),
            pltpu.VMEM((CX, CY, ORB, CZ), F32),
            dma((5,)), dma((NXY,)), dma((2, 23)), dma((2, 23)), dma((12,)), dma((12,)), dma((CX,)), dma((CX,)),
            dma((NG_Z,)), dma((NG_Z,)), dma((PLANE,)), dma((PLANE,)), dma((NG_Z,)), dma((NG_Z,)),
            dma((CX,)), dma((CX,)),
        ],
        compiler_params=pltpu.CompilerParams(
            collective_id=0, has_side_effects=True, vmem_limit_bytes=60 * 1024 * 1024),
        name="filter_project",
    )(
        block.reshape(ORB * NXY, CZ), potential.reshape(NXY, CZ), proj_index, proj_value,
        proj_strength, stored.reshape(NJ, NXY, CZ))
    projected, intersection = pl.pallas_call(
        finish,
        out_shape=(jax.ShapeDtypeStruct(projected.shape, F32), jax.ShapeDtypeStruct(intersection.shape, F32)),
        in_specs=[vmem, vmem],
        out_specs=(vmem, vmem),
        name="finish",
    )(projected, intersection)
    return projected.reshape(block.shape), intersection.T


def solution(mesh):
    in_specs = (
        P("band", "gx", "gyz", None),
        P("gx", "gyz", None),
        P(("gx", "gyz"), None),
        P(("gx", "gyz"), None),
        P(("gx", "gyz")),
        P("band", "gx", "gyz", None),
    )
    out_specs = (P("band", "gx", "gyz", None), P("band", None))
    return jax.shard_map(
        on_device, mesh=mesh, in_specs=in_specs, out_specs=out_specs, check_vma=False
    )
```
